512 devices in a mesh: leaf: 128 (over x, z, core), rep: 4 (over y).
Axes of the slice: x: 4, y: 4, z: 16, core: 2. Of those that a mesh axis runs over, the one named last changes fastest.
Arguments:
- coords: bfloat16 [64, 524288], P(None, 'leaf'), may hold values from -1.5 to 1.5
- right_sides: bfloat16 [32, 524288], P('rep', 'leaf'), may hold values from -0.59765625 to 0.59765625
- leaf_order: int32 [524288], P('leaf'), may hold values from 0 to 4095, as said below
- leaf_basis: bfloat16 [2048, 256, 128], P('leaf'), may hold values from -0.375 to 0.375
- leaf_transfer: bfloat16 [2048, 128, 128], P('leaf'), may hold values from -0.5 to 0.5
- top_transfer: bfloat16 [6, 2, 128, 128], replicated, may hold values from -0.375 to 0.375
- skel_leaf: int32 [2048, 128], P('leaf'), may hold values from 0 to 255, as said below
- skel_root: int32 [128, 128], P('leaf'), may hold values from 0 to 4095, as said below
- admissible: int32 [2048, 8], P('leaf'), may hold values from 0 to 15, as said below
- near_leaves: int32 [2048, 24], P('leaf'), may hold values from 0 to 47, as said below
- near_count: int32 [2048], P('leaf'), may hold values from 2 to 24, as said below
Outputs:
- applied: float32 [32, 524288], P('rep', 'leaf')
The draws below stay inside these ranges and needn't reach their ends.
Inputs may be any that keep to these rules, and one draw needn't show every extreme that they name: `leaf_order`: each subtree's block of 4096 entries is a permutation. `skel_leaf`: each row holds 128 distinct positions. `skel_root`: each row holds 128 distinct positions. `admissible`: never the row's own leaf; entries may repeat. `near_leaves`: entries 0 to 15 are leaves of the previous subtree, the next 16 those of the own one, the last 16 those of the next one; slot 0 is the leaf itself; the first subtree never names the previous one and the last never the next; entries may repeat; only the first near_count entries of a row are live. `near_count`: leaf 0 has all 24 slots live.
All inputs are finite; a program needn't handle non-finite values.
Results may differ from the reference program's by a relative error of at most 0.0029.
Values may be sent and summed in bfloat16 or wider, within the bound.
A program may use at most 64 MiB of HBM per device.

```python
import jax
import jax.numpy as jnp
from jax import lax

DIM = 64
RANK = 128
LEAF = 256
RHS = 32
LEAVES_DEV = 16
NEAR = 24
ADMIT = 8
PTS_DEV = 4096
SUBTREES = 128
LEAVES = 2048
NPTS = 524288
TOPS = 7
UPPER = 6


def first_positions(key, count, width, picked):

    def one_shuffle(sub_key):
        return jax.random.permutation(sub_key, width)
    shuffled = jax.vmap(one_shuffle)(jax.random.split(key, count))
    return shuffled[:, :picked].astype(jnp.int32)


def near_tables(key):
    key_heavy, key_count, key_pick = jax.random.split(key, 3)
    leaf_ids = jnp.arange(LEAVES, dtype=jnp.int32)
    subtree = leaf_ids // LEAVES_DEV
    local = leaf_ids % LEAVES_DEV
    heavy = jax.random.randint(key_heavy, (SUBTREES,), 1, 5)[subtree]
    unpadded_count = jax.random.randint(key_count, (LEAVES,), 0, 1 << 20)
    count = 2 + unpadded_count % (heavy * (NEAR - 2) // 4 + 1)
    count = jnp.where(leaf_ids == 0, NEAR, count)
    lower = jnp.where(subtree > 0, 0, LEAVES_DEV)
    upper = jnp.where(subtree < SUBTREES - 1, 3 * LEAVES_DEV, 2 * LEAVES_DEV)
    raw_pick = jax.random.randint(key_pick, (LEAVES, NEAR), 0, 1 << 20)
    picked = lower[:, None] + raw_pick % (upper - lower)[:, None]
    second = jnp.where((local == 0) & (subtree > 0), LEAVES_DEV - 1, jnp.where((local == LEAVES_DEV - 1) & (subtree < SUBTREES - 1), 2 * LEAVES_DEV, picked[:, 1]))
    picked = picked.at[:, 0].set(LEAVES_DEV + local).at[:, 1].set(second)
    return (picked.astype(jnp.int32), count.astype(jnp.int32))


def draw_leaf_order(key, part):
    key = jax.random.fold_in(key, 11)
    return first_positions(key, SUBTREES, PTS_DEV, PTS_DEV).reshape(NPTS)


def draw_skel_leaf(key, part):
    key = jax.random.fold_in(key, 13)
    return first_positions(key, LEAVES, LEAF, RANK)


def draw_skel_root(key, part):
    key = jax.random.fold_in(key, 17)
    return first_positions(key, SUBTREES, PTS_DEV, RANK)


def draw_admissible(key, part):
    key = jax.random.fold_in(key, 19)
    local = jnp.arange(LEAVES, dtype=jnp.int32) % LEAVES_DEV
    step_by = jax.random.randint(key, (LEAVES, ADMIT), 0, LEAVES_DEV - 1)
    return ((local[:, None] + 1 + step_by) % LEAVES_DEV).astype(jnp.int32)


def draw_near_leaves(key, part):
    picked, count = near_tables(key)
    return picked


def draw_near_count(key, part):
    picked, count = near_tables(key)
    return count


def shard_levels(rng, shape, shards, least, top_value):
    factor_of = 1.0
    for position, shards_of in shards:
        draws = jax.random.uniform(jax.random.fold_in(jax.random.fold_in(rng, 6), position), (shards_of,), jnp.float32, least / len(shards), top_value / len(shards))
        factor_of = factor_of * jnp.repeat(jnp.exp(draws), shape[position] // shards_of).reshape((-1,) + (1,) * (len(shape) - 1 - position))
    return factor_of


def scatter_about(own_key, shape, scale, reach, cuts=(), kind=jnp.bfloat16):
    values = jax.random.normal(own_key, shape, jnp.float32) * scale
    if len(cuts) > 0:
        values = shard_levels(own_key, shape, cuts, -0.22, 0.18) * values
    return jnp.clip(values, min=-reach, max=reach).astype(kind)


def setup_inputs(seed: int = 0) -> dict:
    key_of = jax.random.split(jax.random.key(seed), 12)
    coords = scatter_about(key_of[0], (DIM, NPTS), 0.25, 1.5, ((1, 128),))
    right_sides = scatter_about(key_of[1], (RHS, NPTS), 0.1, 0.59765625, ((0, 4), (1, 128)))
    leaf_order = draw_leaf_order(jax.random.fold_in(key_of[11], 71), 0)
    leaf_basis = scatter_about(key_of[3], (LEAVES, LEAF, RANK), LEAF ** -0.5, 0.375, ((0, 128),))
    leaf_transfer = scatter_about(key_of[4], (LEAVES, RANK, RANK), RANK ** -0.5, 0.5, ((0, 128),))
    top_transfer = scatter_about(key_of[5], (UPPER, 2, RANK, RANK), (2 * RANK) ** -0.5, 0.375)
    skel_leaf = draw_skel_leaf(jax.random.fold_in(key_of[11], 71), 0)
    skel_root = draw_skel_root(jax.random.fold_in(key_of[11], 71), 0)
    admissible = draw_admissible(jax.random.fold_in(key_of[11], 71), 0)
    near_leaves = draw_near_leaves(jax.random.fold_in(key_of[11], 71), 0)
    near_count = draw_near_count(jax.random.fold_in(key_of[11], 71), 0)
    return {"coords": coords, "right_sides": right_sides, "leaf_order": leaf_order, "leaf_basis": leaf_basis, "leaf_transfer": leaf_transfer, "top_transfer": top_transfer, "skel_leaf": skel_leaf, "skel_root": skel_root, "admissible": admissible, "near_leaves": near_leaves, "near_count": near_count}


HIGH_PRECISION = lax.Precision.HIGHEST

def kernel_block(row_points, col_points):
    cross = jnp.einsum('dn,dm->nm', row_points, col_points, precision=HIGH_PRECISION)
    dist_sq = lax.optimization_barrier(jnp.sum(row_points * row_points, 0))[:, None] + lax.optimization_barrier(jnp.sum(col_points * col_points, 0))[None, :] - 2.0 * cross
    return jnp.exp(-0.5 * jnp.sqrt(jnp.maximum(dist_sq, 0.0) + 1.0))

def reference(coords, right_sides, leaf_order, leaf_basis, leaf_transfer, top_transfer, skel_leaf, skel_root, admissible, near_leaves, near_count):
    offsets = (jnp.arange(SUBTREES, dtype=jnp.int32) * PTS_DEV)[:, None]
    sorted_ids = (leaf_order.reshape(SUBTREES, PTS_DEV).astype(jnp.int32) + offsets).reshape(NPTS)
    points = jnp.take(coords, sorted_ids, axis=1).astype(jnp.float32)
    input_vectors = jnp.take(right_sides, sorted_ids, axis=1).astype(jnp.float32)
    basis_wide = leaf_basis.astype(jnp.float32)
    transfer_wide = leaf_transfer.astype(jnp.float32).reshape(SUBTREES, LEAVES_DEV, RANK, RANK)
    s_leaf = jnp.einsum('rlp,lpk->lrk', input_vectors.reshape(RHS, LEAVES, LEAF), basis_wide, precision=HIGH_PRECISION)
    s_root = jnp.einsum('dlrk,dlkj->drj', s_leaf.reshape(SUBTREES, LEAVES_DEV, RHS, RANK), transfer_wide, precision=HIGH_PRECISION)
    sub_points = points.reshape(DIM, SUBTREES, PTS_DEV).transpose(1, 0, 2)
    root_points = jnp.take_along_axis(sub_points, skel_root.astype(jnp.int32)[:, None, :], axis=2)
    level_s = s_root
    level_points = root_points
    couplings = []
    for level in range(TOPS):
        node_count_total = SUBTREES >> level
        sibling = jnp.arange(node_count_total, dtype=jnp.int32) ^ 1
        kernel_mats = jax.vmap(kernel_block)(level_points, level_points[sibling])
        couplings.append(jnp.einsum('nrj,nij->nri', level_s[sibling], kernel_mats, precision=HIGH_PRECISION))
        if level + 1 < TOPS:
            paired = level_s.reshape(node_count_total // 2, 2, RHS, RANK)
            transfer_pair = top_transfer[level].astype(jnp.float32)
            level_s = jnp.einsum('nrk,kj->nrj', paired[:, 0], transfer_pair[0], precision=HIGH_PRECISION) + jnp.einsum('nrk,kj->nrj', paired[:, 1], transfer_pair[1], precision=HIGH_PRECISION)
            level_points = level_points.reshape(node_count_total // 2, 2, DIM, RANK)[:, 0]
    running = couplings[TOPS - 1]
    for level in range(TOPS - 2, -1, -1):
        transfer_pair = top_transfer[level].astype(jnp.float32)
        left_down = jnp.einsum('nrj,kj->nrk', running, transfer_pair[0], precision=HIGH_PRECISION)
        right_down = jnp.einsum('nrj,kj->nrk', running, transfer_pair[1], precision=HIGH_PRECISION)
        running = couplings[level] + jnp.stack([left_down, right_down], axis=1).reshape(-1, RHS, RANK)
    leaf_points = jnp.take_along_axis(points.reshape(DIM, LEAVES, LEAF).transpose(1, 0, 2), skel_leaf.astype(jnp.int32)[:, None, :], axis=2)

    def admit_one(inputs):
        dev_points, dev_s, dev_admit = inputs
        partner = dev_points[dev_admit]
        kernel_mats = jax.vmap(jax.vmap(kernel_block, in_axes=(None, 0)))(dev_points, partner)
        return jnp.einsum('lmrj,lmij->lri', dev_s[dev_admit], kernel_mats, precision=HIGH_PRECISION)
    admitted = lax.map(admit_one, (leaf_points.reshape(SUBTREES, LEAVES_DEV, DIM, RANK), s_leaf.reshape(SUBTREES, LEAVES_DEV, RHS, RANK), admissible.astype(jnp.int32).reshape(SUBTREES, LEAVES_DEV, ADMIT)))
    t_leaf = jnp.einsum('drj,dlkj->dlrk', running, transfer_wide, precision=HIGH_PRECISION) + admitted
    t_low = lax.optimization_barrier(t_leaf.reshape(LEAVES, RHS, RANK).astype(jnp.bfloat16))
    y_far = jnp.einsum('lrk,lpk->rlp', t_low.astype(jnp.float32), basis_wide, precision=HIGH_PRECISION).reshape(RHS, NPTS)
    win_points = points.reshape(DIM, LEAVES, LEAF)
    win_vectors = input_vectors.reshape(RHS, LEAVES, LEAF)

    def near_one(leaf_id):
        subtree = leaf_id // LEAVES_DEV
        partner = (near_leaves[leaf_id].astype(jnp.int32) + (subtree - 1) * LEAVES_DEV).astype(jnp.int32)
        own_points = lax.dynamic_index_in_dim(win_points, leaf_id, 1, keepdims=False)
        col_points = jnp.take(win_points, partner, axis=1)
        kernel_tile_blocks = jax.vmap(kernel_block, in_axes=(None, 1))(own_points, col_points)
        kernel_tile_blocks = lax.optimization_barrier(kernel_tile_blocks.astype(jnp.bfloat16)).astype(jnp.float32)
        is_active_flag = (jnp.arange(NEAR, dtype=jnp.int32) < near_count[leaf_id]).astype(jnp.float32)
        column_vector_block = jnp.take(win_vectors, partner, axis=1)
        return jnp.einsum('vox,tvx,v->to', kernel_tile_blocks, column_vector_block, is_active_flag, precision=HIGH_PRECISION)
    near_part = lax.map(near_one, jnp.arange(LEAVES, dtype=jnp.int32))
    near_part = near_part.transpose(1, 0, 2).reshape(RHS, NPTS)
    y_sorted = near_part + y_far
    return jnp.zeros((RHS, NPTS), jnp.float32).at[:, sorted_ids].set(y_sorted)
```

```python
import functools
import math

import jax
import jax.numpy as jnp
from jax import lax
from jax.experimental import pallas as pl
from jax.experimental.pallas import tpu as pltpu
from jax.sharding import PartitionSpec as P

MESH = pl.DeviceIdType.MESH
F32 = jnp.float32
BF16 = jnp.bfloat16
I32 = jnp.int32

DIM = 64
RANK = 128
LEAF = 256
LEAVES = 16
PTS = 4096
LANES = 128
BLOCKS = PTS // LANES
REPS = 4
QUARTER = LEAVES // REPS
OWN = 8
RHS = 32
SIDES = 3
PARTNERS = SIDES * QUARTER
LOW_LEVELS = 3
VMEM_LIMIT = 60 * 1024 * 1024
HALF_LOG2E = -0.5 * math.log2(math.e)


def dot_nn(a, b):
    return lax.dot_general(a, b, (((1,), (0,)), ((), ())), preferred_element_type=F32)


def dot_nt(a, b):
    return lax.dot_general(a, b, (((1,), (1,)), ((), ())), preferred_element_type=F32)


def kernel_values(shifted):
    shifted = jnp.maximum(shifted, 1.0)
    return jnp.exp2((shifted * HALF_LOG2E) * lax.rsqrt(shifted))


def split_two(x):
    high = x.astype(BF16)
    return high, (x - high.astype(F32)).astype(BF16)


def stack_two(x):
    high = x.astype(BF16).astype(F32)
    return jnp.concatenate([high, x - high], axis=0).astype(BF16)


def fold_two(x):
    half = x.shape[0] // 2
    return x[:half] + x[half:]


def dot_wide(x, matrix):
    return fold_two(dot_nn(stack_two(x), matrix))


def dot_wide_nt(x, matrix):
    return fold_two(dot_nt(stack_two(x), matrix))


def dot_both_wide(x, matrix):
    rows = stack_two(x)
    high, low = split_two(matrix)
    return fold_two(dot_nn(rows, high)) + fold_two(dot_nn(rows, low))


def with_norms(points, own):
    count = points.shape[1]
    norm = jnp.sum(points * points, axis=0, keepdims=True)
    if own:
        norm = norm + 1.0
    high = norm.astype(BF16).astype(F32)
    rest = norm - high
    mid = rest.astype(BF16).astype(F32)
    low = rest - mid
    row = lax.broadcasted_iota(I32, (16, count), 0)
    if not own:
        row = row - 3
    tail = jnp.where(row == 0, high, jnp.where(row == 1, mid, jnp.where(row == 2, low, 0.0)))
    ones = lax.broadcasted_iota(I32, (16, count), 0) - (3 if own else 0)
    tail = jnp.where((ones >= 0) & (ones < 3), 1.0, tail)
    head = points * -2.0 if own else points
    return jnp.concatenate([head, tail, jnp.zeros((LANES - DIM - 16, count), F32)], axis=0)


def pick(table, lanes):
    return jnp.take_along_axis(table, lanes, axis=1, mode="promise_in_bounds")


def sort_kernel(
    coords_ref,
    rhs_ref,
    order_ref,
    basis_ref,
    transfer_ref,
    skel_leaf_ref,
    skel_root_ref,
    admissible_ref,
    near_ref,
    count_ref,
    own_ref,
    rows_ref,
    vectors_ref,
    own_skel_ref,
    skel_rows_ref,
    root_ref,
    s_root_ref,
    times_ref,
    raw_ref,
    sorted_ref,
):
    rep = lax.axis_index("rep")
    groups = (DIM + OWN) // 8

    def widen(block, _):
        lanes = pl.ds(pl.multiple_of(block * LANES, LANES), LANES)
        raw_ref[block, :DIM, :] = coords_ref[:, lanes].astype(F32)
        raw_ref[block, DIM:, :] = rhs_ref[:, lanes].astype(F32)
        return 0

    lax.fori_loop(0, BLOCKS, widen, 0, unroll=4)

    def gather_block(positions, count):
        positions = jnp.broadcast_to(positions, (8, LANES))
        high = positions >> 7
        low = positions & 127
        out = [jnp.zeros((8, LANES), F32)] * count
        for source in range(BLOCKS):
            here = high == source
            for group in range(count):
                table = raw_ref[source, group * 8 : group * 8 + 8, :]
                out[group] = jnp.where(here, pick(table, low), out[group])
        return out

    def sort_leaf(leaf, _):
        for half in range(2):
            parts = gather_block(order_ref[pl.ds(leaf * 2 + half, 1), :], groups)
            span = slice(half * LANES, half * LANES + LANES)
            for group in range(groups):
                sorted_ref[leaf, group * 8 : group * 8 + 8, span] = parts[group]
            points = jnp.concatenate(parts[: DIM // 8], axis=0)
            own_ref[leaf, :, span] = with_norms(points, True).astype(BF16)
        return 0

    lax.fori_loop(0, LEAVES, sort_leaf, 0)

    for k in range(QUARTER):
        leaf = k * REPS + rep
        for half in range(2):
            span = slice(half * LANES, half * LANES + LANES)
            columns = with_norms(sorted_ref[leaf, :DIM, span], False)
            rows_ref[k, span, :] = columns.T.astype(BF16)

    for target in range(REPS):
        for column in range(2):
            top = sorted_ref[column * REPS + target, DIM:, :]
            bottom = sorted_ref[(column + 2) * REPS + target, DIM:, :]
            vectors_ref[target, :, column * LEAF : (column + 1) * LEAF] = jnp.concatenate(
                [top, bottom], axis=0
            ).astype(BF16)

    def leaf_skeleton(leaf, positions):
        positions = jnp.broadcast_to(positions, (8, LANES))
        high = positions >> 7
        low = positions & 127
        parts = []
        for group in range(DIM // 8):
            span = slice(group * 8, group * 8 + 8)
            left = pick(sorted_ref[leaf, span, :LANES], low)
            right = pick(sorted_ref[leaf, span, LANES:], low)
            parts.append(jnp.where(high == 0, left, right))
        return jnp.concatenate(parts, axis=0)

    def skeleton(leaf, _):
        points = leaf_skeleton(leaf, skel_leaf_ref[pl.ds(leaf, 1), :])
        own_skel_ref[leaf] = with_norms(points, True).astype(BF16)
        return 0

    lax.fori_loop(0, LEAVES, skeleton, 0)
    for k in range(QUARTER):
        leaf = k * REPS + rep
        points = leaf_skeleton(leaf, skel_leaf_ref[pl.ds(leaf, 1), :])
        skel_rows_ref[k] = with_norms(points, False).T.astype(BF16)

    positions = jnp.broadcast_to(skel_root_ref[...], (8, LANES))
    low = positions & 127
    leaf_of = positions >> 8
    right_half = ((positions >> 7) & 1) == 1
    parts = []
    for group in range(DIM // 8):
        span = slice(group * 8, group * 8 + 8)
        out = jnp.zeros((8, LANES), F32)
        for leaf in range(LEAVES):
            left = pick(sorted_ref[leaf, span, :LANES], low)
            right = pick(sorted_ref[leaf, span, LANES:], low)
            out = jnp.where(leaf_of == leaf, jnp.where(right_half, right, left), out)
        parts.append(out)
    root_ref[...] = jnp.concatenate(parts, axis=0).astype(BF16)

    def up(leaf, total):
        s_leaf = dot_nn(sorted_ref[leaf, DIM:, :].astype(BF16), basis_ref[leaf])
        return total + dot_wide(s_leaf, transfer_ref[leaf])

    s_root_ref[...] = lax.fori_loop(0, LEAVES, up, jnp.zeros((OWN, RANK), F32), unroll=4)

    near = near_ref[...]
    slot = lax.broadcasted_iota(I32, near.shape, 1)
    live = slot < count_ref[...]
    admissible = admissible_ref[...]
    lane = lax.broadcasted_iota(I32, (LEAVES, LANES), 1)
    times = jnp.zeros((LEAVES, LANES), F32)
    for entry in range(PARTNERS + QUARTER):
        if entry < PARTNERS:
            named = (near == entry * REPS + rep) & live
        else:
            named = admissible == (entry - PARTNERS) * REPS + rep
        total = jnp.sum(jnp.where(named, 1.0, 0.0), axis=1, keepdims=True)
        times = jnp.where(lane == entry, total, times)
    times_ref[...] = times.astype(I32)


def greet(devices):
    barrier = pltpu.get_barrier_semaphore()
    for device in devices:
        pl.semaphore_signal(barrier, inc=1, device_id=device, device_id_type=MESH)
    pl.semaphore_wait(barrier, len(devices))


def climb(first, last, levels, leaf, rep, points_ref, got_points_ref, s_ref, got_s_ref, c_ref, top_ref, sems):
    for level in range(first, last):
        at = level - first
        sibling = (leaf ^ (1 << level), rep)
        copies = [
            pltpu.make_async_remote_copy(
                src_ref=points_ref.at[at],
                dst_ref=got_points_ref.at[at],
                send_sem=sems.at[at, 0],
                recv_sem=sems.at[at, 1],
                device_id=sibling,
                device_id_type=MESH,
            ),
            pltpu.make_async_remote_copy(
                src_ref=s_ref.at[at],
                dst_ref=got_s_ref.at[at],
                send_sem=sems.at[at, 2],
                recv_sem=sems.at[at, 3],
                device_id=sibling,
                device_id_type=MESH,
            ),
        ]
        for copy in copies:
            copy.start()
        mine = points_ref[at].astype(F32)
        mine_s = s_ref[at]
        own = with_norms(mine, True).astype(BF16)
        for copy in copies:
            copy.wait_recv()
        theirs = got_points_ref[at].astype(F32)
        theirs_s = got_s_ref[at]
        if level + 1 < levels:
            on_right = lax.rem(leaf // (1 << level), 2) == 1
            left_s = jnp.where(on_right, theirs_s, mine_s)
            right_s = jnp.where(on_right, mine_s, theirs_s)
            points_ref[at + 1] = jnp.where(on_right, theirs, mine).astype(BF16)
            s_ref[at + 1] = dot_wide(left_s, top_ref[level, 0]) + dot_wide(right_s, top_ref[level, 1])
        rows = with_norms(theirs, False).T.astype(BF16)
        c_ref[level] = dot_both_wide(theirs_s, kernel_values(dot_nn(rows, own)))
        for copy in copies:
            copy.wait_send()


def exchange_kernel(
    count,
    levels,
    rows_ref,
    vectors_ref,
    root_ref,
    s_root_ref,
    top_ref,
    window_ref,
    window_vectors_ref,
    up_points_ref,
    up_s_ref,
    c_ref,
    points_ref,
    got_points_ref,
    s_ref,
    got_s_ref,
    row_sems,
    vector_send_sems,
    vector_recv_sems,
    tree_sems,
    local_sems,
):
    leaf = lax.axis_index("leaf")
    rep = lax.axis_index("rep")
    before = lax.rem(leaf + count - 1, count)
    after = lax.rem(leaf + 1, count)
    others = [lax.rem(rep + step, REPS) for step in range(1, REPS)]
    low = min(LOW_LEVELS, levels)
    partners = [(side, other) for side in (before, after) for other in [rep] + others]
    partners += [(leaf, other) for other in others]
    partners += [(leaf ^ (1 << level), rep) for level in range(low)]
    greet(partners)

    copies = []
    for index, (side, device) in enumerate(((2, before), (0, after))):
        copies.append(
            pltpu.make_async_remote_copy(
                src_ref=rows_ref,
                dst_ref=window_ref.at[side],
                send_sem=row_sems.at[0, index],
                recv_sem=row_sems.at[1, index],
                device_id=(device, rep),
                device_id_type=MESH,
            )
        )
    for index, (side, device) in enumerate(((2, before), (0, after), (1, leaf))):
        for step in range(REPS):
            if side == 1 and step == 0:
                continue
            target = lax.rem(rep + step, REPS)
            copies.append(
                pltpu.make_async_remote_copy(
                    src_ref=vectors_ref.at[target],
                    dst_ref=window_vectors_ref.at[side, rep],
                    send_sem=vector_send_sems.at[index, step],
                    recv_sem=vector_recv_sems.at[index, step],
                    device_id=(device, target),
                    device_id_type=MESH,
                )
            )
    for copy in copies:
        copy.start()
    own_rows = pltpu.make_async_copy(rows_ref, window_ref.at[1], local_sems.at[0])
    own_vectors = pltpu.make_async_copy(
        vectors_ref.at[rep], window_vectors_ref.at[1, rep], local_sems.at[1]
    )
    own_rows.start()
    own_vectors.start()

    points_ref[0] = root_ref[...]
    s_ref[0] = s_root_ref[...]
    climb(0, low, levels, leaf, rep, points_ref, got_points_ref, s_ref, got_s_ref, c_ref, top_ref, tree_sems)
    up_points_ref[...] = points_ref[low]
    up_s_ref[...] = s_ref[low]

    own_rows.wait()
    own_vectors.wait()
    for copy in copies[:2]:
        copy.wait()
    number = 2
    for index, side in enumerate((2, 0, 1)):
        for step in range(REPS):
            if side == 1 and step == 0:
                continue
            source = lax.rem(rep + REPS - step, REPS)
            copies[number].wait_send()
            pltpu.make_async_remote_copy(
                src_ref=vectors_ref.at[rep],
                dst_ref=window_vectors_ref.at[side, source],
                send_sem=vector_send_sems.at[index, step],
                recv_sem=vector_recv_sems.at[index, step],
                device_id=(leaf, lax.rem(rep + 1, REPS)),
                device_id_type=MESH,
            ).wait_recv()
            number += 1


def near_kernel(
    times_ref,
    own_ref,
    window_ref,
    window_vectors_ref,
    basis_ref,
    own_skel_ref,
    skel_rows_ref,
    out_ref,
    list_ref,
    vectors_ref,
    total_ref,
    s_ref,
    t_ref,
):
    rep = lax.axis_index("rep")

    for side in range(SIDES):
        for column in range(2):
            span = slice(column * LEAF, (column + 1) * LEAF)
            blocks = [window_vectors_ref[side, source, :, span].astype(F32) for source in range(REPS)]
            vectors_ref[side * QUARTER + column] = jnp.concatenate(
                [block[:OWN] for block in blocks], axis=0
            ).astype(BF16)
            vectors_ref[side * QUARTER + column + 2] = jnp.concatenate(
                [block[OWN:] for block in blocks], axis=0
            ).astype(BF16)
    for k in range(QUARTER):
        s_leaf = dot_nn(vectors_ref[QUARTER + k], basis_ref[k * REPS + rep])
        s_ref[k] = stack_two(s_leaf)

    total_ref[...] = jnp.zeros_like(total_ref)
    t_ref[...] = jnp.zeros_like(t_ref)

    def make_list(first, width):
        def one_leaf(leaf, filled):
            for entry in range(first, first + width):
                list_ref[filled] = leaf * 16 + entry
                filled = filled + jnp.where(times_ref[leaf, entry] > 0, 1, 0)
            return filled

        filled = lax.fori_loop(0, LEAVES, one_leaf, 0)
        list_ref[filled] = 15
        return filled

    def scale_of(number, filled, code):
        times = times_ref[code // 16, lax.rem(code, 16)]
        return jnp.where(number < filled, times, 0).astype(F32)

    filled = make_list(0, PARTNERS)

    def near_pair(pair, _):
        terms = []
        for offset in range(2):
            number = pair * 2 + offset
            code = list_ref[number]
            leaf = code // 16
            entry = jnp.minimum(lax.rem(code, 16), PARTNERS - 1)
            shifted = dot_nn(window_ref[entry], own_ref[leaf])
            tile = kernel_values(shifted).astype(BF16)
            terms.append((leaf, dot_nn(vectors_ref[entry], tile) * scale_of(number, filled, code)))
        for leaf, term in terms:
            total_ref[leaf] += term
        return 0

    lax.fori_loop(0, (filled + 1) // 2, near_pair, 0)

    filled_far = make_list(PARTNERS, QUARTER)

    def far_pair(pair, _):
        terms = []
        for offset in range(2):
            number = pair * 2 + offset
            code = list_ref[number]
            leaf = code // 16
            entry = jnp.maximum(lax.rem(code, 16) - PARTNERS, 0)
            shifted = dot_nn(skel_rows_ref[entry], own_skel_ref[leaf])
            high, low = split_two(kernel_values(shifted))
            term = fold_two(dot_nn(s_ref[entry], high)) + dot_nn(s_ref[entry, :RHS], low)
            terms.append((leaf, term * scale_of(number, filled_far, code)))
        for leaf, term in terms:
            t_ref[leaf] += term
        return 0

    lax.fori_loop(0, (filled_far + 1) // 2, far_pair, 0)

    for leaf in range(LEAVES):
        far = dot_wide_nt(t_ref[leaf], basis_ref[leaf])
        out_ref[:, :, leaf * LEAF : (leaf + 1) * LEAF] = (total_ref[leaf] + far).reshape(REPS, OWN, LEAF)


def combine_kernel(
    levels,
    part_ref,
    up_points_ref,
    up_s_ref,
    low_c_ref,
    top_ref,
    basis_ref,
    transfer_ref,
    order_ref,
    out_ref,
    inverse_ref,
    got_ref,
    points_ref,
    got_points_ref,
    s_ref,
    got_s_ref,
    c_ref,
    sum_sems,
    tree_sems,
):
    leaf = lax.axis_index("leaf")
    rep = lax.axis_index("rep")
    low = min(LOW_LEVELS, levels)
    others = [lax.rem(rep + step, REPS) for step in range(1, REPS)]
    greet([(leaf, other) for other in others] + [(leaf ^ (1 << level), rep) for level in range(low, levels)])
    copies = []
    for index, other in enumerate(others):
        copy = pltpu.make_async_remote_copy(
            src_ref=part_ref.at[other],
            dst_ref=got_ref.at[index],
            send_sem=sum_sems.at[0, index],
            recv_sem=sum_sems.at[1, index],
            device_id=(leaf, other),
            device_id_type=MESH,
        )
        copy.start()
        copies.append(copy)

    for level in range(low):
        c_ref[level] = low_c_ref[level]
    points_ref[0] = up_points_ref[...]
    s_ref[0] = up_s_ref[...]
    climb(low, levels, levels, leaf, rep, points_ref, got_points_ref, s_ref, got_s_ref, c_ref, top_ref, tree_sems)

    running = c_ref[levels - 1]
    for level in range(levels - 2, -1, -1):
        side = lax.rem(leaf // (1 << level), 2)
        running = c_ref[level] + dot_wide_nt(running, top_ref[level, side])
    rows = stack_two(running)

    def down(number, _):
        t_leaf = fold_two(dot_nt(rows, transfer_ref[number]))
        lanes = pl.ds(pl.multiple_of(number * LEAF, LEAF), LEAF)
        out_ref[:, lanes] = part_ref[rep, :, lanes] + dot_wide_nt(t_leaf, basis_ref[number])
        return 0

    lax.fori_loop(0, LEAVES, down, 0, unroll=2)

    lane = lax.broadcasted_iota(I32, (1, LANES), 1)
    inverse_high = jnp.zeros((BLOCKS, LANES), F32)
    inverse_low = jnp.zeros((BLOCKS, LANES), F32)

    def invert(block, sums):
        positions = order_ref[pl.ds(block, 1), :]
        row = lax.broadcasted_iota(I32, (BLOCKS, LANES), 0)
        column = lax.broadcasted_iota(I32, (LANES, LANES), 0)
        is_row = row == (positions >> 7)
        is_column = jnp.where(column == (positions & 127), 1.0, 0.0).astype(BF16)
        marks = jnp.concatenate(
            [
                jnp.where(is_row, block.astype(F32), 0.0),
                jnp.where(is_row, lane.astype(F32), 0.0),
            ],
            axis=0,
        ).astype(BF16)
        return sums + dot_nt(marks, is_column)

    sums = lax.fori_loop(0, BLOCKS, invert, jnp.zeros((2 * BLOCKS, LANES), F32), unroll=2)
    inverse_ref[...] = (sums[:BLOCKS] * float(LANES) + sums[BLOCKS:]).astype(I32)

    for copy in copies:
        copy.wait()
    out_ref[...] = ((out_ref[...] + got_ref[0]) + got_ref[1]) + got_ref[2]


def unsort_kernel(sorted_ref, inverse_ref, out_ref):
    def one_block(block, _):
        positions = jnp.broadcast_to(inverse_ref[pl.ds(block, 1), :], (OWN, LANES))
        high = positions >> 7
        low = positions & 127
        out = jnp.zeros((OWN, LANES), F32)
        for source in range(BLOCKS):
            table = sorted_ref[:, source * LANES : (source + 1) * LANES]
            out = jnp.where(high == source, pick(table, low), out)
        out_ref[:, pl.ds(pl.multiple_of(block * LANES, LANES), LANES)] = out
        return 0

    lax.fori_loop(0, BLOCKS, one_block, 0, unroll=2)


def vmem(count):
    return [pl.BlockSpec(memory_space=pltpu.VMEM)] * count


def shape(dims, dtype):
    return jax.ShapeDtypeStruct(dims, dtype)


def params(collective_id=None):
    if collective_id is None:
        return pltpu.CompilerParams(vmem_limit_bytes=VMEM_LIMIT)
    return pltpu.CompilerParams(
        collective_id=collective_id, has_side_effects=True, vmem_limit_bytes=VMEM_LIMIT
    )


def on_device(
    count,
    coords,
    right_sides,
    leaf_order,
    leaf_basis,
    leaf_transfer,
    top_transfer,
    skel_leaf,
    skel_root,
    admissible,
    near_leaves,
    near_count,
):
    levels = count.bit_length() - 1
    low = min(LOW_LEVELS, levels)
    high = max(levels - low, 1)
    order = leaf_order.reshape(BLOCKS, LANES)
    own, rows, vectors, own_skel, skel_rows, root, s_root, times = pl.pallas_call(
        sort_kernel,
        out_shape=(
            shape((LEAVES, LANES, LEAF), BF16),
            shape((QUARTER, LEAF, LANES), BF16),
            shape((REPS, 2 * OWN, 2 * LEAF), BF16),
            shape((LEAVES, LANES, RANK), BF16),
            shape((QUARTER, RANK, LANES), BF16),
            shape((DIM, RANK), BF16),
            shape((OWN, RANK), F32),
            shape((LEAVES, LANES), I32),
        ),
        in_specs=vmem(10),
        out_specs=tuple(vmem(8)),
        scratch_shapes=[
            pltpu.VMEM((BLOCKS, DIM + OWN, LANES), F32),
            pltpu.VMEM((LEAVES, DIM + OWN, LEAF), F32),
        ],
        compiler_params=params(),
        name="sort",
    )(
        coords,
        right_sides,
        order,
        leaf_basis,
        leaf_transfer,
        skel_leaf,
        skel_root,
        admissible,
        near_leaves,
        near_count.reshape(LEAVES, 1),
    )

    tree_scratch = [
        pltpu.VMEM((LOW_LEVELS + 2, DIM, RANK), BF16),
        pltpu.VMEM((LOW_LEVELS + 2, DIM, RANK), BF16),
        pltpu.VMEM((LOW_LEVELS + 2, OWN, RANK), F32),
        pltpu.VMEM((LOW_LEVELS + 2, OWN, RANK), F32),
    ]
    window, window_vectors, up_points, up_s, low_c = pl.pallas_call(
        functools.partial(exchange_kernel, count, levels),
        out_shape=(
            shape((SIDES, QUARTER, LEAF, LANES), BF16),
            shape((SIDES, REPS, 2 * OWN, 2 * LEAF), BF16),
            shape((DIM, RANK), BF16),
            shape((OWN, RANK), F32),
            shape((low, OWN, RANK), F32),
        ),
        in_specs=vmem(5),
        out_specs=tuple(vmem(5)),
        scratch_shapes=tree_scratch
        + [
            pltpu.SemaphoreType.DMA((2, 2)),
            pltpu.SemaphoreType.DMA((SIDES, REPS)),
            pltpu.SemaphoreType.DMA((SIDES, REPS)),
            pltpu.SemaphoreType.DMA((low, 4)),
            pltpu.SemaphoreType.DMA((2,)),
        ],
        compiler_params=params(0),
        name="exchange",
    )(rows, vectors, root, s_root, top_transfer)

    part = pl.pallas_call(
        near_kernel,
        out_shape=shape((REPS, OWN, PTS), F32),
        in_specs=[pl.BlockSpec(memory_space=pltpu.SMEM)] + vmem(6),
        out_specs=pl.BlockSpec(memory_space=pltpu.VMEM),
        scratch_shapes=[
            pltpu.SMEM((LEAVES * PARTNERS + 8,), I32),
            pltpu.VMEM((PARTNERS, RHS, LEAF), BF16),
            pltpu.VMEM((LEAVES, RHS, LEAF), F32),
            pltpu.VMEM((QUARTER, 2 * RHS, RANK), BF16),
            pltpu.VMEM((LEAVES, RHS, RANK), F32),
        ],
        compiler_params=params(),
        name="near",
    )(
        times,
        own,
        window.reshape(PARTNERS, LEAF, LANES),
        window_vectors,
        leaf_basis,
        own_skel,
        skel_rows,
    )

    y_sorted, inverse = pl.pallas_call(
        functools.partial(combine_kernel, levels),
        out_shape=(shape((OWN, PTS), F32), shape((BLOCKS, LANES), I32)),
        in_specs=vmem(8),
        out_specs=tuple(vmem(2)),
        scratch_shapes=[pltpu.VMEM((REPS - 1, OWN, PTS), F32)]
        + tree_scratch
        + [
            pltpu.VMEM((levels, OWN, RANK), F32),
            pltpu.SemaphoreType.DMA((2, REPS - 1)),
            pltpu.SemaphoreType.DMA((high, 4)),
        ],
        compiler_params=params(1),
        name="combine",
    )(part, up_points, up_s, low_c, top_transfer, leaf_basis, leaf_transfer, order)

    return pl.pallas_call(
        unsort_kernel,
        out_shape=shape((OWN, PTS), F32),
        in_specs=vmem(2),
        out_specs=pl.BlockSpec(memory_space=pltpu.VMEM),
        compiler_params=params(),
        name="unsort",
    )(y_sorted, inverse)


def solution(mesh):
    placed = (
        P(None, "leaf"),
        P("rep", "leaf"),
        P("leaf"),
        P("leaf", None, None),
        P("leaf", None, None),
        P(),
        P("leaf", None),
        P("leaf", None),
        P("leaf", None),
        P("leaf", None),
        P("leaf"),
    )
    return jax.shard_map(
        functools.partial(on_device, mesh.shape["leaf"]),
        mesh=mesh,
        in_specs=placed,
        out_specs=P("rep", "leaf"),
        check_vma=False,
    )
```

```python
import functools
import math

import jax
import jax.numpy as jnp
from jax import lax
from jax.experimental import pallas as pl
from jax.experimental.pallas import tpu as pltpu
from jax.sharding import PartitionSpec as P

MESH = pl.DeviceIdType.MESH
F32 = jnp.float32
BF16 = jnp.bfloat16
I32 = jnp.int32

DIM = 64
RANK = 128
LEAF = 256
LEAVES = 16
PTS = 4096
LANES = 128
BLOCKS = PTS // LANES
REPS = 4
QUARTER = LEAVES // REPS
OWN = 8
RHS = 32
SIDES = 3
PARTNERS = SIDES * QUARTER
PHASES = (3, 2, 2)
WAYS = 4
VMEM_LIMIT = 60 * 1024 * 1024
HALF_LOG2E = -0.5 * math.log2(math.e)


def dot_nn(a, b):
    return lax.dot_general(a, b, (((1,), (0,)), ((), ())), preferred_element_type=F32)


def dot_nt(a, b):
    return lax.dot_general(a, b, (((1,), (1,)), ((), ())), preferred_element_type=F32)


def kernel_values(shifted):
    shifted = jnp.maximum(shifted, 1.0)
    return jnp.exp2((shifted * HALF_LOG2E) * lax.rsqrt(shifted))


def split_two(x):
    high = x.astype(BF16)
    return high, (x - high.astype(F32)).astype(BF16)


def stack_two(x):
    high = x.astype(BF16).astype(F32)
    return jnp.concatenate([high, x - high], axis=0).astype(BF16)


def fold_two(x):
    half = x.shape[0] // 2
    return x[:half] + x[half:]


def dot_wide(x, matrix):
    return fold_two(dot_nn(stack_two(x), matrix))


def dot_wide_nt(x, matrix):
    return fold_two(dot_nt(stack_two(x), matrix))


def dot_both_wide(x, matrix):
    rows = stack_two(x)
    high, low = split_two(matrix)
    return fold_two(dot_nn(rows, high)) + fold_two(dot_nn(rows, low))


def with_norms(points, own):
    count = points.shape[1]
    norm = jnp.sum(points * points, axis=0, keepdims=True)
    if own:
        norm = norm + 1.0
    high = norm.astype(BF16).astype(F32)
    rest = norm - high
    mid = rest.astype(BF16).astype(F32)
    low = rest - mid
    row = lax.broadcasted_iota(I32, (16, count), 0)
    if not own:
        row = row - 3
    tail = jnp.where(row == 0, high, jnp.where(row == 1, mid, jnp.where(row == 2, low, 0.0)))
    ones = lax.broadcasted_iota(I32, (16, count), 0) - (3 if own else 0)
    tail = jnp.where((ones >= 0) & (ones < 3), 1.0, tail)
    head = points * -2.0 if own else points
    return jnp.concatenate([head, tail, jnp.zeros((LANES - DIM - 16, count), F32)], axis=0)


def pick(table, lanes):
    return jnp.take_along_axis(table, lanes, axis=1, mode="promise_in_bounds")


def greet_signals(devices):
    barrier = pltpu.get_barrier_semaphore()
    for device in devices:
        pl.semaphore_signal(barrier, inc=1, device_id=device, device_id_type=MESH)


def greet_wait(devices):
    pl.semaphore_wait(pltpu.get_barrier_semaphore(), len(devices))


def remote(source, target, send_sem, recv_sem, device):
    return pltpu.make_async_remote_copy(
        src_ref=source,
        dst_ref=target,
        send_sem=send_sem,
        recv_sem=recv_sem,
        device_id=device,
        device_id_type=MESH,
    )


def phases_of(levels):
    spans, first = [], 0
    for width in PHASES:
        width = min(width, levels - first)
        if width > 0:
            spans.append((first, width))
        first += width
    return spans


def gather_kernel(
    count,
    levels,
    coords_ref,
    rhs_ref,
    order_ref,
    basis_hbm,
    transfer_hbm,
    top_ref,
    skel_root_ref,
    admissible_ref,
    near_ref,
    count_ref,
    window_ref,
    columns_ref,
    window_vectors_ref,
    t_root_ref,
    times_ref,
    inverse_ref,
    raw_ref,
    sorted_ref,
    vectors_ref,
    basis_ref,
    transfer_ref,
    points_ref,
    got_points_ref,
    kernel_ref,
    sibling_ref,
    *rest,
):
    spans = phases_of(levels)
    gathered_refs = rest[: len(spans)]
    spread_sems = rest[len(spans) : 2 * len(spans)]
    row_sems, column_sems, vector_sems, hop_sems, local_sems = rest[2 * len(spans) :]

    leaf = lax.axis_index("leaf")
    rep = lax.axis_index("rep")
    before = lax.rem(leaf + count - 1, count)
    after = lax.rem(leaf + 1, count)
    others = [lax.rem(rep + step, REPS) for step in range(1, REPS)]
    partners = [(side, other) for side in (before, after) for other in [rep] + others]
    partners += [(leaf, other) for other in others]
    for first, width in spans:
        partners += [(leaf ^ (number << first), rep) for number in range(1, 1 << width)]
    greet_signals(partners)

    loads = [
        pltpu.make_async_copy(basis_hbm, basis_ref, local_sems.at[0]),
        pltpu.make_async_copy(transfer_hbm, transfer_ref, local_sems.at[1]),
    ]
    for load in loads:
        load.start()

    def widen(block, _):
        lanes = pl.ds(pl.multiple_of(block * LANES, LANES), LANES)
        raw_ref[block, :DIM, :] = coords_ref[:, lanes].astype(F32)
        raw_ref[block, DIM:, :] = rhs_ref[:, lanes].astype(F32)
        return 0

    lax.fori_loop(0, BLOCKS, widen, 0, unroll=4)

    def gather_rows(positions, first, groups):
        high = positions >> 7
        low = positions & 127
        out = [jnp.zeros((8, LANES), F32)] * groups
        for source in range(BLOCKS):
            here = high == source
            for group in range(groups):
                table = raw_ref[source, first + group * 8 : first + group * 8 + 8, :]
                out[group] = jnp.where(here, pick(table, low), out[group])
        return out

    at = jnp.broadcast_to(skel_root_ref[...], (8, LANES))
    at_high = at >> 7
    at_low = at & 127
    initial = jnp.zeros((8, LANES), I32)
    for source in range(BLOCKS):
        table = jnp.broadcast_to(order_ref[source : source + 1, :], (8, LANES))
        initial = jnp.where(at_high == source, pick(table, at_low), initial)
    points_ref[0] = jnp.concatenate(gather_rows(initial, 0, DIM // 8), axis=0).astype(BF16)
    greet_wait(partners)

    sent = []

    hops = []

    def hop_start(level):
        if level >= levels:
            return
        copy = remote(
            points_ref.at[level],
            got_points_ref.at[level],
            hop_sems.at[0, level],
            hop_sems.at[1, level],
            (leaf ^ (1 << level), rep),
        )
        copy.start()
        hops.append(copy)
        sent.append(copy)

    def hop_finish(level):
        if level >= levels:
            return
        hops[level].wait_recv()
        mine = points_ref[level].astype(F32)
        theirs = got_points_ref[level].astype(F32)
        if level + 1 < levels:
            on_right = lax.rem(leaf // (1 << level), 2) == 1
            points_ref[level + 1] = jnp.where(on_right, theirs, mine).astype(BF16)
            hop_start(level + 1)
        own = with_norms(mine, True).astype(BF16)
        rows = with_norms(theirs, False).T.astype(BF16)
        high, low = split_two(kernel_values(dot_nn(rows, own)))
        kernel_ref[level, 0] = high
        kernel_ref[level, 1] = low

    spreads = []

    def spread_start(phase):
        if phase >= len(spans):
            return
        first, width = spans[phase]
        copies = []
        for number in range(1, 1 << width):
            copy = remote(
                gathered_refs[phase].at[0],
                gathered_refs[phase].at[number],
                spread_sems[phase].at[0, number],
                spread_sems[phase].at[1, number],
                (leaf ^ (number << first), rep),
            )
            copy.start()
            copies.append(copy)
            sent.append(copy)
        spreads.append(copies)

    def spread_finish(phase):
        if phase >= len(spans):
            return
        first, width = spans[phase]
        for copy in spreads[phase]:
            copy.wait_recv()
        nodes = [gathered_refs[phase][number] for number in range(1 << width)]
        for level in range(first, first + width):
            sibling_ref[level] = nodes[1]
            if level + 1 == levels:
                return
            on_right = lax.rem(leaf // (1 << level), 2) == 1
            even = jnp.concatenate(nodes[0::2], axis=0)
            odd = jnp.concatenate(nodes[1::2], axis=0)
            parents = dot_wide(jnp.where(on_right, odd, even), top_ref[level, 0]) + dot_wide(
                jnp.where(on_right, even, odd), top_ref[level, 1]
            )
            nodes = [parents[i * OWN : i * OWN + OWN] for i in range(len(nodes) // 2)]
        gathered_refs[phase + 1][0] = nodes[0]
        spread_start(phase + 1)

    def coupling(level):
        rows = stack_two(sibling_ref[level])
        return fold_two(dot_nn(rows, kernel_ref[level, 0])) + fold_two(dot_nn(rows, kernel_ref[level, 1]))

    hop_start(0)

    def sort_vectors(number, _):
        for half in range(2):
            positions = jnp.broadcast_to(order_ref[pl.ds(number * 2 + half, 1), :], (8, LANES))
            sorted_ref[number, :, half * LANES : half * LANES + LANES] = gather_rows(positions, DIM, 1)[0]
        return 0

    lax.fori_loop(0, LEAVES, sort_vectors, 0)
    for target in range(REPS):
        for column in range(2):
            top = sorted_ref[column * REPS + target]
            bottom = sorted_ref[(column + 2) * REPS + target]
            vectors_ref[target, :, column * LEAF : (column + 1) * LEAF] = jnp.concatenate(
                [top, bottom], axis=0
            ).astype(BF16)
    window_vectors_ref[1, rep] = vectors_ref[rep]
    vector_moves = [
        (index, side, device, step)
        for index, (side, device) in enumerate(((2, before), (0, after), (1, leaf)))
        for step in range(REPS)
        if side != 1 or step > 0
    ]
    for index, side, device, step in vector_moves:
        target = lax.rem(rep + step, REPS)
        copy = remote(
            vectors_ref.at[target],
            window_vectors_ref.at[side, rep],
            vector_sems.at[0, index, step],
            vector_sems.at[1, index, step],
            (device, target),
        )
        copy.start()
        sent.append(copy)

    hop_finish(0)

    for load in loads:
        load.wait()

    def up(number, total):
        s_leaf = dot_nn(sorted_ref[number].astype(BF16), basis_ref[number])
        return total + dot_nn(stack_two(s_leaf), transfer_ref[number])

    s_root = fold_two(lax.fori_loop(0, LEAVES, up, jnp.zeros((2 * OWN, RANK), F32), unroll=8))
    gathered_refs[0][0] = s_root
    spread_start(0)
    hop_finish(1)

    row_copies = []

    def sort_points(k):
        number = k * REPS + rep
        for half in range(2):
            span = slice(half * LANES, half * LANES + LANES)
            positions = jnp.broadcast_to(order_ref[pl.ds(number * 2 + half, 1), :], (8, LANES))
            points = jnp.concatenate(gather_rows(positions, 0, DIM // 8), axis=0)
            columns_ref[rep, k, :, span] = points.astype(BF16)
            window_ref[1, k, span, :] = with_norms(points, False).T.astype(BF16)
        for index, (side, device) in enumerate(((2, before), (0, after))):
            copy = remote(
                window_ref.at[1, k],
                window_ref.at[side, k],
                row_sems.at[0, k, index],
                row_sems.at[1, k, index],
                (device, rep),
            )
            copy.start()
            row_copies.append(copy)
            sent.append(copy)
        for step, other in enumerate(others):
            copy = remote(
                columns_ref.at[rep, k],
                columns_ref.at[rep, k],
                column_sems.at[0, k, step],
                column_sems.at[1, k, step],
                (leaf, other),
            )
            copy.start()
            sent.append(copy)

    sort_points(0)
    sort_points(1)
    hop_finish(2)
    spread_finish(0)
    sort_points(2)
    sort_points(3)
    hop_finish(3)
    spread_finish(1)

    diagonal = lax.broadcasted_iota(I32, (LEAVES, LEAVES), 0) == lax.broadcasted_iota(
        I32, (LEAVES, LEAVES), 1
    )

    def as_column(row):
        return jnp.sum(jnp.where(diagonal, row, 0.0), axis=1, keepdims=True)

    near = near_ref[...]
    slot = lax.broadcasted_iota(I32, near.shape, 1)
    live = slot.astype(F32) < as_column(count_ref[...].astype(F32))
    admissible = admissible_ref[...]
    lane = lax.broadcasted_iota(I32, (LEAVES, LANES), 1)
    times = jnp.zeros((LEAVES, LANES), F32)
    for entry in range(PARTNERS + QUARTER):
        if entry < PARTNERS:
            named = jnp.where(near == entry * REPS + rep, 1.0, 0.0)
            total = jnp.sum(jnp.where(live, named, 0.0), axis=1, keepdims=True)
        else:
            named = jnp.where(admissible == (entry - PARTNERS) * REPS + rep, 1.0, 0.0)
            total = as_column(jnp.sum(named, axis=0, keepdims=True))
        times = jnp.where(lane == entry, total, times)
    times_ref[...] = times.astype(I32)

    lane = lax.broadcasted_iota(I32, (1, LANES), 1)

    def invert(block, sums):
        positions = order_ref[pl.ds(block, 1), :]
        row = lax.broadcasted_iota(I32, (BLOCKS, LANES), 0)
        column = lax.broadcasted_iota(I32, (LANES, LANES), 0)
        is_row = row == (positions >> 7)
        is_column = jnp.where(column == (positions & 127), 1.0, 0.0).astype(BF16)
        marks = jnp.concatenate(
            [
                jnp.where(is_row, block.astype(F32), 0.0),
                jnp.where(is_row, lane.astype(F32), 0.0),
            ],
            axis=0,
        ).astype(BF16)
        return sums + dot_nt(marks, is_column)

    sums = lax.fori_loop(0, BLOCKS // 2, invert, jnp.zeros((2 * BLOCKS, LANES), F32), unroll=4)
    hop_finish(4)
    spread_finish(2)
    sums = lax.fori_loop(BLOCKS // 2, BLOCKS, invert, sums, unroll=4)
    inverse_ref[...] = (sums[:BLOCKS] * float(LANES) + sums[BLOCKS:]).astype(I32)
    hop_finish(5)
    hop_finish(6)

    running = coupling(levels - 1)
    for level in range(levels - 2, -1, -1):
        side = lax.rem(leaf // (1 << level), 2)
        running = coupling(level) + dot_wide_nt(running, top_ref[level, side])
    t_root_ref[...] = running

    for copy in row_copies:
        copy.wait_recv()
    for k in range(QUARTER):
        for step, other in enumerate(others):
            source = lax.rem(rep + REPS - 1 - step, REPS)
            remote(
                columns_ref.at[rep, k],
                columns_ref.at[source, k],
                column_sems.at[0, k, step],
                column_sems.at[1, k, step],
                (leaf, other),
            ).wait_recv()
    for index, side, device, step in vector_moves:
        source = lax.rem(rep + REPS - step, REPS)
        remote(
            vectors_ref.at[rep],
            window_vectors_ref.at[side, source],
            vector_sems.at[0, index, step],
            vector_sems.at[1, index, step],
            (device, lax.rem(rep + step, REPS)),
        ).wait_recv()
    for copy in sent:
        copy.wait_send()


def near_kernel(
    times_ref,
    columns_ref,
    window_ref,
    window_vectors_ref,
    basis_ref,
    transfer_ref,
    skel_leaf_ref,
    t_root_ref,
    out_ref,
    list_ref,
    own_ref,
    own_skel_ref,
    skel_rows_ref,
    vectors_ref,
    total_ref,
    s_ref,
    t_ref,
):
    rep = lax.axis_index("rep")
    root_rows = stack_two(t_root_ref[...])
    t_ref[...] = jnp.zeros_like(t_ref)

    def prepare(leaf, _):
        source = lax.rem(leaf, REPS)
        k = leaf // REPS
        points = columns_ref[source, k].astype(F32)
        columns = with_norms(points, True)
        own_ref[leaf] = columns.astype(BF16)
        positions = jnp.broadcast_to(skel_leaf_ref[pl.ds(leaf, 1), :], (8, LANES))
        high = positions >> 7
        low = positions & 127
        parts = []
        for group in range(DIM // 8):
            span = slice(group * 8, group * 8 + 8)
            left = pick(points[span, :LANES], low)
            right = pick(points[span, LANES:], low)
            parts.append(jnp.where(high == 0, left, right))
        own_skel_ref[leaf] = with_norms(jnp.concatenate(parts, axis=0), True).astype(BF16)
        t_ref[leaf, pl.ds(pl.multiple_of(rep * OWN, OWN), OWN), :] = fold_two(
            dot_nt(root_rows, transfer_ref[leaf])
        )
        return 0

    lax.fori_loop(0, LEAVES, prepare, 0, unroll=2)

    for side in range(SIDES):
        for column in range(2):
            span = slice(column * LEAF, (column + 1) * LEAF)
            blocks = [window_vectors_ref[side, source, :, span].astype(F32) for source in range(REPS)]
            vectors_ref[side * QUARTER + column] = jnp.concatenate(
                [block[:OWN] for block in blocks], axis=0
            ).astype(BF16)
            vectors_ref[side * QUARTER + column + 2] = jnp.concatenate(
                [block[OWN:] for block in blocks], axis=0
            ).astype(BF16)
    for k in range(QUARTER):
        leaf = k * REPS + rep
        s_leaf = dot_nn(vectors_ref[QUARTER + k], basis_ref[leaf])
        s_ref[k] = stack_two(s_leaf)
        skel = own_skel_ref[leaf].astype(F32)
        skel_rows_ref[k] = with_norms(skel[:DIM] * -0.5, False).T.astype(BF16)

    total_ref[...] = jnp.zeros_like(total_ref)

    def make_list(first, width):
        def one_leaf(leaf, filled):
            for entry in range(first, first + width):
                list_ref[filled] = leaf * 16 + entry
                filled = filled + jnp.where(times_ref[leaf, entry] > 0, 1, 0)
            return filled

        filled = lax.fori_loop(0, LEAVES, one_leaf, 0)
        for way in range(WAYS):
            list_ref[filled + way] = first
        return filled

    def scale_of(number, filled, code):
        times = times_ref[code // 16, lax.rem(code, 16)]
        return jnp.where(number < filled, times, 0).astype(F32)

    filled = make_list(0, PARTNERS)

    def near_group(group, _):
        terms = []
        for way in range(WAYS):
            number = group * WAYS + way
            code = list_ref[number]
            leaf = code // 16
            entry = lax.rem(code, 16)
            shifted = dot_nn(window_ref[entry], own_ref[leaf])
            tile = kernel_values(shifted).astype(BF16)
            terms.append((leaf, dot_nn(vectors_ref[entry], tile) * scale_of(number, filled, code)))
        for leaf, term in terms:
            total_ref[leaf] += term
        return 0

    lax.fori_loop(0, (filled + WAYS - 1) // WAYS, near_group, 0)

    filled_far = make_list(PARTNERS, QUARTER)

    def far_group(group, _):
        terms = []
        for way in range(WAYS):
            number = group * WAYS + way
            code = list_ref[number]
            leaf = code // 16
            entry = lax.rem(code, 16) - PARTNERS
            shifted = dot_nn(skel_rows_ref[entry], own_skel_ref[leaf])
            high, low = split_two(kernel_values(shifted))
            term = fold_two(dot_nn(s_ref[entry], high)) + dot_nn(s_ref[entry, :RHS], low)
            terms.append((leaf, term * scale_of(number, filled_far, code)))
        for leaf, term in terms:
            t_ref[leaf] += term
        return 0

    lax.fori_loop(0, (filled_far + WAYS - 1) // WAYS, far_group, 0)

    for leaf in range(LEAVES):
        far = dot_wide_nt(t_ref[leaf], basis_ref[leaf])
        out_ref[:, :, leaf * LEAF : (leaf + 1) * LEAF] = (total_ref[leaf] + far).reshape(REPS, OWN, LEAF)


def combine_kernel(part_ref, inverse_ref, out_ref, got_ref, total_ref, sems):
    leaf = lax.axis_index("leaf")
    rep = lax.axis_index("rep")
    partners = [(leaf, lax.rem(rep + step, REPS)) for step in range(1, REPS)]
    greet_signals(partners)
    greet_wait(partners)
    copies = []
    for index, partner in enumerate(partners):
        copy = remote(
            part_ref.at[partner[1]], got_ref.at[index], sems.at[0, index], sems.at[1, index], partner
        )
        copy.start()
        copies.append(copy)
    for copy in copies:
        copy.wait()
    total_ref[...] = ((part_ref[rep] + got_ref[0]) + got_ref[1]) + got_ref[2]

    def one_block(block, _):
        positions = jnp.broadcast_to(inverse_ref[pl.ds(block, 1), :], (OWN, LANES))
        high = positions >> 7
        low = positions & 127
        out = jnp.zeros((OWN, LANES), F32)
        for source in range(BLOCKS):
            table = total_ref[:, source * LANES : (source + 1) * LANES]
            out = jnp.where(high == source, pick(table, low), out)
        out_ref[:, pl.ds(pl.multiple_of(block * LANES, LANES), LANES)] = out
        return 0

    lax.fori_loop(0, BLOCKS, one_block, 0, unroll=4)


def vmem(count):
    return [pl.BlockSpec(memory_space=pltpu.VMEM)] * count


def anywhere(count):
    return [pl.BlockSpec(memory_space=pl.ANY)] * count


def shape(dims, dtype):
    return jax.ShapeDtypeStruct(dims, dtype)


def params(collective_id=None):
    if collective_id is None:
        return pltpu.CompilerParams(vmem_limit_bytes=VMEM_LIMIT)
    return pltpu.CompilerParams(
        collective_id=collective_id, has_side_effects=True, vmem_limit_bytes=VMEM_LIMIT
    )


def on_device(
    count,
    coords,
    right_sides,
    leaf_order,
    leaf_basis,
    leaf_transfer,
    top_transfer,
    skel_leaf,
    skel_root,
    admissible,
    near_leaves,
    near_count,
):
    levels = count.bit_length() - 1
    spans = phases_of(levels)
    dma = pltpu.SemaphoreType.DMA
    window, columns, window_vectors, t_root, times, inverse = pl.pallas_call(
        functools.partial(gather_kernel, count, levels),
        out_shape=(
            shape((SIDES, QUARTER, LEAF, LANES), BF16),
            shape((REPS, QUARTER, DIM, LEAF), BF16),
            shape((SIDES, REPS, 2 * OWN, 2 * LEAF), BF16),
            shape((OWN, RANK), F32),
            shape((LEAVES, LANES), I32),
            shape((BLOCKS, LANES), I32),
        ),
        in_specs=vmem(3) + anywhere(2) + vmem(5),
        out_specs=tuple(vmem(6)),
        scratch_shapes=[
            pltpu.VMEM((BLOCKS, DIM + OWN, LANES), F32),
            pltpu.VMEM((LEAVES, OWN, LEAF), F32),
            pltpu.VMEM((REPS, 2 * OWN, 2 * LEAF), BF16),
            pltpu.VMEM((LEAVES, LEAF, RANK), BF16),
            pltpu.VMEM((LEAVES, RANK, RANK), BF16),
            pltpu.VMEM((levels, DIM, RANK), BF16),
            pltpu.VMEM((levels, DIM, RANK), BF16),
            pltpu.VMEM((levels, 2, RANK, RANK), BF16),
            pltpu.VMEM((levels, OWN, RANK), F32),
        ]
        + [pltpu.VMEM((1 << width, OWN, RANK), F32) for _, width in spans]
        + [dma((2, 1 << width)) for _, width in spans]
        + [
            dma((2, QUARTER, 2)),
            dma((2, QUARTER, REPS - 1)),
            dma((2, SIDES, REPS)),
            dma((2, levels)),
            dma((2,)),
        ],
        compiler_params=params(0),
        name="gather",
    )(
        coords,
        right_sides,
        leaf_order.reshape(BLOCKS, LANES),
        leaf_basis,
        leaf_transfer,
        top_transfer,
        skel_root,
        admissible.T,
        near_leaves,
        near_count.reshape(1, LEAVES),
    )

    part = pl.pallas_call(
        near_kernel,
        out_shape=shape((REPS, OWN, PTS), F32),
        in_specs=[pl.BlockSpec(memory_space=pltpu.SMEM)] + vmem(7),
        out_specs=pl.BlockSpec(memory_space=pltpu.VMEM),
        scratch_shapes=[
            pltpu.SMEM((LEAVES * PARTNERS + 2 * WAYS,), I32),
            pltpu.VMEM((LEAVES, LANES, LEAF), BF16),
            pltpu.VMEM((LEAVES, LANES, RANK), BF16),
            pltpu.VMEM((QUARTER, RANK, LANES), BF16),
            pltpu.VMEM((PARTNERS, RHS, LEAF), BF16),
            pltpu.VMEM((LEAVES, RHS, LEAF), F32),
            pltpu.VMEM((QUARTER, 2 * RHS, RANK), BF16),
            pltpu.VMEM((LEAVES, RHS, RANK), F32),
        ],
        compiler_params=params(),
        name="near",
    )(
        times,
        columns,
        window.reshape(PARTNERS, LEAF, LANES),
        window_vectors,
        leaf_basis,
        leaf_transfer,
        skel_leaf,
        t_root,
    )

    return pl.pallas_call(
        combine_kernel,
        out_shape=shape((OWN, PTS), F32),
        in_specs=vmem(2),
        out_specs=pl.BlockSpec(memory_space=pltpu.VMEM),
        scratch_shapes=[
            pltpu.VMEM((REPS - 1, OWN, PTS), F32),
            pltpu.VMEM((OWN, PTS), F32),
            dma((2, REPS - 1)),
        ],
        compiler_params=params(1),
        name="combine",
    )(part, inverse)


def solution(mesh):
    placed = (
        P(None, "leaf"),
        P("rep", "leaf"),
        P("leaf"),
        P("leaf", None, None),
        P("leaf", None, None),
        P(),
        P("leaf", None),
        P("leaf", None),
        P("leaf", None),
        P("leaf", None),
        P("leaf"),
    )
    return jax.shard_map(
        functools.partial(on_device, mesh.shape["leaf"]),
        mesh=mesh,
        in_specs=placed,
        out_specs=P("rep", "leaf"),
        check_vma=False,
    )
```

```python
import functools

import jax
import jax.numpy as jnp
from jax import lax
from jax.experimental import pallas as pl
from jax.experimental.pallas import tpu as pltpu
from jax.sharding import PartitionSpec as P

MESH = pl.DeviceIdType.MESH
F32 = jnp.float32
BF16 = jnp.bfloat16
I32 = jnp.int32

DIM = 64
RANK = 128
LEAF = 256
LEAVES = 16
PTS = 4096
LANES = 128
BLOCKS = PTS // LANES
REPS = 4
QUARTER = LEAVES // REPS
OWN = 8
RHS = 32
SIDES = 3
PARTNERS = SIDES * QUARTER
PHASES = (3, 2, 2)
WAYS = 2
VMEM_LIMIT = 60 * 1024 * 1024


def dot_nn(a, b):
    return lax.dot_general(a, b, (((1,), (0,)), ((), ())), preferred_element_type=F32)


def dot_nt(a, b):
    return lax.dot_general(a, b, (((1,), (1,)), ((), ())), preferred_element_type=F32)


def kernel_values(shifted):
    shifted = jnp.maximum(shifted, 1.0)
    return jnp.exp((shifted * -0.5) * lax.rsqrt(shifted))


def split_two(x):
    high = x.astype(BF16)
    return high, (x - high.astype(F32)).astype(BF16)


def stack_two(x):
    high = x.astype(BF16).astype(F32)
    return jnp.concatenate([high, x - high], axis=0).astype(BF16)


def fold_two(x):
    half = x.shape[0] // 2
    return x[:half] + x[half:]


def dot_wide(x, matrix):
    return fold_two(dot_nn(stack_two(x), matrix))


def dot_wide_nt(x, matrix):
    return fold_two(dot_nt(stack_two(x), matrix))


def dot_both_wide(x, matrix):
    rows = stack_two(x)
    high, low = split_two(matrix)
    return fold_two(dot_nn(rows, high)) + fold_two(dot_nn(rows, low))


def with_norms(points, own):
    count = points.shape[1]
    norm = jnp.sum(points * points, axis=0, keepdims=True)
    if own:
        norm = norm + 1.0
    high = norm.astype(BF16).astype(F32)
    rest = norm - high
    mid = rest.astype(BF16).astype(F32)
    low = rest - mid
    row = lax.broadcasted_iota(I32, (16, count), 0)
    if not own:
        row = row - 3
    tail = jnp.where(row == 0, high, jnp.where(row == 1, mid, jnp.where(row == 2, low, 0.0)))
    ones = lax.broadcasted_iota(I32, (16, count), 0) - (3 if own else 0)
    tail = jnp.where((ones >= 0) & (ones < 3), 1.0, tail)
    head = points * -2.0 if own else points
    return jnp.concatenate([head, tail, jnp.zeros((LANES - DIM - 16, count), F32)], axis=0)


def pick(table, lanes):
    return jnp.take_along_axis(table, lanes, axis=1, mode="promise_in_bounds")


def greet_signals(devices):
    barrier = pltpu.get_barrier_semaphore()
    for device in devices:
        pl.semaphore_signal(barrier, inc=1, device_id=device, device_id_type=MESH)


def greet_wait(devices):
    pl.semaphore_wait(pltpu.get_barrier_semaphore(), len(devices))


def remote(source, target, send_sem, recv_sem, device):
    return pltpu.make_async_remote_copy(
        src_ref=source,
        dst_ref=target,
        send_sem=send_sem,
        recv_sem=recv_sem,
        device_id=device,
        device_id_type=MESH,
    )


def phases_of(levels):
    spans, first = [], 0
    for width in PHASES:
        width = min(width, levels - first)
        if width > 0:
            spans.append((first, width))
        first += width
    return spans


def gather_kernel(
    count,
    levels,
    coords_ref,
    rhs_ref,
    order_ref,
    basis_hbm,
    transfer_hbm,
    top_ref,
    skel_root_ref,
    admissible_ref,
    near_ref,
    count_ref,
    window_ref,
    columns_ref,
    window_vectors_ref,
    t_root_ref,
    times_ref,
    inverse_ref,
    raw_ref,
    sorted_ref,
    vectors_ref,
    basis_ref,
    transfer_ref,
    points_ref,
    got_points_ref,
    kernel_ref,
    sibling_ref,
    *rest,
):
    spans = phases_of(levels)
    gathered_refs = rest[: len(spans)]
    spread_sems = rest[len(spans) : 2 * len(spans)]
    row_sems, column_sems, vector_sems, push_sems, local_sems = rest[2 * len(spans) :]

    leaf = lax.axis_index("leaf")
    rep = lax.axis_index("rep")
    before = lax.rem(leaf + count - 1, count)
    after = lax.rem(leaf + 1, count)
    others = [lax.rem(rep + step, REPS) for step in range(1, REPS)]
    partners = [(side, other) for side in (before, after) for other in [rep] + others]
    partners += [(leaf, other) for other in others]
    for first, width in spans:
        partners += [(leaf ^ (number << first), rep) for number in range(1, 1 << width)]
    greet_signals(partners)

    loads = [
        pltpu.make_async_copy(basis_hbm, basis_ref, local_sems.at[0]),
        pltpu.make_async_copy(transfer_hbm, transfer_ref, local_sems.at[1]),
    ]
    for load in loads:
        load.start()

    def widen(block, _):
        lanes = pl.ds(pl.multiple_of(block * LANES, LANES), LANES)
        raw_ref[block, :DIM, :] = coords_ref[:, lanes].astype(F32)
        raw_ref[block, DIM:, :] = rhs_ref[:, lanes].astype(F32)
        return 0

    lax.fori_loop(0, BLOCKS, widen, 0, unroll=4)

    def gather_rows(positions, first, groups):
        high = positions >> 7
        low = positions & 127
        out = [jnp.zeros((8, LANES), F32)] * groups
        for source in range(BLOCKS):
            here = high == source
            for group in range(groups):
                table = raw_ref[source, first + group * 8 : first + group * 8 + 8, :]
                out[group] = jnp.where(here, pick(table, low), out[group])
        return out

    at = jnp.broadcast_to(skel_root_ref[...], (8, LANES))
    at_high = at >> 7
    at_low = at & 127
    initial = jnp.zeros((8, LANES), I32)
    for source in range(BLOCKS):
        table = jnp.broadcast_to(order_ref[source : source + 1, :], (8, LANES))
        initial = jnp.where(at_high == source, pick(table, at_low), initial)
    points_ref[0] = jnp.concatenate(gather_rows(initial, 0, DIM // 8), axis=0).astype(BF16)
    greet_wait(partners)

    sent = []

    pushes = [[] for _ in spans]

    def push_start(phase):
        if phase >= len(spans):
            return
        first, width = spans[phase]
        for level in range(first, first + width):
            for number in range(1 << (level - first), 2 << (level - first)):
                copy = remote(
                    points_ref.at[first],
                    got_points_ref.at[level],
                    push_sems.at[0, level, number - (1 << (level - first))],
                    push_sems.at[1, level, 0],
                    (leaf ^ (number << first), rep),
                )
                pushes[phase].append((level, copy))
                if level == first:
                    copy.start()
                else:
                    pl.when(lax.rem(leaf // (1 << first), 1 << (level - first)) == 0)(copy.start)

    def push_finish(phase):
        if phase >= len(spans):
            return
        first, width = spans[phase]
        for level in range(first, first + width):
            [copy for at, copy in pushes[phase] if at == level][0].wait_recv()
            if level + 1 < levels:
                on_right = lax.rem(leaf // (1 << level), 2) == 1
                points_ref[level + 1] = jnp.where(
                    on_right, got_points_ref[level].astype(F32), points_ref[level].astype(F32)
                ).astype(BF16)
        push_start(phase + 1)

    def push_wait_send():
        for (first, width), copies in zip(spans, pushes):
            for level, copy in copies:
                if level == first:
                    copy.wait_send()
                else:
                    pl.when(lax.rem(leaf // (1 << first), 1 << (level - first)) == 0)(copy.wait_send)

    def kernels(phase):
        if phase >= len(spans):
            return
        first, width = spans[phase]
        values = []
        for level in range(first, first + width):
            own = with_norms(points_ref[level].astype(F32), True).astype(BF16)
            rows = with_norms(got_points_ref[level].astype(F32), False).T.astype(BF16)
            values.append(split_two(kernel_values(dot_nn(rows, own))))
        for level, (high, low) in zip(range(first, first + width), values):
            kernel_ref[level, 0] = high
            kernel_ref[level, 1] = low

    spreads = []

    def spread_start(phase):
        if phase >= len(spans):
            return
        first, width = spans[phase]
        copies = []
        for number in range(1, 1 << width):
            copy = remote(
                gathered_refs[phase].at[0],
                gathered_refs[phase].at[number],
                spread_sems[phase].at[0, number],
                spread_sems[phase].at[1, number],
                (leaf ^ (number << first), rep),
            )
            copy.start()
            copies.append(copy)
            sent.append(copy)
        spreads.append(copies)

    def spread_finish(phase):
        if phase >= len(spans):
            return
        first, width = spans[phase]
        for copy in spreads[phase]:
            copy.wait_recv()
        nodes = [gathered_refs[phase][number] for number in range(1 << width)]
        for level in range(first, first + width):
            sibling_ref[level] = nodes[1]
            if level + 1 == levels:
                return
            on_right = lax.rem(leaf // (1 << level), 2) == 1
            even = jnp.concatenate(nodes[0::2], axis=0)
            odd = jnp.concatenate(nodes[1::2], axis=0)
            parents = dot_wide(jnp.where(on_right, odd, even), top_ref[level, 0]) + dot_wide(
                jnp.where(on_right, even, odd), top_ref[level, 1]
            )
            nodes = [parents[i * OWN : i * OWN + OWN] for i in range(len(nodes) // 2)]
        gathered_refs[phase + 1][0] = nodes[0]
        spread_start(phase + 1)

    def coupling(level):
        rows = stack_two(sibling_ref[level])
        return fold_two(dot_nn(rows, kernel_ref[level, 0])) + fold_two(dot_nn(rows, kernel_ref[level, 1]))

    push_start(0)

    def sort_vectors(number, _):
        for half in range(2):
            positions = jnp.broadcast_to(order_ref[pl.ds(number * 2 + half, 1), :], (8, LANES))
            sorted_ref[number, :, half * LANES : half * LANES + LANES] = gather_rows(positions, DIM, 1)[0]
        return 0

    lax.fori_loop(0, LEAVES, sort_vectors, 0)
    for target in range(REPS):
        for column in range(2):
            top = sorted_ref[column * REPS + target]
            bottom = sorted_ref[(column + 2) * REPS + target]
            vectors_ref[target, :, column * LEAF : (column + 1) * LEAF] = jnp.concatenate(
                [top, bottom], axis=0
            ).astype(BF16)
    window_vectors_ref[1, rep] = vectors_ref[rep]
    vector_moves = [
        (index, side, device, step)
        for index, (side, device) in enumerate(((2, before), (0, after), (1, leaf)))
        for step in range(REPS)
        if side != 1 or step > 0
    ]
    for index, side, device, step in vector_moves:
        target = lax.rem(rep + step, REPS)
        copy = remote(
            vectors_ref.at[target],
            window_vectors_ref.at[side, rep],
            vector_sems.at[0, index, step],
            vector_sems.at[1, index, step],
            (device, target),
        )
        copy.start()
        sent.append(copy)

    for load in loads:
        load.wait()

    def up(number, total):
        s_leaf = dot_nn(sorted_ref[number].astype(BF16), basis_ref[number])
        return total + dot_nn(stack_two(s_leaf), transfer_ref[number])

    s_root = fold_two(lax.fori_loop(0, LEAVES, up, jnp.zeros((2 * OWN, RANK), F32), unroll=8))
    gathered_refs[0][0] = s_root
    spread_start(0)

    row_copies = []

    def sort_points(k):
        number = k * REPS + rep
        for half in range(2):
            span = slice(half * LANES, half * LANES + LANES)
            positions = jnp.broadcast_to(order_ref[pl.ds(number * 2 + half, 1), :], (8, LANES))
            points = jnp.concatenate(gather_rows(positions, 0, DIM // 8), axis=0)
            columns_ref[rep, k, :, span] = points.astype(BF16)
            window_ref[1, k, span, :] = with_norms(points, False).T.astype(BF16)
        for index, (side, device) in enumerate(((2, before), (0, after))):
            copy = remote(
                window_ref.at[1, k],
                window_ref.at[side, k],
                row_sems.at[0, k, index],
                row_sems.at[1, k, index],
                (device, rep),
            )
            copy.start()
            row_copies.append(copy)
            sent.append(copy)
        for step, other in enumerate(others):
            copy = remote(
                columns_ref.at[rep, k],
                columns_ref.at[rep, k],
                column_sems.at[0, k, step],
                column_sems.at[1, k, step],
                (leaf, other),
            )
            copy.start()
            sent.append(copy)

    sort_points(0)
    sort_points(1)
    push_finish(0)
    spread_finish(0)
    sort_points(2)
    sort_points(3)
    push_finish(1)
    spread_finish(1)
    kernels(0)
    kernels(1)

    diagonal = lax.broadcasted_iota(I32, (LEAVES, LEAVES), 0) == lax.broadcasted_iota(
        I32, (LEAVES, LEAVES), 1
    )

    def as_column(row):
        return jnp.sum(jnp.where(diagonal, row, 0.0), axis=1, keepdims=True)

    near = near_ref[...]
    slot = lax.broadcasted_iota(I32, near.shape, 1)
    live = slot.astype(F32) < as_column(count_ref[...].astype(F32))
    admissible = admissible_ref[...]
    lane = lax.broadcasted_iota(I32, (LEAVES, LANES), 1)
    times = jnp.zeros((LEAVES, LANES), F32)
    for entry in range(PARTNERS + QUARTER):
        if entry < PARTNERS:
            named = jnp.where(near == entry * REPS + rep, 1.0, 0.0)
            total = jnp.sum(jnp.where(live, named, 0.0), axis=1, keepdims=True)
        else:
            named = jnp.where(admissible == (entry - PARTNERS) * REPS + rep, 1.0, 0.0)
            total = as_column(jnp.sum(named, axis=0, keepdims=True))
        times = jnp.where(lane == entry, total, times)
    times_ref[...] = times.astype(I32)

    lane = lax.broadcasted_iota(I32, (1, LANES), 1)

    def invert(block, sums):
        positions = order_ref[pl.ds(block, 1), :]
        row = lax.broadcasted_iota(I32, (BLOCKS, LANES), 0)
        column = lax.broadcasted_iota(I32, (LANES, LANES), 0)
        is_row = row == (positions >> 7)
        is_column = jnp.where(column == (positions & 127), 1.0, 0.0).astype(BF16)
        marks = jnp.concatenate(
            [
                jnp.where(is_row, block.astype(F32), 0.0),
                jnp.where(is_row, lane.astype(F32), 0.0),
            ],
            axis=0,
        ).astype(BF16)
        return sums + dot_nt(marks, is_column)

    sums = lax.fori_loop(0, BLOCKS, invert, jnp.zeros((2 * BLOCKS, LANES), F32), unroll=4)
    inverse_ref[...] = (sums[:BLOCKS] * float(LANES) + sums[BLOCKS:]).astype(I32)
    push_finish(2)
    spread_finish(2)
    kernels(2)

    running = coupling(levels - 1)
    for level in range(levels - 2, -1, -1):
        side = lax.rem(leaf // (1 << level), 2)
        running = coupling(level) + dot_wide_nt(running, top_ref[level, side])
    t_root_ref[...] = running

    for copy in row_copies:
        copy.wait_recv()
    for k in range(QUARTER):
        for step, other in enumerate(others):
            source = lax.rem(rep + REPS - 1 - step, REPS)
            remote(
                columns_ref.at[rep, k],
                columns_ref.at[source, k],
                column_sems.at[0, k, step],
                column_sems.at[1, k, step],
                (leaf, other),
            ).wait_recv()
    for index, side, device, step in vector_moves:
        source = lax.rem(rep + REPS - step, REPS)
        remote(
            vectors_ref.at[rep],
            window_vectors_ref.at[side, source],
            vector_sems.at[0, index, step],
            vector_sems.at[1, index, step],
            (device, lax.rem(rep + step, REPS)),
        ).wait_recv()
    for copy in sent:
        copy.wait_send()
    push_wait_send()


def near_kernel(
    times_ref,
    columns_ref,
    window_ref,
    window_vectors_ref,
    basis_ref,
    transfer_ref,
    skel_leaf_ref,
    t_root_ref,
    out_ref,
    own_out_ref,
    list_ref,
    own_ref,
    own_skel_ref,
    skel_rows_ref,
    vectors_ref,
    total_ref,
    s_ref,
    t_ref,
    near_shifted_even,
    near_shifted_odd,
    near_even,
    near_odd,
    far_shifted_even,
    far_shifted_odd,
    far_even,
    far_odd,
):
    near_shifted, near_tiles = (near_shifted_even, near_shifted_odd), (near_even, near_odd)
    far_shifted, far_tiles = (far_shifted_even, far_shifted_odd), (far_even, far_odd)
    rep = lax.axis_index("rep")
    root_rows = stack_two(t_root_ref[...])
    t_ref[...] = jnp.zeros_like(t_ref)

    def prepare(leaf, _):
        source = lax.rem(leaf, REPS)
        k = leaf // REPS
        points = columns_ref[source, k].astype(F32)
        columns = with_norms(points, True)
        own_ref[leaf] = columns.astype(BF16)
        positions = jnp.broadcast_to(skel_leaf_ref[pl.ds(leaf, 1), :], (8, LANES))
        high = positions >> 7
        low = positions & 127
        parts = []
        for group in range(DIM // 8):
            span = slice(group * 8, group * 8 + 8)
            left = pick(points[span, :LANES], low)
            right = pick(points[span, LANES:], low)
            parts.append(jnp.where(high == 0, left, right))
        own_skel_ref[leaf] = with_norms(jnp.concatenate(parts, axis=0), True).astype(BF16)
        t_ref[leaf, pl.ds(pl.multiple_of(rep * OWN, OWN), OWN), :] = fold_two(
            dot_nt(root_rows, transfer_ref[leaf])
        )
        return 0

    lax.fori_loop(0, LEAVES, prepare, 0, unroll=4)

    for side in range(SIDES):
        for column in range(2):
            span = slice(column * LEAF, (column + 1) * LEAF)
            blocks = [window_vectors_ref[side, source, :, span].astype(F32) for source in range(REPS)]
            vectors_ref[side * QUARTER + column] = jnp.concatenate(
                [block[:OWN] for block in blocks], axis=0
            ).astype(BF16)
            vectors_ref[side * QUARTER + column + 2] = jnp.concatenate(
                [block[OWN:] for block in blocks], axis=0
            ).astype(BF16)
    for k in range(QUARTER):
        leaf = k * REPS + rep
        s_leaf = dot_nn(vectors_ref[QUARTER + k], basis_ref[leaf])
        s_ref[k] = stack_two(s_leaf)
        skel = own_skel_ref[leaf].astype(F32)
        skel_rows_ref[k] = with_norms(skel[:DIM] * -0.5, False).T.astype(BF16)

    total_ref[...] = jnp.zeros_like(total_ref)

    def make_list(first, width):
        def one_leaf(leaf, filled):
            for entry in range(first, first + width):
                list_ref[filled] = leaf * 16 + entry
                filled = filled + jnp.where(times_ref[leaf, entry] > 0, 1, 0)
            return filled

        filled = lax.fori_loop(0, LEAVES, one_leaf, 0, unroll=2)
        for pad in range(4 * WAYS):
            list_ref[filled + pad] = first
        return filled

    def run(filled, product, keep, apply, shifted_refs, tile_refs):
        def start(group, shifted_ref):
            for way in range(WAYS):
                code = list_ref[group * WAYS + way]
                shifted_ref[way] = product(code >> 4, code & 15)

        def middle(shifted_ref, tile_ref):
            for way in range(WAYS):
                keep(tile_ref, way, kernel_values(shifted_ref[way]))

        def finish(group, tile_ref):
            for way in range(WAYS):
                number = group * WAYS + way
                code = list_ref[jnp.maximum(number, 0)]
                leaf, entry = code >> 4, code & 15
                times = jnp.where((number >= 0) & (number < filled), times_ref[leaf, entry], 0)
                apply(leaf, entry, times.astype(F32), tile_ref, way)

        start(0, shifted_refs[0])
        tile_refs[1][...] = jnp.zeros_like(tile_refs[1])

        def step(number, _):
            even = number * 2
            start(even + 1, shifted_refs[1])
            middle(shifted_refs[0], tile_refs[0])
            finish(even - 1, tile_refs[1])
            start(even + 2, shifted_refs[0])
            middle(shifted_refs[1], tile_refs[1])
            finish(even, tile_refs[0])
            return 0

        steps = (filled + 2 * WAYS - 1) // (2 * WAYS)
        lax.fori_loop(0, steps, step, 0)
        finish(2 * steps - 1, tile_refs[1])

    def near_keep(tile_ref, way, values):
        tile_ref[way] = values.astype(BF16)

    def near_apply(leaf, entry, times, tile_ref, way):
        total_ref[leaf] += dot_nn(vectors_ref[entry], tile_ref[way]) * times

    run(
        make_list(0, PARTNERS),
        lambda leaf, entry: dot_nn(window_ref[entry], own_ref[leaf]),
        near_keep,
        near_apply,
        near_shifted,
        near_tiles,
    )

    def far_keep(tile_ref, way, values):
        high, low = split_two(values)
        tile_ref[way, 0] = high
        tile_ref[way, 1] = low

    def far_apply(leaf, entry, times, tile_ref, way):
        rows = s_ref[entry - PARTNERS]
        term = fold_two(dot_nn(rows, tile_ref[way, 0])) + dot_nn(rows[:RHS], tile_ref[way, 1])
        t_ref[leaf] += term * times

    run(
        make_list(PARTNERS, QUARTER),
        lambda leaf, entry: dot_nn(skel_rows_ref[entry - PARTNERS], own_skel_ref[leaf]),
        far_keep,
        far_apply,
        far_shifted,
        far_tiles,
    )

    for leaf in range(LEAVES):
        total_ref[leaf] += dot_wide_nt(t_ref[leaf], basis_ref[leaf])
    mine = pl.ds(pl.multiple_of(rep * OWN, OWN), OWN)
    for leaf in range(LEAVES):
        own_out_ref[:, leaf * LEAF : (leaf + 1) * LEAF] = total_ref[leaf, mine, :]
    for leaf in range(LEAVES // 2):
        top = total_ref[leaf].reshape(REPS, OWN, LEAF)
        bottom = total_ref[leaf + LEAVES // 2].reshape(REPS, OWN, LEAF)
        out_ref[:, :, leaf * LEAF : (leaf + 1) * LEAF] = jnp.concatenate([top, bottom], axis=1).astype(BF16)


def combine_kernel(part_ref, own_ref, inverse_ref, out_ref, got_ref, total_ref, sems):
    leaf = lax.axis_index("leaf")
    rep = lax.axis_index("rep")
    partners = [(leaf, lax.rem(rep + step, REPS)) for step in range(1, REPS)]
    greet_signals(partners)
    greet_wait(partners)
    copies = []
    for index, partner in enumerate(partners):
        copy = remote(
            part_ref.at[partner[1]], got_ref.at[index], sems.at[0, index], sems.at[1, index], partner
        )
        copy.start()
        copies.append(copy)
    for copy in copies:
        copy.wait()
    half = PTS // 2
    for number in range(2):
        span = slice(number * half, (number + 1) * half)
        rows = slice(number * OWN, (number + 1) * OWN)
        terms = [got_ref[index].astype(F32)[rows] for index in range(REPS - 1)]
        total_ref[:, span] = ((own_ref[:, span] + terms[0]) + terms[1]) + terms[2]

    def one_block(block, _):
        positions = jnp.broadcast_to(inverse_ref[pl.ds(block, 1), :], (OWN, LANES))
        high = positions >> 7
        low = positions & 127
        out = jnp.zeros((OWN, LANES), F32)
        for source in range(BLOCKS):
            table = total_ref[:, source * LANES : (source + 1) * LANES]
            out = jnp.where(high == source, pick(table, low), out)
        out_ref[:, pl.ds(pl.multiple_of(block * LANES, LANES), LANES)] = out
        return 0

    lax.fori_loop(0, BLOCKS, one_block, 0, unroll=4)


def vmem(count):
    return [pl.BlockSpec(memory_space=pltpu.VMEM)] * count


def anywhere(count):
    return [pl.BlockSpec(memory_space=pl.ANY)] * count


def shape(dims, dtype):
    return jax.ShapeDtypeStruct(dims, dtype)


def params(collective_id=None):
    if collective_id is None:
        return pltpu.CompilerParams(vmem_limit_bytes=VMEM_LIMIT)
    return pltpu.CompilerParams(
        collective_id=collective_id, has_side_effects=True, vmem_limit_bytes=VMEM_LIMIT
    )


def on_device(
    count,
    coords,
    right_sides,
    leaf_order,
    leaf_basis,
    leaf_transfer,
    top_transfer,
    skel_leaf,
    skel_root,
    admissible,
    near_leaves,
    near_count,
):
    levels = count.bit_length() - 1
    spans = phases_of(levels)
    dma = pltpu.SemaphoreType.DMA
    window, columns, window_vectors, t_root, times, inverse = pl.pallas_call(
        functools.partial(gather_kernel, count, levels),
        out_shape=(
            shape((SIDES, QUARTER, LEAF, LANES), BF16),
            shape((REPS, QUARTER, DIM, LEAF), BF16),
            shape((SIDES, REPS, 2 * OWN, 2 * LEAF), BF16),
            shape((OWN, RANK), F32),
            shape((LEAVES, LANES), I32),
            shape((BLOCKS, LANES), I32),
        ),
        in_specs=vmem(3) + anywhere(2) + vmem(5),
        out_specs=tuple(vmem(6)),
        scratch_shapes=[
            pltpu.VMEM((BLOCKS, DIM + OWN, LANES), F32),
            pltpu.VMEM((LEAVES, OWN, LEAF), F32),
            pltpu.VMEM((REPS, 2 * OWN, 2 * LEAF), BF16),
            pltpu.VMEM((LEAVES, LEAF, RANK), BF16),
            pltpu.VMEM((LEAVES, RANK, RANK), BF16),
            pltpu.VMEM((levels, DIM, RANK), BF16),
            pltpu.VMEM((levels, DIM, RANK), BF16),
            pltpu.VMEM((levels, 2, RANK, RANK), BF16),
            pltpu.VMEM((levels, OWN, RANK), F32),
        ]
        + [pltpu.VMEM((1 << width, OWN, RANK), F32) for _, width in spans]
        + [dma((2, 1 << width)) for _, width in spans]
        + [
            dma((2, QUARTER, 2)),
            dma((2, QUARTER, REPS - 1)),
            dma((2, SIDES, REPS)),
            dma((2, levels, 1 << (max(PHASES) - 1))),
            dma((2,)),
        ],
        compiler_params=params(0),
        name="gather",
    )(
        coords,
        right_sides,
        leaf_order.reshape(BLOCKS, LANES),
        leaf_basis,
        leaf_transfer,
        top_transfer,
        skel_root,
        admissible.T,
        near_leaves,
        near_count.reshape(1, LEAVES),
    )

    part, own_part = pl.pallas_call(
        near_kernel,
        out_shape=(shape((REPS, 2 * OWN, PTS // 2), BF16), shape((OWN, PTS), F32)),
        in_specs=[pl.BlockSpec(memory_space=pltpu.SMEM)] + vmem(7),
        out_specs=tuple(vmem(2)),
        scratch_shapes=[
            pltpu.SMEM((LEAVES * PARTNERS + 4 * WAYS + 8,), I32),
            pltpu.VMEM((LEAVES, LANES, LEAF), BF16),
            pltpu.VMEM((LEAVES, LANES, RANK), BF16),
            pltpu.VMEM((QUARTER, RANK, LANES), BF16),
            pltpu.VMEM((PARTNERS, RHS, LEAF), BF16),
            pltpu.VMEM((LEAVES, RHS, LEAF), F32),
            pltpu.VMEM((QUARTER, 2 * RHS, RANK), BF16),
            pltpu.VMEM((LEAVES, RHS, RANK), F32),
        ]
        + [pltpu.VMEM((WAYS, LEAF, LEAF), F32)] * 2
        + [pltpu.VMEM((WAYS, LEAF, LEAF), BF16)] * 2
        + [pltpu.VMEM((WAYS, RANK, RANK), F32)] * 2
        + [pltpu.VMEM((WAYS, 2, RANK, RANK), BF16)] * 2,
        compiler_params=params(),
        name="near",
    )(
        times,
        columns,
        window.reshape(PARTNERS, LEAF, LANES),
        window_vectors,
        leaf_basis,
        leaf_transfer,
        skel_leaf,
        t_root,
    )

    return pl.pallas_call(
        combine_kernel,
        out_shape=shape((OWN, PTS), F32),
        in_specs=vmem(3),
        out_specs=pl.BlockSpec(memory_space=pltpu.VMEM),
        scratch_shapes=[
            pltpu.VMEM((REPS - 1, 2 * OWN, PTS // 2), BF16),
            pltpu.VMEM((OWN, PTS), F32),
            dma((2, REPS - 1)),
        ],
        compiler_params=params(1),
        name="combine",
    )(part, own_part, inverse)


def solution(mesh):
    placed = (
        P(None, "leaf"),
        P("rep", "leaf"),
        P("leaf"),
        P("leaf", None, None),
        P("leaf", None, None),
        P(),
        P("leaf", None),
        P("leaf", None),
        P("leaf", None),
        P("leaf", None),
        P("leaf"),
    )
    return jax.shard_map(
        functools.partial(on_device, mesh.shape["leaf"]),
        mesh=mesh,
        in_specs=placed,
        out_specs=P("rep", "leaf"),
        check_vma=False,
    )
```

```python
import functools

import jax
import jax.numpy as jnp
from jax import lax
from jax.experimental import pallas as pl
from jax.experimental.pallas import tpu as pltpu
from jax.sharding import PartitionSpec as P

MESH = pl.DeviceIdType.MESH
F32 = jnp.float32
BF16 = jnp.bfloat16
I32 = jnp.int32

DIM = 64
RANK = 128
LEAF = 256
LEAVES = 16
PTS = 4096
LANES = 128
BLOCKS = PTS // LANES
REPS = 4
QUARTER = LEAVES // REPS
OWN = 8
RHS = 32
SIDES = 3
PARTNERS = SIDES * QUARTER
PHASES = (3, 2, 2)
WAYS = 2
CHUNKS = 4
VMEM_LIMIT = 60 * 1024 * 1024


def dot_nn(a, b):
    return lax.dot_general(a, b, (((1,), (0,)), ((), ())), preferred_element_type=F32)


def dot_nt(a, b):
    return lax.dot_general(a, b, (((1,), (1,)), ((), ())), preferred_element_type=F32)


def kernel_values(shifted):
    shifted = jnp.maximum(shifted, 1.0)
    return jnp.exp((shifted * -0.5) * lax.rsqrt(shifted))


def split_two(x):
    high = x.astype(BF16)
    return high, (x - high.astype(F32)).astype(BF16)


def stack_two(x):
    high = x.astype(BF16).astype(F32)
    return jnp.concatenate([high, x - high], axis=0).astype(BF16)


def fold_two(x):
    half = x.shape[0] // 2
    return x[:half] + x[half:]


def dot_wide(x, matrix):
    return fold_two(dot_nn(stack_two(x), matrix))


def dot_wide_nt(x, matrix):
    return fold_two(dot_nt(stack_two(x), matrix))


def dot_both_wide(x, matrix):
    rows = stack_two(x)
    high, low = split_two(matrix)
    return fold_two(dot_nn(rows, high)) + fold_two(dot_nn(rows, low))


def with_norms(points, own):
    count = points.shape[1]
    norm = jnp.sum(points * points, axis=0, keepdims=True)
    if own:
        norm = norm + 1.0
    high = norm.astype(BF16).astype(F32)
    rest = norm - high
    mid = rest.astype(BF16).astype(F32)
    low = rest - mid
    row = lax.broadcasted_iota(I32, (16, count), 0)
    if not own:
        row = row - 3
    tail = jnp.where(row == 0, high, jnp.where(row == 1, mid, jnp.where(row == 2, low, 0.0)))
    ones = lax.broadcasted_iota(I32, (16, count), 0) - (3 if own else 0)
    tail = jnp.where((ones >= 0) & (ones < 3), 1.0, tail)
    head = points * -2.0 if own else points
    return jnp.concatenate([head, tail, jnp.zeros((LANES - DIM - 16, count), F32)], axis=0)


def pick(table, lanes):
    return jnp.take_along_axis(table, lanes, axis=1, mode="promise_in_bounds")


def greet_signals(devices):
    barrier = pltpu.get_barrier_semaphore()
    for device in devices:
        pl.semaphore_signal(barrier, inc=1, device_id=device, device_id_type=MESH)


def greet_wait(devices):
    pl.semaphore_wait(pltpu.get_barrier_semaphore(), len(devices))


def remote(source, target, send_sem, recv_sem, device):
    return pltpu.make_async_remote_copy(
        src_ref=source,
        dst_ref=target,
        send_sem=send_sem,
        recv_sem=recv_sem,
        device_id=device,
        device_id_type=MESH,
    )


def phases_of(levels):
    spans, first = [], 0
    for width in PHASES:
        width = min(width, levels - first)
        if width > 0:
            spans.append((first, width))
        first += width
    return spans


def gather_kernel(
    count,
    levels,
    coords_ref,
    rhs_ref,
    order_ref,
    basis_hbm,
    transfer_hbm,
    top_hbm,
    skel_root_ref,
    admissible_ref,
    near_ref,
    count_ref,
    window_ref,
    columns_ref,
    window_vectors_ref,
    t_root_ref,
    times_ref,
    raw_ref,
    sorted_ref,
    vectors_ref,
    basis_ref,
    transfer_ref,
    top_ref,
    points_ref,
    got_points_ref,
    kernel_ref,
    sibling_ref,
    *rest,
):
    spans = phases_of(levels)
    gathered_refs = rest[: len(spans)]
    spread_sems = rest[len(spans) : 2 * len(spans)]
    row_sems, column_sems, vector_sems, push_sems, local_sems = rest[2 * len(spans) :]

    leaf = lax.axis_index("leaf")
    rep = lax.axis_index("rep")
    before = lax.rem(leaf + count - 1, count)
    after = lax.rem(leaf + 1, count)
    others = [lax.rem(rep + step, REPS) for step in range(1, REPS)]
    partners = [(side, other) for side in (before, after) for other in [rep] + others]
    partners += [(leaf, other) for other in others]
    for first, width in spans:
        partners += [(leaf ^ (number << first), rep) for number in range(1, 1 << width)]
    greet_signals(partners)

    loads = [
        pltpu.make_async_copy(basis_hbm, basis_ref, local_sems.at[0]),
        pltpu.make_async_copy(transfer_hbm, transfer_ref, local_sems.at[1]),
        pltpu.make_async_copy(top_hbm, top_ref, local_sems.at[2]),
    ]
    for load in loads:
        load.start()

    def widen(block, _):
        lanes = pl.ds(pl.multiple_of(block * LANES, LANES), LANES)
        raw_ref[block, :DIM, :] = coords_ref[:, lanes].astype(F32)
        raw_ref[block, DIM:, :] = rhs_ref[:, lanes].astype(F32)
        return 0

    lax.fori_loop(0, BLOCKS, widen, 0, unroll=4)

    def gather_rows(positions, first, groups):
        high = positions >> 7
        low = positions & 127
        out = [jnp.zeros((8, LANES), F32)] * groups
        for source in range(BLOCKS):
            here = high == source
            for group in range(groups):
                table = raw_ref[source, first + group * 8 : first + group * 8 + 8, :]
                out[group] = jnp.where(here, pick(table, low), out[group])
        return out

    at = jnp.broadcast_to(skel_root_ref[...], (8, LANES))
    at_high = at >> 7
    at_low = at & 127
    initial = jnp.zeros((8, LANES), I32)
    for source in range(BLOCKS):
        table = jnp.broadcast_to(order_ref[source : source + 1, :], (8, LANES))
        initial = jnp.where(at_high == source, pick(table, at_low), initial)
    points_ref[0] = jnp.concatenate(gather_rows(initial, 0, DIM // 8), axis=0).astype(BF16)
    greet_wait(partners)

    sent = []

    pushes = [[] for _ in spans]

    def push_start(phase):
        if phase >= len(spans):
            return
        first, width = spans[phase]
        for level in range(first, first + width):
            for number in range(1 << (level - first), 2 << (level - first)):
                copy = remote(
                    points_ref.at[first],
                    got_points_ref.at[level],
                    push_sems.at[0, level, number - (1 << (level - first))],
                    push_sems.at[1, level, 0],
                    (leaf ^ (number << first), rep),
                )
                pushes[phase].append((level, copy))
                if level == first:
                    copy.start()
                else:
                    pl.when(lax.rem(leaf // (1 << first), 1 << (level - first)) == 0)(copy.start)

    def push_finish(phase):
        if phase >= len(spans):
            return
        first, width = spans[phase]
        for level in range(first, first + width):
            [copy for at, copy in pushes[phase] if at == level][0].wait_recv()
            if level + 1 < levels:
                on_right = lax.rem(leaf // (1 << level), 2) == 1
                points_ref[level + 1] = jnp.where(
                    on_right, got_points_ref[level].astype(F32), points_ref[level].astype(F32)
                ).astype(BF16)
        push_start(phase + 1)

    def push_wait_send():
        for (first, width), copies in zip(spans, pushes):
            for level, copy in copies:
                if level == first:
                    copy.wait_send()
                else:
                    pl.when(lax.rem(leaf // (1 << first), 1 << (level - first)) == 0)(copy.wait_send)

    def kernels(phase):
        if phase >= len(spans):
            return
        first, width = spans[phase]
        values = []
        for level in range(first, first + width):
            own = with_norms(points_ref[level].astype(F32), True).astype(BF16)
            rows = with_norms(got_points_ref[level].astype(F32), False).T.astype(BF16)
            values.append(split_two(kernel_values(dot_nn(rows, own))))
        for level, (high, low) in zip(range(first, first + width), values):
            kernel_ref[level, 0] = high
            kernel_ref[level, 1] = low

    spreads = []

    def spread_start(phase):
        if phase >= len(spans):
            return
        first, width = spans[phase]
        copies = []
        for number in range(1, 1 << width):
            copy = remote(
                gathered_refs[phase].at[0],
                gathered_refs[phase].at[number],
                spread_sems[phase].at[0, number],
                spread_sems[phase].at[1, number],
                (leaf ^ (number << first), rep),
            )
            copy.start()
            copies.append(copy)
            sent.append(copy)
        spreads.append(copies)

    def spread_finish(phase):
        if phase >= len(spans):
            return
        first, width = spans[phase]
        for copy in spreads[phase]:
            copy.wait_recv()
        nodes = [gathered_refs[phase][number] for number in range(1 << width)]
        for level in range(first, first + width):
            sibling_ref[level] = nodes[1]
            if level + 1 == levels:
                return
            on_right = lax.rem(leaf // (1 << level), 2) == 1
            even = jnp.concatenate(nodes[0::2], axis=0)
            odd = jnp.concatenate(nodes[1::2], axis=0)
            parents = dot_wide(jnp.where(on_right, odd, even), top_ref[level, 0]) + dot_wide(
                jnp.where(on_right, even, odd), top_ref[level, 1]
            )
            nodes = [parents[i * OWN : i * OWN + OWN] for i in range(len(nodes) // 2)]
        gathered_refs[phase + 1][0] = nodes[0]
        spread_start(phase + 1)

    def coupling(level):
        rows = stack_two(sibling_ref[level])
        return fold_two(dot_nn(rows, kernel_ref[level, 0])) + fold_two(dot_nn(rows, kernel_ref[level, 1]))

    push_start(0)

    def sort_vectors(number, _):
        for half in range(2):
            positions = jnp.broadcast_to(order_ref[pl.ds(number * 2 + half, 1), :], (8, LANES))
            sorted_ref[number, :, half * LANES : half * LANES + LANES] = gather_rows(positions, DIM, 1)[0]
        return 0

    lax.fori_loop(0, LEAVES, sort_vectors, 0, unroll=2)
    for load in loads:
        load.wait()

    def up(number, total):
        s_leaf = dot_nn(sorted_ref[number].astype(BF16), basis_ref[number])
        return total + dot_nn(stack_two(s_leaf), transfer_ref[number])

    s_root = fold_two(lax.fori_loop(0, LEAVES, up, jnp.zeros((2 * OWN, RANK), F32), unroll=LEAVES))
    gathered_refs[0][0] = s_root
    spread_start(0)

    for target in range(REPS):
        for column in range(2):
            top = sorted_ref[column * REPS + target]
            bottom = sorted_ref[(column + 2) * REPS + target]
            vectors_ref[target, :, column * LEAF : (column + 1) * LEAF] = jnp.concatenate(
                [top, bottom], axis=0
            ).astype(BF16)
    window_vectors_ref[1, rep] = vectors_ref[rep]
    vector_moves = [
        (index, side, device, step)
        for index, (side, device) in enumerate(((2, before), (0, after), (1, leaf)))
        for step in range(REPS)
        if side != 1 or step > 0
    ]
    for index, side, device, step in vector_moves:
        target = lax.rem(rep + step, REPS)
        copy = remote(
            vectors_ref.at[target],
            window_vectors_ref.at[side, rep],
            vector_sems.at[0, index, step],
            vector_sems.at[1, index, step],
            (device, target),
        )
        copy.start()
        sent.append(copy)

    row_copies = []

    def sort_points(k):
        number = k * REPS + rep
        for half in range(2):
            span = slice(half * LANES, half * LANES + LANES)
            positions = jnp.broadcast_to(order_ref[pl.ds(number * 2 + half, 1), :], (8, LANES))
            points = jnp.concatenate(gather_rows(positions, 0, DIM // 8), axis=0)
            columns_ref[rep, k, :, span] = points.astype(BF16)
            window_ref[1, k, span, :] = with_norms(points, False).T.astype(BF16)
        for index, (side, device) in enumerate(((2, before), (0, after))):
            copy = remote(
                window_ref.at[1, k],
                window_ref.at[side, k],
                row_sems.at[0, k, index],
                row_sems.at[1, k, index],
                (device, rep),
            )
            copy.start()
            row_copies.append(copy)
            sent.append(copy)
        for step, other in enumerate(others):
            copy = remote(
                columns_ref.at[rep, k],
                columns_ref.at[rep, k],
                column_sems.at[0, k, step],
                column_sems.at[1, k, step],
                (leaf, other),
            )
            copy.start()
            sent.append(copy)

    sort_points(0)
    sort_points(1)
    push_finish(0)
    spread_finish(0)
    sort_points(2)
    sort_points(3)
    push_finish(1)
    spread_finish(1)
    kernels(0)
    kernels(1)
    push_finish(2)
    kernels(2)

    diagonal = lax.broadcasted_iota(I32, (LEAVES, LEAVES), 0) == lax.broadcasted_iota(
        I32, (LEAVES, LEAVES), 1
    )

    def as_column(row):
        return jnp.sum(jnp.where(diagonal, row, 0.0), axis=1, keepdims=True)

    near = near_ref[...]
    slot = lax.broadcasted_iota(I32, near.shape, 1)
    live = slot.astype(F32) < as_column(count_ref[...].astype(F32))
    admissible = admissible_ref[...]
    lane = lax.broadcasted_iota(I32, (LEAVES, LANES), 1)
    times = jnp.zeros((LEAVES, LANES), F32)
    for entry in range(PARTNERS + QUARTER):
        if entry < PARTNERS:
            named = jnp.where(near == entry * REPS + rep, 1.0, 0.0)
            total = jnp.sum(jnp.where(live, named, 0.0), axis=1, keepdims=True)
        else:
            named = jnp.where(admissible == (entry - PARTNERS) * REPS + rep, 1.0, 0.0)
            total = as_column(jnp.sum(named, axis=0, keepdims=True))
        times = jnp.where(lane == entry, total, times)
    times_ref[...] = times.astype(I32)

    spread_finish(2)

    running = coupling(levels - 1)
    for level in range(levels - 2, -1, -1):
        side = lax.rem(leaf // (1 << level), 2)
        running = coupling(level) + dot_wide_nt(running, top_ref[level, side])
    t_root_ref[...] = running

    for copy in row_copies:
        copy.wait_recv()
    for k in range(QUARTER):
        for step, other in enumerate(others):
            source = lax.rem(rep + REPS - 1 - step, REPS)
            remote(
                columns_ref.at[rep, k],
                columns_ref.at[source, k],
                column_sems.at[0, k, step],
                column_sems.at[1, k, step],
                (leaf, other),
            ).wait_recv()
    for index, side, device, step in vector_moves:
        source = lax.rem(rep + REPS - step, REPS)
        remote(
            vectors_ref.at[rep],
            window_vectors_ref.at[side, source],
            vector_sems.at[0, index, step],
            vector_sems.at[1, index, step],
            (device, lax.rem(rep + step, REPS)),
        ).wait_recv()
    for copy in sent:
        copy.wait_send()
    push_wait_send()


def near_kernel(
    times_ref,
    columns_ref,
    skel_leaf_ref,
    t_root_ref,
    window_vectors_ref,
    transfer_hbm,
    basis_hbm,
    window_hbm,
    out_ref,
    own_out_ref,
    transfer_ref,
    basis_ref,
    window_ref,
    load_sems,
    list_ref,
    own_ref,
    own_skel_ref,
    skel_rows_ref,
    vectors_ref,
    total_ref,
    s_ref,
    t_ref,
    near_shifted_even,
    near_shifted_odd,
    near_even,
    near_odd,
    far_shifted_even,
    far_shifted_odd,
    far_even,
    far_odd,
):
    near_shifted, near_tiles = (near_shifted_even, near_shifted_odd), (near_even, near_odd)
    far_shifted, far_tiles = (far_shifted_even, far_shifted_odd), (far_even, far_odd)
    rep = lax.axis_index("rep")
    pairs = ((transfer_hbm, transfer_ref), (basis_hbm, basis_ref), (window_hbm, window_ref))
    loads = [
        pltpu.make_async_copy(source, target, load_sems.at[index])
        for index, (source, target) in enumerate(pairs)
    ]
    for load in loads:
        load.start()
    root_rows = stack_two(t_root_ref[...])
    t_ref[...] = jnp.zeros_like(t_ref)

    def prepare(leaf, _):
        source = lax.rem(leaf, REPS)
        k = leaf // REPS
        points = columns_ref[source, k].astype(F32)
        columns = with_norms(points, True)
        own_ref[leaf] = columns.astype(BF16)
        positions = jnp.broadcast_to(skel_leaf_ref[pl.ds(leaf, 1), :], (8, LANES))
        high = positions >> 7
        low = positions & 127
        parts = []
        for group in range(DIM // 8):
            span = slice(group * 8, group * 8 + 8)
            left = pick(points[span, :LANES], low)
            right = pick(points[span, LANES:], low)
            parts.append(jnp.where(high == 0, left, right))
        own_skel_ref[leaf] = with_norms(jnp.concatenate(parts, axis=0), True).astype(BF16)
        return 0

    lax.fori_loop(0, LEAVES, prepare, 0, unroll=4)
    for load in loads:
        load.wait()

    def from_root(leaf, _):
        t_ref[leaf, pl.ds(pl.multiple_of(rep * OWN, OWN), OWN), :] = fold_two(
            dot_nt(root_rows, transfer_ref[leaf])
        )
        return 0

    lax.fori_loop(0, LEAVES, from_root, 0, unroll=8)

    for side in range(SIDES):
        for column in range(2):
            span = slice(column * LEAF, (column + 1) * LEAF)
            blocks = [window_vectors_ref[side, source, :, span].astype(F32) for source in range(REPS)]
            vectors_ref[side * QUARTER + column] = jnp.concatenate(
                [block[:OWN] for block in blocks], axis=0
            ).astype(BF16)
            vectors_ref[side * QUARTER + column + 2] = jnp.concatenate(
                [block[OWN:] for block in blocks], axis=0
            ).astype(BF16)
    for k in range(QUARTER):
        leaf = k * REPS + rep
        s_leaf = dot_nn(vectors_ref[QUARTER + k], basis_ref[leaf])
        s_ref[k] = stack_two(s_leaf)
        skel = own_skel_ref[leaf].astype(F32)
        skel_rows_ref[k] = with_norms(skel[:DIM] * -0.5, False).T.astype(BF16)

    total_ref[...] = jnp.zeros_like(total_ref)

    def make_list(first, width):
        def one_leaf(leaf, filled):
            for entry in range(first, first + width):
                list_ref[filled] = leaf * 16 + entry
                filled = filled + jnp.where(times_ref[leaf, entry] > 0, 1, 0)
            return filled

        filled = lax.fori_loop(0, LEAVES, one_leaf, 0, unroll=2)
        for pad in range(4 * WAYS):
            list_ref[filled + pad] = first
        return filled

    def run(filled, product, keep, apply, shifted_refs, tile_refs):
        def start(group, shifted_ref):
            for way in range(WAYS):
                code = list_ref[group * WAYS + way]
                shifted_ref[way] = product(code >> 4, code & 15)

        def middle(shifted_ref, tile_ref):
            for way in range(WAYS):
                keep(tile_ref, way, kernel_values(shifted_ref[way]))

        def finish(group, tile_ref):
            for way in range(WAYS):
                number = group * WAYS + way
                code = list_ref[jnp.maximum(number, 0)]
                leaf, entry = code >> 4, code & 15
                times = jnp.where((number >= 0) & (number < filled), times_ref[leaf, entry], 0)
                apply(leaf, entry, times.astype(F32), tile_ref, way)

        start(0, shifted_refs[0])
        tile_refs[1][...] = jnp.zeros_like(tile_refs[1])

        def step(number, _):
            even = number * 2
            start(even + 1, shifted_refs[1])
            middle(shifted_refs[0], tile_refs[0])
            finish(even - 1, tile_refs[1])
            start(even + 2, shifted_refs[0])
            middle(shifted_refs[1], tile_refs[1])
            finish(even, tile_refs[0])
            return 0

        steps = (filled + 2 * WAYS - 1) // (2 * WAYS)
        lax.fori_loop(0, steps, step, 0)
        finish(2 * steps - 1, tile_refs[1])

    def near_keep(tile_ref, way, values):
        tile_ref[way] = values.astype(BF16)

    def near_apply(leaf, entry, times, tile_ref, way):
        total_ref[leaf] += dot_nn(vectors_ref[entry], tile_ref[way]) * times

    run(
        make_list(0, PARTNERS),
        lambda leaf, entry: dot_nn(window_ref[entry], own_ref[leaf]),
        near_keep,
        near_apply,
        near_shifted,
        near_tiles,
    )

    def far_keep(tile_ref, way, values):
        high, low = split_two(values)
        tile_ref[way, 0] = high
        tile_ref[way, 1] = low

    def far_apply(leaf, entry, times, tile_ref, way):
        rows = s_ref[entry - PARTNERS]
        term = fold_two(dot_nn(rows, tile_ref[way, 0])) + dot_nn(rows[:RHS], tile_ref[way, 1])
        t_ref[leaf] += term * times

    run(
        make_list(PARTNERS, QUARTER),
        lambda leaf, entry: dot_nn(skel_rows_ref[entry - PARTNERS], own_skel_ref[leaf]),
        far_keep,
        far_apply,
        far_shifted,
        far_tiles,
    )

    for leaf in range(LEAVES):
        total_ref[leaf] += dot_wide_nt(t_ref[leaf], basis_ref[leaf])
    mine = pl.ds(pl.multiple_of(rep * OWN, OWN), OWN)
    for leaf in range(LEAVES):
        own_out_ref[:, leaf * LEAF : (leaf + 1) * LEAF] = total_ref[leaf, mine, :]
    for leaf in range(LEAVES // 2):
        top = total_ref[leaf].reshape(REPS, OWN, LEAF)
        bottom = total_ref[leaf + LEAVES // 2].reshape(REPS, OWN, LEAF)
        out_ref[:, :, leaf * LEAF : (leaf + 1) * LEAF] = jnp.concatenate([top, bottom], axis=1).astype(BF16)


def combine_kernel(part_ref, own_ref, order_ref, out_ref, got_ref, inverse_ref, sems):
    leaf = lax.axis_index("leaf")
    rep = lax.axis_index("rep")
    half = PTS // 2
    width = half // CHUNKS
    partners = [(leaf, lax.rem(rep + step, REPS)) for step in range(1, REPS)]
    greet_signals(partners)
    greet_wait(partners)
    copies = []
    for chunk in range(CHUNKS):
        span = pl.ds(chunk * width, width)
        for index, partner in enumerate(partners):
            copy = remote(
                part_ref.at[partner[1], :, span],
                got_ref.at[index, :, span],
                sems.at[0, index, chunk],
                sems.at[1, index, chunk],
                partner,
            )
            copy.start()
            copies.append(copy)

    lane = lax.broadcasted_iota(I32, (1, LANES), 1).astype(F32)
    row = lax.broadcasted_iota(I32, (BLOCKS, LANES), 0)
    column = lax.broadcasted_iota(I32, (LANES, LANES), 0)

    def invert(group, sums):
        marks, columns = [], []
        for number in range(4):
            block = group * 4 + number
            positions = order_ref[pl.ds(block, 1), :]
            is_row = row == (positions >> 7)
            marks.append(
                jnp.concatenate(
                    [jnp.where(is_row, block.astype(F32), 0.0), jnp.where(is_row, lane, 0.0)], axis=0
                ).astype(BF16)
            )
            columns.append(jnp.where(column == (positions & 127), 1.0, 0.0).astype(BF16))
        return sums + dot_nt(jnp.concatenate(marks, axis=1), jnp.concatenate(columns, axis=1))

    sums = lax.fori_loop(0, BLOCKS // 4, invert, jnp.zeros((2 * BLOCKS, LANES), F32), unroll=2)
    inverse_ref[...] = (sums[:BLOCKS] * float(LANES) + sums[BLOCKS:]).astype(I32)

    for chunk in range(CHUNKS):
        for copy in copies[chunk * len(partners) : (chunk + 1) * len(partners)]:
            copy.wait_recv()
        tables = []
        for number in range(2):
            rows = slice(number * OWN, (number + 1) * OWN)
            total = own_ref[:, number * half + chunk * width : number * half + (chunk + 1) * width]
            for index in range(REPS - 1):
                total = total + got_ref[index, :, chunk * width : (chunk + 1) * width].astype(F32)[rows]
            for at in range(width // LANES):
                first = (number * half + chunk * width) // LANES
                tables.append((first + at, -total[:, at * LANES : (at + 1) * LANES]))

        def one_block(block, _):
            positions = jnp.broadcast_to(inverse_ref[pl.ds(block, 1), :], (OWN, LANES))
            high = positions >> 7
            low = positions & 127
            lanes = pl.ds(pl.multiple_of(block * LANES, LANES), LANES)
            out = jnp.zeros((OWN, LANES), F32) if chunk == 0 else out_ref[:, lanes]
            for source, table in tables:
                out = jnp.where(high == source, pick(table, low), out)
            out_ref[:, lanes] = out
            return 0

        lax.fori_loop(0, BLOCKS, one_block, 0, unroll=8)
    for copy in copies:
        copy.wait_send()


def vmem(count):
    return [pl.BlockSpec(memory_space=pltpu.VMEM)] * count


def anywhere(count):
    return [pl.BlockSpec(memory_space=pl.ANY)] * count


def shape(dims, dtype):
    return jax.ShapeDtypeStruct(dims, dtype)


def params(collective_id=None):
    if collective_id is None:
        return pltpu.CompilerParams(vmem_limit_bytes=VMEM_LIMIT)
    return pltpu.CompilerParams(
        collective_id=collective_id, has_side_effects=True, vmem_limit_bytes=VMEM_LIMIT
    )


def on_device(
    count,
    coords,
    right_sides,
    leaf_order,
    leaf_basis,
    leaf_transfer,
    top_transfer,
    skel_leaf,
    skel_root,
    admissible,
    near_leaves,
    near_count,
):
    levels = count.bit_length() - 1
    spans = phases_of(levels)
    order = leaf_order.reshape(BLOCKS, LANES)
    dma = pltpu.SemaphoreType.DMA
    window, columns, window_vectors, t_root, times = pl.pallas_call(
        functools.partial(gather_kernel, count, levels),
        out_shape=(
            shape((SIDES, QUARTER, LEAF, LANES), BF16),
            shape((REPS, QUARTER, DIM, LEAF), BF16),
            shape((SIDES, REPS, 2 * OWN, 2 * LEAF), BF16),
            shape((OWN, RANK), F32),
            shape((LEAVES, LANES), I32),
        ),
        in_specs=vmem(3) + anywhere(3) + vmem(4),
        out_specs=tuple(vmem(5)),
        scratch_shapes=[
            pltpu.VMEM((BLOCKS, DIM + OWN, LANES), F32),
            pltpu.VMEM((LEAVES, OWN, LEAF), F32),
            pltpu.VMEM((REPS, 2 * OWN, 2 * LEAF), BF16),
            pltpu.VMEM((LEAVES, LEAF, RANK), BF16),
            pltpu.VMEM((LEAVES, RANK, RANK), BF16),
            pltpu.VMEM((levels - 1, 2, RANK, RANK), BF16),
            pltpu.VMEM((levels, DIM, RANK), BF16),
            pltpu.VMEM((levels, DIM, RANK), BF16),
            pltpu.VMEM((levels, 2, RANK, RANK), BF16),
            pltpu.VMEM((levels, OWN, RANK), F32),
        ]
        + [pltpu.VMEM((1 << width, OWN, RANK), F32) for _, width in spans]
        + [dma((2, 1 << width)) for _, width in spans]
        + [
            dma((2, QUARTER, 2)),
            dma((2, QUARTER, REPS - 1)),
            dma((2, SIDES, REPS)),
            dma((2, levels, 1 << (max(PHASES) - 1))),
            dma((3,)),
        ],
        compiler_params=params(0),
        name="gather",
    )(
        coords,
        right_sides,
        order,
        leaf_basis,
        leaf_transfer,
        top_transfer[: levels - 1],
        skel_root,
        admissible.T,
        near_leaves,
        near_count.reshape(1, LEAVES),
    )

    part, own_part = pl.pallas_call(
        near_kernel,
        out_shape=(shape((REPS, 2 * OWN, PTS // 2), BF16), shape((OWN, PTS), F32)),
        in_specs=[pl.BlockSpec(memory_space=pltpu.SMEM)] + vmem(4) + anywhere(3),
        out_specs=tuple(vmem(2)),
        scratch_shapes=[
            pltpu.VMEM((LEAVES, RANK, RANK), BF16),
            pltpu.VMEM((LEAVES, LEAF, RANK), BF16),
            pltpu.VMEM((PARTNERS, LEAF, LANES), BF16),
            dma((3,)),
            pltpu.SMEM((LEAVES * PARTNERS + 4 * WAYS + 8,), I32),
            pltpu.VMEM((LEAVES, LANES, LEAF), BF16),
            pltpu.VMEM((LEAVES, LANES, RANK), BF16),
            pltpu.VMEM((QUARTER, RANK, LANES), BF16),
            pltpu.VMEM((PARTNERS, RHS, LEAF), BF16),
            pltpu.VMEM((LEAVES, RHS, LEAF), F32),
            pltpu.VMEM((QUARTER, 2 * RHS, RANK), BF16),
            pltpu.VMEM((LEAVES, RHS, RANK), F32),
        ]
        + [pltpu.VMEM((WAYS, LEAF, LEAF), F32)] * 2
        + [pltpu.VMEM((WAYS, LEAF, LEAF), BF16)] * 2
        + [pltpu.VMEM((WAYS, RANK, RANK), F32)] * 2
        + [pltpu.VMEM((WAYS, 2, RANK, RANK), BF16)] * 2,
        compiler_params=params(),
        name="near",
    )(
        times,
        columns,
        skel_leaf,
        t_root,
        window_vectors,
        leaf_transfer,
        leaf_basis,
        window.reshape(PARTNERS, LEAF, LANES),
    )

    negative = pl.pallas_call(
        combine_kernel,
        out_shape=shape((OWN, PTS), F32),
        in_specs=vmem(3),
        out_specs=pl.BlockSpec(memory_space=pltpu.VMEM),
        scratch_shapes=[
            pltpu.VMEM((REPS - 1, 2 * OWN, PTS // 2), BF16),
            pltpu.VMEM((BLOCKS, LANES), I32),
            dma((2, REPS - 1, CHUNKS)),
        ],
        compiler_params=params(1),
        name="combine",
    )(part, own_part, order)
    return -negative


def solution(mesh):
    placed = (
        P(None, "leaf"),
        P("rep", "leaf"),
        P("leaf"),
        P("leaf", None, None),
        P("leaf", None, None),
        P(),
        P("leaf", None),
        P("leaf", None),
        P("leaf", None),
        P("leaf", None),
        P("leaf"),
    )
    return jax.shard_map(
        functools.partial(on_device, mesh.shape["leaf"]),
        mesh=mesh,
        in_specs=placed,
        out_specs=P("rep", "leaf"),
        check_vma=False,
    )
```

```python
import functools

import jax
import jax.numpy as jnp
from jax import lax
from jax.experimental import pallas as pl
from jax.experimental.pallas import tpu as pltpu
from jax.sharding import PartitionSpec as P

MESH = pl.DeviceIdType.MESH
F32 = jnp.float32
BF16 = jnp.bfloat16
I32 = jnp.int32

DIM = 64
RANK = 128
LEAF = 256
LEAVES = 16
PTS = 4096
LANES = 128
BLOCKS = PTS // LANES
REPS = 4
QUARTER = LEAVES // REPS
OWN = 8
RHS = 32
SIDES = 3
PARTNERS = SIDES * QUARTER
PHASES = (3, 2, 2)
WAYS = 2
CHUNKS = 4
VMEM_LIMIT = 60 * 1024 * 1024


def dot_nn(a, b):
    return lax.dot_general(a, b, (((1,), (0,)), ((), ())), preferred_element_type=F32)


def dot_nt(a, b):
    return lax.dot_general(a, b, (((1,), (1,)), ((), ())), preferred_element_type=F32)


def kernel_values(shifted):
    shifted = jnp.maximum(shifted, 1.0)
    return jnp.exp((shifted * -0.5) * lax.rsqrt(shifted))


def split_two(x):
    high = x.astype(BF16)
    return high, (x - high.astype(F32)).astype(BF16)


def stack_two(x):
    high = x.astype(BF16).astype(F32)
    return jnp.concatenate([high, x - high], axis=0).astype(BF16)


def fold_two(x):
    half = x.shape[0] // 2
    return x[:half] + x[half:]


def dot_wide(x, matrix):
    return fold_two(dot_nn(stack_two(x), matrix))


def dot_wide_nt(x, matrix):
    return fold_two(dot_nt(stack_two(x), matrix))


def dot_both_wide(x, matrix):
    rows = stack_two(x)
    high, low = split_two(matrix)
    return fold_two(dot_nn(rows, high)) + fold_two(dot_nn(rows, low))


def with_norms(points, own):
    count = points.shape[1]
    norm = jnp.sum(points * points, axis=0, keepdims=True)
    if own:
        norm = norm + 1.0
    high = norm.astype(BF16).astype(F32)
    rest = norm - high
    mid = rest.astype(BF16).astype(F32)
    low = rest - mid
    row = lax.broadcasted_iota(I32, (16, count), 0)
    if not own:
        row = row - 3
    tail = jnp.where(row == 0, high, jnp.where(row == 1, mid, jnp.where(row == 2, low, 0.0)))
    ones = lax.broadcasted_iota(I32, (16, count), 0) - (3 if own else 0)
    tail = jnp.where((ones >= 0) & (ones < 3), 1.0, tail)
    head = points * -2.0 if own else points
    return jnp.concatenate([head, tail, jnp.zeros((LANES - DIM - 16, count), F32)], axis=0)


def one_hot(low):
    row = lax.broadcasted_iota(I32, (LEAF, low.shape[1]), 0)
    return jnp.where(row == low, 1.0, 0.0).astype(BF16)


def choose(slices, positions):
    marks = one_hot(positions & 255)
    rows = slices[0].shape[0]
    high = jnp.broadcast_to(positions >> 8, (rows, positions.shape[1]))
    out = jnp.zeros((rows, positions.shape[1]), F32)
    together = min(len(slices), 512 // rows)
    for first in range(0, len(slices), together):
        block = dot_nn(jnp.concatenate(slices[first : first + together], axis=0), marks)
        for number in range(together):
            out = jnp.where(high == first + number, block[number * rows : (number + 1) * rows], out)
    return out


def order_of(order_ref, leaf):
    return jnp.concatenate([order_ref[pl.ds(leaf * 2 + half, 1), :] for half in range(2)], axis=1)


def pick(table, lanes):
    return jnp.take_along_axis(table, lanes, axis=1, mode="promise_in_bounds")


def greet_signals(devices):
    barrier = pltpu.get_barrier_semaphore()
    for device in devices:
        pl.semaphore_signal(barrier, inc=1, device_id=device, device_id_type=MESH)


def greet_wait(devices):
    pl.semaphore_wait(pltpu.get_barrier_semaphore(), len(devices))


def remote(source, target, send_sem, recv_sem, device):
    return pltpu.make_async_remote_copy(
        src_ref=source,
        dst_ref=target,
        send_sem=send_sem,
        recv_sem=recv_sem,
        device_id=device,
        device_id_type=MESH,
    )


def phases_of(levels):
    spans, first = [], 0
    for width in PHASES:
        width = min(width, levels - first)
        if width > 0:
            spans.append((first, width))
        first += width
    return spans


def gather_kernel(
    count,
    levels,
    coords_ref,
    rhs_ref,
    order_ref,
    basis_hbm,
    transfer_hbm,
    top_hbm,
    skel_root_ref,
    admissible_ref,
    near_ref,
    count_ref,
    window_ref,
    columns_ref,
    window_vectors_ref,
    t_root_ref,
    times_ref,
    sorted_ref,
    vectors_ref,
    basis_ref,
    transfer_ref,
    top_ref,
    points_ref,
    got_points_ref,
    kernel_ref,
    sibling_ref,
    *rest,
):
    spans = phases_of(levels)
    gathered_refs = rest[: len(spans)]
    spread_sems = rest[len(spans) : 2 * len(spans)]
    row_sems, column_sems, vector_sems, push_sems, local_sems = rest[2 * len(spans) :]

    leaf = lax.axis_index("leaf")
    rep = lax.axis_index("rep")
    before = lax.rem(leaf + count - 1, count)
    after = lax.rem(leaf + 1, count)
    others = [lax.rem(rep + step, REPS) for step in range(1, REPS)]
    partners = [(side, other) for side in (before, after) for other in [rep] + others]
    partners += [(leaf, other) for other in others]
    for first, width in spans:
        partners += [(leaf ^ (number << first), rep) for number in range(1, 1 << width)]
    greet_signals(partners)

    loads = [
        pltpu.make_async_copy(basis_hbm, basis_ref, local_sems.at[0]),
        pltpu.make_async_copy(transfer_hbm, transfer_ref, local_sems.at[1]),
        pltpu.make_async_copy(top_hbm, top_ref, local_sems.at[2]),
    ]
    for load in loads:
        load.start()

    def coordinate_slices():
        return [coords_ref[:, high * LEAF : (high + 1) * LEAF] for high in range(LEAVES)]

    at = jnp.broadcast_to(skel_root_ref[...], (8, LANES))
    at_high = at >> 7
    at_low = at & 127
    initial = jnp.zeros((8, LANES), I32)
    for source in range(BLOCKS):
        table = jnp.broadcast_to(order_ref[source : source + 1, :], (8, LANES))
        initial = jnp.where(at_high == source, pick(table, at_low), initial)
    points_ref[0] = choose(coordinate_slices(), initial[:1]).astype(BF16)
    greet_wait(partners)

    sent = []

    pushes = [[] for _ in spans]

    def push_start(phase):
        if phase >= len(spans):
            return
        first, width = spans[phase]
        for level in range(first, first + width):
            for number in range(1 << (level - first), 2 << (level - first)):
                copy = remote(
                    points_ref.at[first],
                    got_points_ref.at[level],
                    push_sems.at[0, level, number - (1 << (level - first))],
                    push_sems.at[1, level, 0],
                    (leaf ^ (number << first), rep),
                )
                pushes[phase].append((level, copy))
                if level == first:
                    copy.start()
                else:
                    pl.when(lax.rem(leaf // (1 << first), 1 << (level - first)) == 0)(copy.start)

    def push_finish(phase):
        if phase >= len(spans):
            return
        first, width = spans[phase]
        for level in range(first, first + width):
            [copy for at, copy in pushes[phase] if at == level][0].wait_recv()
            if level + 1 < levels:
                on_right = lax.rem(leaf // (1 << level), 2) == 1
                points_ref[level + 1] = jnp.where(
                    on_right, got_points_ref[level].astype(F32), points_ref[level].astype(F32)
                ).astype(BF16)
        push_start(phase + 1)

    def push_wait_send():
        for (first, width), copies in zip(spans, pushes):
            for level, copy in copies:
                if level == first:
                    copy.wait_send()
                else:
                    pl.when(lax.rem(leaf // (1 << first), 1 << (level - first)) == 0)(copy.wait_send)

    def kernels(first, last):
        first, last = min(first, levels), min(last, levels)
        values = []
        for level in range(first, last):
            own = with_norms(points_ref[level].astype(F32), True).astype(BF16)
            rows = with_norms(got_points_ref[level].astype(F32), False).T.astype(BF16)
            values.append(split_two(kernel_values(dot_nn(rows, own))))
        for level, (high, low) in zip(range(first, last), values):
            kernel_ref[level, 0] = high
            kernel_ref[level, 1] = low

    spreads = []

    def spread_start(phase):
        if phase >= len(spans):
            return
        first, width = spans[phase]
        copies = []
        for number in range(1, 1 << width):
            copy = remote(
                gathered_refs[phase].at[0],
                gathered_refs[phase].at[number],
                spread_sems[phase].at[0, number],
                spread_sems[phase].at[1, number],
                (leaf ^ (number << first), rep),
            )
            copy.start()
            copies.append(copy)
            sent.append(copy)
        spreads.append(copies)

    def spread_finish(phase):
        if phase >= len(spans):
            return
        first, width = spans[phase]
        for copy in spreads[phase]:
            copy.wait_recv()
        nodes = [gathered_refs[phase][number] for number in range(1 << width)]
        for level in range(first, first + width):
            sibling_ref[level] = nodes[1]
            if level + 1 == levels:
                return
            on_right = lax.rem(leaf // (1 << level), 2) == 1
            even = jnp.concatenate(nodes[0::2], axis=0)
            odd = jnp.concatenate(nodes[1::2], axis=0)
            parents = dot_wide(jnp.where(on_right, odd, even), top_ref[level, 0]) + dot_wide(
                jnp.where(on_right, even, odd), top_ref[level, 1]
            )
            nodes = [parents[i * OWN : i * OWN + OWN] for i in range(len(nodes) // 2)]
        gathered_refs[phase + 1][0] = nodes[0]
        spread_start(phase + 1)

    def coupling(level):
        rows = stack_two(sibling_ref[level])
        return fold_two(dot_nn(rows, kernel_ref[level, 0])) + fold_two(dot_nn(rows, kernel_ref[level, 1]))

    push_start(0)

    vector_rows = jnp.concatenate(
        [rhs_ref[:, high * LEAF : (high + 1) * LEAF].astype(F32) for high in range(LEAVES)], axis=0
    ).astype(BF16)

    def sort_vectors(number, _):
        positions = order_of(order_ref, number)
        block = dot_nn(vector_rows, one_hot(positions & 255))
        high = jnp.broadcast_to(positions >> 8, (OWN, LEAF))
        out = jnp.zeros((OWN, LEAF), F32)
        for source in range(LEAVES):
            out = jnp.where(high == source, block[source * OWN : (source + 1) * OWN], out)
        sorted_ref[number] = out
        return 0

    lax.fori_loop(0, LEAVES, sort_vectors, 0, unroll=4)

    for load in loads:
        load.wait()

    def up(number, total):
        s_leaf = dot_nn(sorted_ref[number].astype(BF16), basis_ref[number])
        return total + dot_nn(stack_two(s_leaf), transfer_ref[number])

    s_root = fold_two(lax.fori_loop(0, LEAVES, up, jnp.zeros((2 * OWN, RANK), F32), unroll=LEAVES))
    gathered_refs[0][0] = s_root
    spread_start(0)

    for target in range(REPS):
        for column in range(2):
            top = sorted_ref[column * REPS + target]
            bottom = sorted_ref[(column + 2) * REPS + target]
            vectors_ref[target, :, column * LEAF : (column + 1) * LEAF] = jnp.concatenate(
                [top, bottom], axis=0
            ).astype(BF16)
    window_vectors_ref[1, rep] = vectors_ref[rep]
    vector_moves = [
        (index, side, device, step)
        for index, (side, device) in enumerate(((2, before), (0, after), (1, leaf)))
        for step in range(REPS)
        if side != 1 or step > 0
    ]
    for index, side, device, step in vector_moves:
        target = lax.rem(rep + step, REPS)
        copy = remote(
            vectors_ref.at[target],
            window_vectors_ref.at[side, rep],
            vector_sems.at[0, index, step],
            vector_sems.at[1, index, step],
            (device, target),
        )
        copy.start()
        sent.append(copy)

    row_copies = []

    def sort_points(k):
        number = k * REPS + rep
        points = choose(coordinate_slices(), order_of(order_ref, number))
        columns_ref[rep, k] = points.astype(BF16)
        window_ref[1, k] = with_norms(points, False).T.astype(BF16)
        for index, (side, device) in enumerate(((2, before), (0, after))):
            copy = remote(
                window_ref.at[1, k],
                window_ref.at[side, k],
                row_sems.at[0, k, index],
                row_sems.at[1, k, index],
                (device, rep),
            )
            copy.start()
            row_copies.append(copy)
            sent.append(copy)
        for step, other in enumerate(others):
            copy = remote(
                columns_ref.at[rep, k],
                columns_ref.at[rep, k],
                column_sems.at[0, k, step],
                column_sems.at[1, k, step],
                (leaf, other),
            )
            copy.start()
            sent.append(copy)

    sort_points(0)
    sort_points(1)
    push_finish(0)
    spread_finish(0)
    sort_points(2)
    sort_points(3)
    push_finish(1)
    spread_finish(1)
    kernels(0, 5)
    push_finish(2)
    kernels(5, 7)

    diagonal = lax.broadcasted_iota(I32, (LEAVES, LEAVES), 0) == lax.broadcasted_iota(
        I32, (LEAVES, LEAVES), 1
    )

    def as_column(row):
        return jnp.sum(jnp.where(diagonal, row, 0.0), axis=1, keepdims=True)

    near = near_ref[...]
    slot = lax.broadcasted_iota(I32, near.shape, 1)
    live = slot.astype(F32) < as_column(count_ref[...].astype(F32))
    admissible = admissible_ref[...]
    lane = lax.broadcasted_iota(I32, (LEAVES, LANES), 1)
    times = jnp.zeros((LEAVES, LANES), F32)
    for entry in range(PARTNERS + QUARTER):
        if entry < PARTNERS:
            named = jnp.where(near == entry * REPS + rep, 1.0, 0.0)
            total = jnp.sum(jnp.where(live, named, 0.0), axis=1, keepdims=True)
        else:
            named = jnp.where(admissible == (entry - PARTNERS) * REPS + rep, 1.0, 0.0)
            total = as_column(jnp.sum(named, axis=0, keepdims=True))
        times = jnp.where(lane == entry, total, times)
    times_ref[...] = times.astype(I32)

    spread_finish(2)

    running = coupling(levels - 1)
    for level in range(levels - 2, -1, -1):
        side = lax.rem(leaf // (1 << level), 2)
        running = coupling(level) + dot_wide_nt(running, top_ref[level, side])
    t_root_ref[...] = running

    for copy in row_copies:
        copy.wait_recv()
    for k in range(QUARTER):
        for step, other in enumerate(others):
            source = lax.rem(rep + REPS - 1 - step, REPS)
            remote(
                columns_ref.at[rep, k],
                columns_ref.at[source, k],
                column_sems.at[0, k, step],
                column_sems.at[1, k, step],
                (leaf, other),
            ).wait_recv()
    for index, side, device, step in vector_moves:
        source = lax.rem(rep + REPS - step, REPS)
        remote(
            vectors_ref.at[rep],
            window_vectors_ref.at[side, source],
            vector_sems.at[0, index, step],
            vector_sems.at[1, index, step],
            (device, lax.rem(rep + step, REPS)),
        ).wait_recv()
    for copy in sent:
        copy.wait_send()
    push_wait_send()


def near_kernel(
    times_ref,
    columns_ref,
    skel_leaf_ref,
    t_root_ref,
    window_vectors_ref,
    transfer_hbm,
    basis_hbm,
    window_hbm,
    out_ref,
    own_out_ref,
    transfer_ref,
    basis_ref,
    window_ref,
    load_sems,
    list_ref,
    own_ref,
    own_skel_ref,
    skel_rows_ref,
    vectors_ref,
    total_ref,
    s_ref,
    t_ref,
    near_shifted_even,
    near_shifted_odd,
    near_even,
    near_odd,
    far_shifted_even,
    far_shifted_odd,
    far_even,
    far_odd,
):
    near_shifted, near_tiles = (near_shifted_even, near_shifted_odd), (near_even, near_odd)
    far_shifted, far_tiles = (far_shifted_even, far_shifted_odd), (far_even, far_odd)
    rep = lax.axis_index("rep")
    pairs = ((transfer_hbm, transfer_ref), (basis_hbm, basis_ref), (window_hbm, window_ref))
    loads = [
        pltpu.make_async_copy(source, target, load_sems.at[index])
        for index, (source, target) in enumerate(pairs)
    ]
    for load in loads:
        load.start()
    root_rows = stack_two(t_root_ref[...])
    t_ref[...] = jnp.zeros_like(t_ref)

    def prepare(leaf, _):
        source = lax.rem(leaf, REPS)
        k = leaf // REPS
        points = columns_ref[source, k].astype(F32)
        columns = with_norms(points, True)
        own_ref[leaf] = columns.astype(BF16)
        marks = one_hot(skel_leaf_ref[pl.ds(leaf, 1), :])
        own_skel_ref[leaf] = with_norms(dot_nn(columns_ref[source, k], marks), True).astype(BF16)
        return 0

    lax.fori_loop(0, LEAVES, prepare, 0, unroll=4)
    for load in loads:
        load.wait()

    def from_root(leaf, _):
        t_ref[leaf, pl.ds(pl.multiple_of(rep * OWN, OWN), OWN), :] = fold_two(
            dot_nt(root_rows, transfer_ref[leaf])
        )
        return 0

    lax.fori_loop(0, LEAVES, from_root, 0, unroll=8)

    for side in range(SIDES):
        for column in range(2):
            span = slice(column * LEAF, (column + 1) * LEAF)
            blocks = [window_vectors_ref[side, source, :, span].astype(F32) for source in range(REPS)]
            vectors_ref[side * QUARTER + column] = jnp.concatenate(
                [block[:OWN] for block in blocks], axis=0
            ).astype(BF16)
            vectors_ref[side * QUARTER + column + 2] = jnp.concatenate(
                [block[OWN:] for block in blocks], axis=0
            ).astype(BF16)
    for k in range(QUARTER):
        leaf = k * REPS + rep
        s_leaf = dot_nn(vectors_ref[QUARTER + k], basis_ref[leaf])
        s_ref[k] = stack_two(s_leaf)
        skel = own_skel_ref[leaf].astype(F32)
        skel_rows_ref[k] = with_norms(skel[:DIM] * -0.5, False).T.astype(BF16)

    total_ref[...] = jnp.zeros_like(total_ref)

    def make_list(first, width):
        def one_leaf(leaf, filled):
            for entry in range(first, first + width):
                list_ref[filled] = leaf * 16 + entry
                filled = filled + jnp.where(times_ref[leaf, entry] > 0, 1, 0)
            return filled

        filled = lax.fori_loop(0, LEAVES, one_leaf, 0, unroll=2)
        for pad in range(4 * WAYS):
            list_ref[filled + pad] = first
        return filled

    def run(filled, product, keep, apply, shifted_refs, tile_refs):
        def start(group, shifted_ref):
            for way in range(WAYS):
                code = list_ref[group * WAYS + way]
                shifted_ref[way] = product(code >> 4, code & 15)

        def middle(shifted_ref, tile_ref):
            for way in range(WAYS):
                keep(tile_ref, way, kernel_values(shifted_ref[way]))

        def finish(group, tile_ref):
            for way in range(WAYS):
                number = group * WAYS + way
                code = list_ref[jnp.maximum(number, 0)]
                leaf, entry = code >> 4, code & 15
                times = jnp.where((number >= 0) & (number < filled), times_ref[leaf, entry], 0)
                apply(leaf, entry, times.astype(F32), tile_ref, way)

        start(0, shifted_refs[0])
        tile_refs[1][...] = jnp.zeros_like(tile_refs[1])

        def step(number, _):
            even = number * 2
            start(even + 1, shifted_refs[1])
            middle(shifted_refs[0], tile_refs[0])
            finish(even - 1, tile_refs[1])
            start(even + 2, shifted_refs[0])
            middle(shifted_refs[1], tile_refs[1])
            finish(even, tile_refs[0])
            return 0

        steps = (filled + 2 * WAYS - 1) // (2 * WAYS)
        lax.fori_loop(0, steps, step, 0)
        finish(2 * steps - 1, tile_refs[1])

    def near_keep(tile_ref, way, values):
        tile_ref[way] = values.astype(BF16)

    def near_apply(leaf, entry, times, tile_ref, way):
        total_ref[leaf] += dot_nn(vectors_ref[entry], tile_ref[way]) * times

    run(
        make_list(0, PARTNERS),
        lambda leaf, entry: dot_nn(window_ref[entry], own_ref[leaf]),
        near_keep,
        near_apply,
        near_shifted,
        near_tiles,
    )

    def far_keep(tile_ref, way, values):
        high, low = split_two(values)
        tile_ref[way, 0] = high
        tile_ref[way, 1] = low

    def far_apply(leaf, entry, times, tile_ref, way):
        rows = s_ref[entry - PARTNERS]
        term = fold_two(dot_nn(rows, tile_ref[way, 0])) + dot_nn(rows[:RHS], tile_ref[way, 1])
        t_ref[leaf] += term * times

    run(
        make_list(PARTNERS, QUARTER),
        lambda leaf, entry: dot_nn(skel_rows_ref[entry - PARTNERS], own_skel_ref[leaf]),
        far_keep,
        far_apply,
        far_shifted,
        far_tiles,
    )

    for leaf in range(LEAVES):
        total_ref[leaf] += dot_wide_nt(t_ref[leaf], basis_ref[leaf])
    mine = pl.ds(pl.multiple_of(rep * OWN, OWN), OWN)
    for leaf in range(LEAVES):
        own_out_ref[:, leaf * LEAF : (leaf + 1) * LEAF] = total_ref[leaf, mine, :]
    for leaf in range(LEAVES // 2):
        top = total_ref[leaf].reshape(REPS, OWN, LEAF)
        bottom = total_ref[leaf + LEAVES // 2].reshape(REPS, OWN, LEAF)
        out_ref[:, :, leaf * LEAF : (leaf + 1) * LEAF] = jnp.concatenate([top, bottom], axis=1).astype(BF16)


def combine_kernel(part_ref, own_ref, order_ref, out_ref, got_ref, sems):
    leaf = lax.axis_index("leaf")
    rep = lax.axis_index("rep")
    half = PTS // 2
    width = half // CHUNKS
    partners = [(leaf, lax.rem(rep + step, REPS)) for step in range(1, REPS)]
    greet_signals(partners)
    greet_wait(partners)
    copies = []
    for chunk in range(CHUNKS):
        span = pl.ds(chunk * width, width)
        for index, partner in enumerate(partners):
            copy = remote(
                part_ref.at[partner[1], :, span],
                got_ref.at[index, :, span],
                sems.at[0, index, chunk],
                sems.at[1, index, chunk],
                partner,
            )
            copy.start()
            copies.append(copy)

    scattered = jnp.zeros((LEAVES * 2 * OWN, LEAF), F32)
    for chunk in range(CHUNKS):
        here = [(number, (number * half + chunk * width) // LANES) for number in range(2)]
        positions = jnp.concatenate(
            [
                order_ref[first + at : first + at + 1, :]
                for _, first in here
                for at in range(width // LANES)
            ],
            axis=1,
        )
        marks = one_hot(positions & 255)
        high = jnp.broadcast_to(positions >> 8, (2 * OWN, 2 * width))
        for copy in copies[chunk * len(partners) : (chunk + 1) * len(partners)]:
            copy.wait_recv()
        totals = []
        for number, first in here:
            rows = slice(number * OWN, (number + 1) * OWN)
            total = -own_ref[:, first * LANES : first * LANES + width]
            for index in range(REPS - 1):
                total = total - got_ref[index, :, chunk * width : (chunk + 1) * width].astype(F32)[rows]
            totals.append(total)
        total = jnp.concatenate(totals, axis=1)
        rounded = total.astype(BF16).astype(F32)
        terms = jnp.concatenate([rounded, total - rounded], axis=0)
        rows = jnp.concatenate(
            [jnp.where(high == source, terms, 0.0).astype(BF16) for source in range(LEAVES)], axis=0
        )
        scattered = scattered + dot_nt(rows, marks)
    for source in range(LEAVES):
        first = source * 2 * OWN
        out_ref[:, source * LEAF : (source + 1) * LEAF] = (
            scattered[first : first + OWN] + scattered[first + OWN : first + 2 * OWN]
        )
    for copy in copies:
        copy.wait_send()


def vmem(count):
    return [pl.BlockSpec(memory_space=pltpu.VMEM)] * count


def anywhere(count):
    return [pl.BlockSpec(memory_space=pl.ANY)] * count


def shape(dims, dtype):
    return jax.ShapeDtypeStruct(dims, dtype)


def params(collective_id=None):
    if collective_id is None:
        return pltpu.CompilerParams(vmem_limit_bytes=VMEM_LIMIT)
    return pltpu.CompilerParams(
        collective_id=collective_id, has_side_effects=True, vmem_limit_bytes=VMEM_LIMIT
    )


def on_device(
    count,
    coords,
    right_sides,
    leaf_order,
    leaf_basis,
    leaf_transfer,
    top_transfer,
    skel_leaf,
    skel_root,
    admissible,
    near_leaves,
    near_count,
):
    levels = count.bit_length() - 1
    spans = phases_of(levels)
    order = leaf_order.reshape(BLOCKS, LANES)
    dma = pltpu.SemaphoreType.DMA
    window, columns, window_vectors, t_root, times = pl.pallas_call(
        functools.partial(gather_kernel, count, levels),
        out_shape=(
            shape((SIDES, QUARTER, LEAF, LANES), BF16),
            shape((REPS, QUARTER, DIM, LEAF), BF16),
            shape((SIDES, REPS, 2 * OWN, 2 * LEAF), BF16),
            shape((OWN, RANK), F32),
            shape((LEAVES, LANES), I32),
        ),
        in_specs=vmem(3) + anywhere(3) + vmem(4),
        out_specs=tuple(vmem(5)),
        scratch_shapes=[
            pltpu.VMEM((LEAVES, OWN, LEAF), F32),
            pltpu.VMEM((REPS, 2 * OWN, 2 * LEAF), BF16),
            pltpu.VMEM((LEAVES, LEAF, RANK), BF16),
            pltpu.VMEM((LEAVES, RANK, RANK), BF16),
            pltpu.VMEM((levels - 1, 2, RANK, RANK), BF16),
            pltpu.VMEM((levels, DIM, RANK), BF16),
            pltpu.VMEM((levels, DIM, RANK), BF16),
            pltpu.VMEM((levels, 2, RANK, RANK), BF16),
            pltpu.VMEM((levels, OWN, RANK), F32),
        ]
        + [pltpu.VMEM((1 << width, OWN, RANK), F32) for _, width in spans]
        + [dma((2, 1 << width)) for _, width in spans]
        + [
            dma((2, QUARTER, 2)),
            dma((2, QUARTER, REPS - 1)),
            dma((2, SIDES, REPS)),
            dma((2, levels, 1 << (max(PHASES) - 1))),
            dma((3,)),
        ],
        compiler_params=params(0),
        name="gather",
    )(
        coords,
        right_sides,
        order,
        leaf_basis,
        leaf_transfer,
        top_transfer[: levels - 1],
        skel_root,
        admissible.T,
        near_leaves,
        near_count.reshape(1, LEAVES),
    )

    part, own_part = pl.pallas_call(
        near_kernel,
        out_shape=(shape((REPS, 2 * OWN, PTS // 2), BF16), shape((OWN, PTS), F32)),
        in_specs=[pl.BlockSpec(memory_space=pltpu.SMEM)] + vmem(4) + anywhere(3),
        out_specs=tuple(vmem(2)),
        scratch_shapes=[
            pltpu.VMEM((LEAVES, RANK, RANK), BF16),
            pltpu.VMEM((LEAVES, LEAF, RANK), BF16),
            pltpu.VMEM((PARTNERS, LEAF, LANES), BF16),
            dma((3,)),
            pltpu.SMEM((LEAVES * PARTNERS + 4 * WAYS + 8,), I32),
            pltpu.VMEM((LEAVES, LANES, LEAF), BF16),
            pltpu.VMEM((LEAVES, LANES, RANK), BF16),
            pltpu.VMEM((QUARTER, RANK, LANES), BF16),
            pltpu.VMEM((PARTNERS, RHS, LEAF), BF16),
            pltpu.VMEM((LEAVES, RHS, LEAF), F32),
            pltpu.VMEM((QUARTER, 2 * RHS, RANK), BF16),
            pltpu.VMEM((LEAVES, RHS, RANK), F32),
        ]
        + [pltpu.VMEM((WAYS, LEAF, LEAF), F32)] * 2
        + [pltpu.VMEM((WAYS, LEAF, LEAF), BF16)] * 2
        + [pltpu.VMEM((WAYS, RANK, RANK), F32)] * 2
        + [pltpu.VMEM((WAYS, 2, RANK, RANK), BF16)] * 2,
        compiler_params=params(),
        name="near",
    )(
        times,
        columns,
        skel_leaf,
        t_root,
        window_vectors,
        leaf_transfer,
        leaf_basis,
        window.reshape(PARTNERS, LEAF, LANES),
    )

    negative = pl.pallas_call(
        combine_kernel,
        out_shape=shape((OWN, PTS), F32),
        in_specs=vmem(3),
        out_specs=pl.BlockSpec(memory_space=pltpu.VMEM),
        scratch_shapes=[
            pltpu.VMEM((REPS - 1, 2 * OWN, PTS // 2), BF16),
            dma((2, REPS - 1, CHUNKS)),
        ],
        compiler_params=params(1),
        name="combine",
    )(part, own_part, order)
    return -negative


def solution(mesh):
    placed = (
        P(None, "leaf"),
        P("rep", "leaf"),
        P("leaf"),
        P("leaf", None, None),
        P("leaf", None, None),
        P(),
        P("leaf", None),
        P("leaf", None),
        P("leaf", None),
        P("leaf", None),
        P("leaf"),
    )
    return jax.shard_map(
        functools.partial(on_device, mesh.shape["leaf"]),
        mesh=mesh,
        in_specs=placed,
        out_specs=P("rep", "leaf"),
        check_vma=False,
    )
```

```python
import functools

import jax
import jax.numpy as jnp
from jax import lax
from jax.experimental import pallas as pl
from jax.experimental.pallas import tpu as pltpu
from jax.sharding import PartitionSpec as P

MESH = pl.DeviceIdType.MESH
F32 = jnp.float32
BF16 = jnp.bfloat16
I32 = jnp.int32

DIM = 64
RANK = 128
LEAF = 256
LEAVES = 16
PTS = 4096
LANES = 128
BLOCKS = PTS // LANES
REPS = 4
QUARTER = LEAVES // REPS
OWN = 8
RHS = 32
SIDES = 3
PARTNERS = SIDES * QUARTER
PHASES = (3, 2, 2)
WAYS = 2
CHUNKS = 4
VMEM_LIMIT = 24 * 1024 * 1024


def dot_nn(a, b):
    return lax.dot_general(a, b, (((1,), (0,)), ((), ())), preferred_element_type=F32)


def dot_nt(a, b):
    return lax.dot_general(a, b, (((1,), (1,)), ((), ())), preferred_element_type=F32)


def kernel_values(shifted):
    shifted = jnp.maximum(shifted, 1.0)
    return jnp.exp((shifted * -0.5) * lax.rsqrt(shifted))


def split_two(x):
    high = x.astype(BF16)
    return high, (x - high.astype(F32)).astype(BF16)


def stack_two(x):
    high = x.astype(BF16).astype(F32)
    return jnp.concatenate([high, x - high], axis=0).astype(BF16)


def fold_two(x):
    half = x.shape[0] // 2
    return x[:half] + x[half:]


def dot_wide(x, matrix):
    return fold_two(dot_nn(stack_two(x), matrix))


def dot_wide_nt(x, matrix):
    return fold_two(dot_nt(stack_two(x), matrix))


def dot_both_wide(x, matrix):
    rows = stack_two(x)
    high, low = split_two(matrix)
    return fold_two(dot_nn(rows, high)) + fold_two(dot_nn(rows, low))


def with_norms(points, own):
    count = points.shape[1]
    norm = jnp.sum(points * points, axis=0, keepdims=True)
    if own:
        norm = norm + 1.0
    high = norm.astype(BF16).astype(F32)
    rest = norm - high
    mid = rest.astype(BF16).astype(F32)
    low = rest - mid
    row = lax.broadcasted_iota(I32, (16, count), 0)
    if not own:
        row = row - 3
    tail = jnp.where(row == 0, high, jnp.where(row == 1, mid, jnp.where(row == 2, low, 0.0)))
    ones = lax.broadcasted_iota(I32, (16, count), 0) - (3 if own else 0)
    tail = jnp.where((ones >= 0) & (ones < 3), 1.0, tail)
    head = points * -2.0 if own else points
    return jnp.concatenate([head, tail, jnp.zeros((LANES - DIM - 16, count), F32)], axis=0)


def one_hot(low):
    row = lax.broadcasted_iota(I32, (LEAF, low.shape[1]), 0)
    return jnp.where(row == low, 1.0, 0.0).astype(BF16)


def choose(slices, positions):
    marks = one_hot(positions & 255)
    rows = slices[0].shape[0]
    high = jnp.broadcast_to(positions >> 8, (rows, positions.shape[1]))
    out = jnp.zeros((rows, positions.shape[1]), F32)
    together = min(len(slices), 512 // rows)
    for first in range(0, len(slices), together):
        block = dot_nn(jnp.concatenate(slices[first : first + together], axis=0), marks)
        for number in range(together):
            out = jnp.where(high == first + number, block[number * rows : (number + 1) * rows], out)
    return out


def order_of(order_ref, leaf):
    return jnp.concatenate([order_ref[pl.ds(leaf * 2 + half, 1), :] for half in range(2)], axis=1)


def pick(table, lanes):
    return jnp.take_along_axis(table, lanes, axis=1, mode="promise_in_bounds")


def greet_signals(devices):
    barrier = pltpu.get_barrier_semaphore()
    for device in devices:
        pl.semaphore_signal(barrier, inc=1, device_id=device, device_id_type=MESH)


def greet_wait(devices):
    pl.semaphore_wait(pltpu.get_barrier_semaphore(), len(devices))


def remote(source, target, send_sem, recv_sem, device):
    return pltpu.make_async_remote_copy(
        src_ref=source,
        dst_ref=target,
        send_sem=send_sem,
        recv_sem=recv_sem,
        device_id=device,
        device_id_type=MESH,
    )


def phases_of(levels):
    spans, first = [], 0
    for width in PHASES:
        width = min(width, levels - first)
        if width > 0:
            spans.append((first, width))
        first += width
    return spans


def gather_kernel(
    count,
    levels,
    coords_ref,
    rhs_ref,
    order_ref,
    basis_hbm,
    transfer_hbm,
    top_hbm,
    skel_root_ref,
    admissible_ref,
    near_ref,
    count_ref,
    window_ref,
    columns_ref,
    window_vectors_ref,
    t_root_ref,
    times_ref,
    sorted_ref,
    vectors_ref,
    basis_ref,
    transfer_ref,
    top_ref,
    points_ref,
    got_points_ref,
    kernel_ref,
    sibling_ref,
    *rest,
):
    spans = phases_of(levels)
    gathered_refs = rest[: len(spans)]
    spread_sems = rest[len(spans) : 2 * len(spans)]
    row_sems, column_sems, vector_sems, push_sems, local_sems = rest[2 * len(spans) :]

    leaf = lax.axis_index("leaf")
    rep = lax.axis_index("rep")
    before = lax.rem(leaf + count - 1, count)
    after = lax.rem(leaf + 1, count)
    others = [lax.rem(rep + step, REPS) for step in range(1, REPS)]
    partners = [(side, other) for side in (before, after) for other in [rep] + others]
    partners += [(leaf, other) for other in others]
    for first, width in spans:
        partners += [(leaf ^ (number << first), rep) for number in range(1, 1 << width)]
    greet_signals(partners)

    loads = [
        pltpu.make_async_copy(basis_hbm, basis_ref, local_sems.at[0]),
        pltpu.make_async_copy(transfer_hbm, transfer_ref, local_sems.at[1]),
        pltpu.make_async_copy(top_hbm, top_ref, local_sems.at[2]),
    ]
    for load in loads:
        load.start()

    def coordinate_slices():
        return [coords_ref[:, high * LEAF : (high + 1) * LEAF] for high in range(LEAVES)]

    at = jnp.broadcast_to(skel_root_ref[...], (8, LANES))
    at_high = at >> 7
    at_low = at & 127
    initial = jnp.zeros((8, LANES), I32)
    for source in range(BLOCKS):
        table = jnp.broadcast_to(order_ref[source : source + 1, :], (8, LANES))
        initial = jnp.where(at_high == source, pick(table, at_low), initial)
    points_ref[0] = choose(coordinate_slices(), initial[:1]).astype(BF16)
    sent = []

    pushes = [[] for _ in spans]

    def push_start(phase):
        if phase >= len(spans):
            return
        first, width = spans[phase]
        for level in range(first, first + width):
            for number in range(1 << (level - first), 2 << (level - first)):
                copy = remote(
                    points_ref.at[first],
                    got_points_ref.at[level],
                    push_sems.at[0, level, number - (1 << (level - first))],
                    push_sems.at[1, level, 0],
                    (leaf ^ (number << first), rep),
                )
                pushes[phase].append((level, copy))
                if level == first:
                    copy.start()
                else:
                    pl.when(lax.rem(leaf // (1 << first), 1 << (level - first)) == 0)(copy.start)

    def push_finish(phase):
        if phase >= len(spans):
            return
        first, width = spans[phase]
        for level in range(first, first + width):
            [copy for at, copy in pushes[phase] if at == level][0].wait_recv()
            if level + 1 < levels:
                on_right = lax.rem(leaf // (1 << level), 2) == 1
                points_ref[level + 1] = jnp.where(
                    on_right, got_points_ref[level].astype(F32), points_ref[level].astype(F32)
                ).astype(BF16)
        push_start(phase + 1)

    def push_wait_send():
        for (first, width), copies in zip(spans, pushes):
            for level, copy in copies:
                if level == first:
                    copy.wait_send()
                else:
                    pl.when(lax.rem(leaf // (1 << first), 1 << (level - first)) == 0)(copy.wait_send)

    def kernels(first, last):
        first, last = min(first, levels), min(last, levels)
        values = []
        for level in range(first, last):
            own = with_norms(points_ref[level].astype(F32), True).astype(BF16)
            rows = with_norms(got_points_ref[level].astype(F32), False).T.astype(BF16)
            values.append(split_two(kernel_values(dot_nn(rows, own))))
        for level, (high, low) in zip(range(first, last), values):
            kernel_ref[level, 0] = high
            kernel_ref[level, 1] = low

    spreads = []

    def spread_start(phase):
        if phase >= len(spans):
            return
        first, width = spans[phase]
        copies = []
        for number in range(1, 1 << width):
            copy = remote(
                gathered_refs[phase].at[0],
                gathered_refs[phase].at[number],
                spread_sems[phase].at[0, number],
                spread_sems[phase].at[1, number],
                (leaf ^ (number << first), rep),
            )
            copy.start()
            copies.append(copy)
            sent.append(copy)
        spreads.append(copies)

    def spread_finish(phase):
        if phase >= len(spans):
            return
        first, width = spans[phase]
        for copy in spreads[phase]:
            copy.wait_recv()
        nodes = [gathered_refs[phase][number] for number in range(1 << width)]
        for level in range(first, first + width):
            sibling_ref[level] = nodes[1]
            if level + 1 == levels:
                return
            on_right = lax.rem(leaf // (1 << level), 2) == 1
            even = jnp.concatenate(nodes[0::2], axis=0)
            odd = jnp.concatenate(nodes[1::2], axis=0)
            parents = dot_wide(jnp.where(on_right, odd, even), top_ref[level, 0]) + dot_wide(
                jnp.where(on_right, even, odd), top_ref[level, 1]
            )
            nodes = [parents[i * OWN : i * OWN + OWN] for i in range(len(nodes) // 2)]
        gathered_refs[phase + 1][0] = nodes[0]
        spread_start(phase + 1)

    def coupling(level):
        rows = stack_two(sibling_ref[level])
        return fold_two(dot_nn(rows, kernel_ref[level, 0])) + fold_two(dot_nn(rows, kernel_ref[level, 1]))

    vector_rows = jnp.concatenate(
        [rhs_ref[:, high * LEAF : (high + 1) * LEAF].astype(F32) for high in range(LEAVES)], axis=0
    ).astype(BF16)

    def sort_vectors(number, _):
        positions = order_of(order_ref, number)
        block = dot_nn(vector_rows, one_hot(positions & 255))
        high = jnp.broadcast_to(positions >> 8, (OWN, LEAF))
        out = jnp.zeros((OWN, LEAF), F32)
        for source in range(LEAVES):
            out = jnp.where(high == source, block[source * OWN : (source + 1) * OWN], out)
        sorted_ref[number] = out
        return 0

    lax.fori_loop(0, LEAVES, sort_vectors, 0, unroll=4)

    for load in loads:
        load.wait()

    def up(number, total):
        s_leaf = dot_nn(sorted_ref[number].astype(BF16), basis_ref[number])
        return total + dot_nn(stack_two(s_leaf), transfer_ref[number])

    s_root = fold_two(lax.fori_loop(0, LEAVES, up, jnp.zeros((2 * OWN, RANK), F32), unroll=LEAVES))
    gathered_refs[0][0] = s_root
    greet_wait(partners)
    spread_start(0)
    push_start(0)

    for target in range(REPS):
        for column in range(2):
            top = sorted_ref[column * REPS + target]
            bottom = sorted_ref[(column + 2) * REPS + target]
            vectors_ref[target, :, column * LEAF : (column + 1) * LEAF] = jnp.concatenate(
                [top, bottom], axis=0
            ).astype(BF16)
    window_vectors_ref[1, rep] = vectors_ref[rep]
    vector_moves = [
        (index, side, device, step)
        for index, (side, device) in enumerate(((2, before), (0, after), (1, leaf)))
        for step in range(REPS)
        if side != 1 or step > 0
    ]
    for index, side, device, step in vector_moves:
        target = lax.rem(rep + step, REPS)
        copy = remote(
            vectors_ref.at[target],
            window_vectors_ref.at[side, rep],
            vector_sems.at[0, index, step],
            vector_sems.at[1, index, step],
            (device, target),
        )
        copy.start()
        sent.append(copy)

    row_copies = []

    def sort_points(k):
        number = k * REPS + rep
        points = choose(coordinate_slices(), order_of(order_ref, number))
        columns_ref[rep, k] = points.astype(BF16)
        window_ref[1, k] = with_norms(points, False).T.astype(BF16)

    def send_points(pair):
        span = pl.ds(pair * 2, 2)
        for index, (side, device) in enumerate(((2, before), (0, after))):
            copy = remote(
                window_ref.at[1, span],
                window_ref.at[side, span],
                row_sems.at[0, pair, index],
                row_sems.at[1, pair, index],
                (device, rep),
            )
            copy.start()
            row_copies.append(copy)
            sent.append(copy)
        for step, other in enumerate(others):
            copy = remote(
                columns_ref.at[rep, span],
                columns_ref.at[rep, span],
                column_sems.at[0, pair, step],
                column_sems.at[1, pair, step],
                (leaf, other),
            )
            copy.start()
            sent.append(copy)

    sort_points(0)
    sort_points(1)
    send_points(0)
    push_finish(0)
    spread_finish(0)
    sort_points(2)
    sort_points(3)
    send_points(1)
    push_finish(1)
    spread_finish(1)
    kernels(0, 5)
    push_finish(2)
    kernels(5, 7)

    diagonal = lax.broadcasted_iota(I32, (LEAVES, LEAVES), 0) == lax.broadcasted_iota(
        I32, (LEAVES, LEAVES), 1
    )

    def as_column(row):
        return jnp.sum(jnp.where(diagonal, row, 0.0), axis=1, keepdims=True)

    near = near_ref[...]
    slot = lax.broadcasted_iota(I32, near.shape, 1)
    live = slot.astype(F32) < as_column(count_ref[...].astype(F32))
    admissible = admissible_ref[...]
    lane = lax.broadcasted_iota(I32, (LEAVES, LANES), 1)
    times = jnp.zeros((LEAVES, LANES), F32)
    for entry in range(PARTNERS + QUARTER):
        if entry < PARTNERS:
            named = jnp.where(near == entry * REPS + rep, 1.0, 0.0)
            total = jnp.sum(jnp.where(live, named, 0.0), axis=1, keepdims=True)
        else:
            named = jnp.where(admissible == (entry - PARTNERS) * REPS + rep, 1.0, 0.0)
            total = as_column(jnp.sum(named, axis=0, keepdims=True))
        times = jnp.where(lane == entry, total, times)
    times_ref[...] = times.astype(I32)

    spread_finish(2)

    running = coupling(levels - 1)
    for level in range(levels - 2, -1, -1):
        side = lax.rem(leaf // (1 << level), 2)
        running = coupling(level) + dot_wide_nt(running, top_ref[level, side])
    t_root_ref[...] = running

    for copy in row_copies:
        copy.wait_recv()
    for pair in range(2):
        span = pl.ds(pair * 2, 2)
        for step, other in enumerate(others):
            source = lax.rem(rep + REPS - 1 - step, REPS)
            remote(
                columns_ref.at[rep, span],
                columns_ref.at[source, span],
                column_sems.at[0, pair, step],
                column_sems.at[1, pair, step],
                (leaf, other),
            ).wait_recv()
    for index, side, device, step in vector_moves:
        source = lax.rem(rep + REPS - step, REPS)
        remote(
            vectors_ref.at[rep],
            window_vectors_ref.at[side, source],
            vector_sems.at[0, index, step],
            vector_sems.at[1, index, step],
            (device, lax.rem(rep + step, REPS)),
        ).wait_recv()
    for copy in sent:
        copy.wait_send()
    push_wait_send()


def near_kernel(
    times_ref,
    columns_ref,
    skel_leaf_ref,
    t_root_ref,
    window_vectors_ref,
    transfer_ref,
    basis_ref,
    window_ref,
    out_ref,
    own_out_ref,
    list_ref,
    own_ref,
    own_skel_ref,
    skel_rows_ref,
    vectors_ref,
    total_ref,
    s_ref,
    t_ref,
    near_shifted_even,
    near_shifted_odd,
    near_even,
    near_odd,
    far_shifted_even,
    far_shifted_odd,
    far_even,
    far_odd,
):
    near_shifted, near_tiles = (near_shifted_even, near_shifted_odd), (near_even, near_odd)
    far_shifted, far_tiles = (far_shifted_even, far_shifted_odd), (far_even, far_odd)
    rep = lax.axis_index("rep")
    root_rows = stack_two(t_root_ref[...])
    t_ref[...] = jnp.zeros_like(t_ref)

    def prepare(leaf, _):
        source = lax.rem(leaf, REPS)
        k = leaf // REPS
        points = columns_ref[source, k].astype(F32)
        columns = with_norms(points, True)
        own_ref[leaf] = columns.astype(BF16)
        marks = one_hot(skel_leaf_ref[pl.ds(leaf, 1), :])
        own_skel_ref[leaf] = with_norms(dot_nn(columns_ref[source, k], marks), True).astype(BF16)
        return 0

    lax.fori_loop(0, LEAVES, prepare, 0, unroll=4)

    def from_root(leaf, _):
        t_ref[leaf, pl.ds(pl.multiple_of(rep * OWN, OWN), OWN), :] = fold_two(
            dot_nt(root_rows, transfer_ref[leaf])
        )
        return 0

    lax.fori_loop(0, LEAVES, from_root, 0, unroll=8)

    for side in range(SIDES):
        for column in range(2):
            span = slice(column * LEAF, (column + 1) * LEAF)
            blocks = [window_vectors_ref[side, source, :, span].astype(F32) for source in range(REPS)]
            vectors_ref[side * QUARTER + column] = jnp.concatenate(
                [block[:OWN] for block in blocks], axis=0
            ).astype(BF16)
            vectors_ref[side * QUARTER + column + 2] = jnp.concatenate(
                [block[OWN:] for block in blocks], axis=0
            ).astype(BF16)
    for k in range(QUARTER):
        leaf = k * REPS + rep
        s_leaf = dot_nn(vectors_ref[QUARTER + k], basis_ref[leaf])
        s_ref[k] = stack_two(s_leaf)
        skel = own_skel_ref[leaf].astype(F32)
        skel_rows_ref[k] = with_norms(skel[:DIM] * -0.5, False).T.astype(BF16)

    total_ref[...] = jnp.zeros_like(total_ref)

    def make_list(first, width):
        def one_leaf(leaf, filled):
            for entry in range(first, first + width):
                list_ref[filled] = leaf * 16 + entry
                filled = filled + jnp.where(times_ref[leaf, entry] > 0, 1, 0)
            return filled

        filled = lax.fori_loop(0, LEAVES, one_leaf, 0, unroll=2)
        for pad in range(4 * WAYS):
            list_ref[filled + pad] = first
        return filled

    def run(filled, product, keep, apply, shifted_refs, tile_refs):
        def start(group, shifted_ref):
            for way in range(WAYS):
                code = list_ref[group * WAYS + way]
                shifted_ref[way] = product(code >> 4, code & 15)

        def middle(shifted_ref, tile_ref):
            for way in range(WAYS):
                keep(tile_ref, way, kernel_values(shifted_ref[way]))

        def finish(group, tile_ref):
            for way in range(WAYS):
                number = group * WAYS + way
                code = list_ref[jnp.maximum(number, 0)]
                leaf, entry = code >> 4, code & 15
                times = jnp.where((number >= 0) & (number < filled), times_ref[leaf, entry], 0)
                apply(leaf, entry, times.astype(F32), tile_ref, way)

        start(0, shifted_refs[0])
        tile_refs[1][...] = jnp.zeros_like(tile_refs[1])

        def step(number, _):
            even = number * 2
            start(even + 1, shifted_refs[1])
            middle(shifted_refs[0], tile_refs[0])
            finish(even - 1, tile_refs[1])
            start(even + 2, shifted_refs[0])
            middle(shifted_refs[1], tile_refs[1])
            finish(even, tile_refs[0])
            return 0

        steps = (filled + 2 * WAYS - 1) // (2 * WAYS)
        lax.fori_loop(0, steps, step, 0)
        finish(2 * steps - 1, tile_refs[1])

    def near_keep(tile_ref, way, values):
        tile_ref[way] = values.astype(BF16)

    def near_apply(leaf, entry, times, tile_ref, way):
        total_ref[leaf] += dot_nn(vectors_ref[entry], tile_ref[way]) * times

    run(
        make_list(0, PARTNERS),
        lambda leaf, entry: dot_nn(window_ref[entry], own_ref[leaf]),
        near_keep,
        near_apply,
        near_shifted,
        near_tiles,
    )

    def far_keep(tile_ref, way, values):
        high, low = split_two(values)
        tile_ref[way, 0] = high
        tile_ref[way, 1] = low

    def far_apply(leaf, entry, times, tile_ref, way):
        rows = s_ref[entry - PARTNERS]
        term = fold_two(dot_nn(rows, tile_ref[way, 0])) + dot_nn(rows[:RHS], tile_ref[way, 1])
        t_ref[leaf] += term * times

    run(
        make_list(PARTNERS, QUARTER),
        lambda leaf, entry: dot_nn(skel_rows_ref[entry - PARTNERS], own_skel_ref[leaf]),
        far_keep,
        far_apply,
        far_shifted,
        far_tiles,
    )

    for leaf in range(LEAVES):
        total_ref[leaf] += dot_wide_nt(t_ref[leaf], basis_ref[leaf])
    mine = pl.ds(pl.multiple_of(rep * OWN, OWN), OWN)
    for leaf in range(LEAVES):
        own_out_ref[:, leaf * LEAF : (leaf + 1) * LEAF] = total_ref[leaf, mine, :]
    for leaf in range(LEAVES // 2):
        top = total_ref[leaf].reshape(REPS, OWN, LEAF)
        bottom = total_ref[leaf + LEAVES // 2].reshape(REPS, OWN, LEAF)
        out_ref[:, :, leaf * LEAF : (leaf + 1) * LEAF] = jnp.concatenate([top, bottom], axis=1).astype(BF16)


def combine_kernel(part_ref, own_ref, order_ref, out_ref, got_ref, sems):
    leaf = lax.axis_index("leaf")
    rep = lax.axis_index("rep")
    half = PTS // 2
    width = half // CHUNKS
    partners = [(leaf, lax.rem(rep + step, REPS)) for step in range(1, REPS)]
    greet_signals(partners)
    greet_wait(partners)
    copies = []
    for chunk in range(CHUNKS):
        span = pl.ds(chunk * width, width)
        for index, partner in enumerate(partners):
            copy = remote(
                part_ref.at[partner[1], :, span],
                got_ref.at[index, :, span],
                sems.at[0, index, chunk],
                sems.at[1, index, chunk],
                partner,
            )
            copy.start()
            copies.append(copy)

    scattered = jnp.zeros((LEAVES * 2 * OWN, LEAF), F32)
    for chunk in range(CHUNKS):
        here = [(number, (number * half + chunk * width) // LANES) for number in range(2)]
        positions = jnp.concatenate(
            [
                order_ref[first + at : first + at + 1, :]
                for _, first in here
                for at in range(width // LANES)
            ],
            axis=1,
        )
        marks = one_hot(positions & 255)
        high = jnp.broadcast_to(positions >> 8, (2 * OWN, 2 * width))
        for copy in copies[chunk * len(partners) : (chunk + 1) * len(partners)]:
            copy.wait_recv()
        totals = []
        for number, first in here:
            rows = slice(number * OWN, (number + 1) * OWN)
            total = -own_ref[:, first * LANES : first * LANES + width]
            for index in range(REPS - 1):
                total = total - got_ref[index, :, chunk * width : (chunk + 1) * width].astype(F32)[rows]
            totals.append(total)
        total = jnp.concatenate(totals, axis=1)
        rounded = total.astype(BF16).astype(F32)
        terms = jnp.concatenate([rounded, total - rounded], axis=0)
        rows = jnp.concatenate(
            [jnp.where(high == source, terms, 0.0).astype(BF16) for source in range(LEAVES)], axis=0
        )
        scattered = scattered + dot_nt(rows, marks)
    for source in range(LEAVES):
        first = source * 2 * OWN
        out_ref[:, source * LEAF : (source + 1) * LEAF] = (
            scattered[first : first + OWN] + scattered[first + OWN : first + 2 * OWN]
        )
    for copy in copies:
        copy.wait_send()


def vmem(count):
    return [pl.BlockSpec(memory_space=pltpu.VMEM)] * count


def in_hbm(count):
    return [pl.BlockSpec(memory_space=pltpu.HBM)] * count


def shape(dims, dtype):
    return jax.ShapeDtypeStruct(dims, dtype)


def params(collective_id=None):
    if collective_id is None:
        return pltpu.CompilerParams(vmem_limit_bytes=VMEM_LIMIT)
    return pltpu.CompilerParams(
        collective_id=collective_id, has_side_effects=True, vmem_limit_bytes=VMEM_LIMIT
    )


def on_device(
    count,
    coords,
    right_sides,
    leaf_order,
    leaf_basis,
    leaf_transfer,
    top_transfer,
    skel_leaf,
    skel_root,
    admissible,
    near_leaves,
    near_count,
):
    levels = count.bit_length() - 1
    spans = phases_of(levels)
    order = leaf_order.reshape(BLOCKS, LANES)
    dma = pltpu.SemaphoreType.DMA
    window, columns, window_vectors, t_root, times = pl.pallas_call(
        functools.partial(gather_kernel, count, levels),
        out_shape=(
            shape((SIDES, QUARTER, LEAF, LANES), BF16),
            shape((REPS, QUARTER, DIM, LEAF), BF16),
            shape((SIDES, REPS, 2 * OWN, 2 * LEAF), BF16),
            shape((OWN, RANK), F32),
            shape((LEAVES, LANES), I32),
        ),
        in_specs=vmem(3) + in_hbm(3) + vmem(4),
        out_specs=tuple(vmem(5)),
        scratch_shapes=[
            pltpu.VMEM((LEAVES, OWN, LEAF), F32),
            pltpu.VMEM((REPS, 2 * OWN, 2 * LEAF), BF16),
            pltpu.VMEM((LEAVES, LEAF, RANK), BF16),
            pltpu.VMEM((LEAVES, RANK, RANK), BF16),
            pltpu.VMEM((levels - 1, 2, RANK, RANK), BF16),
            pltpu.VMEM((levels, DIM, RANK), BF16),
            pltpu.VMEM((levels, DIM, RANK), BF16),
            pltpu.VMEM((levels, 2, RANK, RANK), BF16),
            pltpu.VMEM((levels, OWN, RANK), F32),
        ]
        + [pltpu.VMEM((1 << width, OWN, RANK), F32) for _, width in spans]
        + [dma((2, 1 << width)) for _, width in spans]
        + [
            dma((2, 2, 2)),
            dma((2, 2, REPS - 1)),
            dma((2, SIDES, REPS)),
            dma((2, levels, 1 << (max(PHASES) - 1))),
            dma((3,)),
        ],
        compiler_params=params(0),
        name="gather",
    )(
        coords,
        right_sides,
        order,
        leaf_basis,
        leaf_transfer,
        top_transfer[: levels - 1],
        skel_root,
        admissible.T,
        near_leaves,
        near_count.reshape(1, LEAVES),
    )

    part, own_part = pl.pallas_call(
        near_kernel,
        out_shape=(shape((REPS, 2 * OWN, PTS // 2), BF16), shape((OWN, PTS), F32)),
        in_specs=[pl.BlockSpec(memory_space=pltpu.SMEM)] + vmem(7),
        out_specs=tuple(vmem(2)),
        scratch_shapes=[
            pltpu.SMEM((LEAVES * PARTNERS + 4 * WAYS + 8,), I32),
            pltpu.VMEM((LEAVES, LANES, LEAF), BF16),
            pltpu.VMEM((LEAVES, LANES, RANK), BF16),
            pltpu.VMEM((QUARTER, RANK, LANES), BF16),
            pltpu.VMEM((PARTNERS, RHS, LEAF), BF16),
            pltpu.VMEM((LEAVES, RHS, LEAF), F32),
            pltpu.VMEM((QUARTER, 2 * RHS, RANK), BF16),
            pltpu.VMEM((LEAVES, RHS, RANK), F32),
        ]
        + [pltpu.VMEM((WAYS, LEAF, LEAF), F32)] * 2
        + [pltpu.VMEM((WAYS, LEAF, LEAF), BF16)] * 2
        + [pltpu.VMEM((WAYS, RANK, RANK), F32)] * 2
        + [pltpu.VMEM((WAYS, 2, RANK, RANK), BF16)] * 2,
        compiler_params=params(),
        name="near",
    )(
        times,
        columns,
        skel_leaf,
        t_root,
        window_vectors,
        leaf_transfer,
        leaf_basis,
        window.reshape(PARTNERS, LEAF, LANES),
    )

    negative = pl.pallas_call(
        combine_kernel,
        out_shape=shape((OWN, PTS), F32),
        in_specs=vmem(3),
        out_specs=pl.BlockSpec(memory_space=pltpu.VMEM),
        scratch_shapes=[
            pltpu.VMEM((REPS - 1, 2 * OWN, PTS // 2), BF16),
            dma((2, REPS - 1, CHUNKS)),
        ],
        compiler_params=params(1),
        name="combine",
    )(part, own_part, order)
    return -negative


def solution(mesh):
    placed = (
        P(None, "leaf"),
        P("rep", "leaf"),
        P("leaf"),
        P("leaf", None, None),
        P("leaf", None, None),
        P(),
        P("leaf", None),
        P("leaf", None),
        P("leaf", None),
        P("leaf", None),
        P("leaf"),
    )
    return jax.shard_map(
        functools.partial(on_device, mesh.shape["leaf"]),
        mesh=mesh,
        in_specs=placed,
        out_specs=P("rep", "leaf"),
        check_vma=False,
    )
```

```python
import functools

import jax
import jax.numpy as jnp
from jax import lax
from jax.experimental import pallas as pl
from jax.experimental.pallas import tpu as pltpu
from jax.sharding import PartitionSpec as P

MESH = pl.DeviceIdType.MESH
F32 = jnp.float32
BF16 = jnp.bfloat16
I32 = jnp.int32

DIM = 64
RANK = 128
LEAF = 256
LEAVES = 16
PTS = 4096
LANES = 128
BLOCKS = PTS // LANES
REPS = 4
QUARTER = LEAVES // REPS
OWN = 8
RHS = 32
SIDES = 3
PARTNERS = SIDES * QUARTER
PHASES = (3, 2, 2)
WAYS = 2
CHUNKS = 4
VMEM_LIMIT = 24 * 1024 * 1024


def dot_nn(a, b):
    return lax.dot_general(a, b, (((1,), (0,)), ((), ())), preferred_element_type=F32)


def dot_nt(a, b):
    return lax.dot_general(a, b, (((1,), (1,)), ((), ())), preferred_element_type=F32)


def kernel_values(shifted):
    shifted = jnp.maximum(shifted, 1.0)
    return jnp.exp((shifted * -0.5) * lax.rsqrt(shifted))


def split_two(x):
    high = x.astype(BF16)
    return high, (x - high.astype(F32)).astype(BF16)


def stack_two(x):
    high = x.astype(BF16).astype(F32)
    return jnp.concatenate([high, x - high], axis=0).astype(BF16)


def fold_two(x):
    half = x.shape[0] // 2
    return x[:half] + x[half:]


def dot_wide(x, matrix):
    return fold_two(dot_nn(stack_two(x), matrix))


def dot_wide_nt(x, matrix):
    return fold_two(dot_nt(stack_two(x), matrix))


def dot_both_wide(x, matrix):
    rows = stack_two(x)
    high, low = split_two(matrix)
    return fold_two(dot_nn(rows, high)) + fold_two(dot_nn(rows, low))


def with_norms(points, own):
    count = points.shape[1]
    norm = jnp.sum(points * points, axis=0, keepdims=True)
    if own:
        norm = norm + 1.0
    high = norm.astype(BF16).astype(F32)
    rest = norm - high
    mid = rest.astype(BF16).astype(F32)
    low = rest - mid
    row = lax.broadcasted_iota(I32, (16, count), 0)
    if not own:
        row = row - 3
    tail = jnp.where(row == 0, high, jnp.where(row == 1, mid, jnp.where(row == 2, low, 0.0)))
    ones = lax.broadcasted_iota(I32, (16, count), 0) - (3 if own else 0)
    tail = jnp.where((ones >= 0) & (ones < 3), 1.0, tail)
    head = points * -2.0 if own else points
    return jnp.concatenate([head, tail, jnp.zeros((LANES - DIM - 16, count), F32)], axis=0)


def one_hot(low):
    row = lax.broadcasted_iota(I32, (LEAF, low.shape[1]), 0)
    return jnp.where(row == low, 1.0, 0.0).astype(BF16)


def choose(slices, positions):
    marks = one_hot(positions & 255)
    rows = slices[0].shape[0]
    high = jnp.broadcast_to(positions >> 8, (rows, positions.shape[1]))
    out = jnp.zeros((rows, positions.shape[1]), F32)
    together = min(len(slices), 512 // rows)
    for first in range(0, len(slices), together):
        block = dot_nn(jnp.concatenate(slices[first : first + together], axis=0), marks)
        for number in range(together):
            out = jnp.where(high == first + number, block[number * rows : (number + 1) * rows], out)
    return out


def order_of(order_ref, leaf):
    return jnp.concatenate([order_ref[pl.ds(leaf * 2 + half, 1), :] for half in range(2)], axis=1)


def pick(table, lanes):
    return jnp.take_along_axis(table, lanes, axis=1, mode="promise_in_bounds")


def greet_signals(devices):
    barrier = pltpu.get_barrier_semaphore()
    for device in devices:
        pl.semaphore_signal(barrier, inc=1, device_id=device, device_id_type=MESH)


def greet_wait(devices):
    pl.semaphore_wait(pltpu.get_barrier_semaphore(), len(devices))


def remote(source, target, send_sem, recv_sem, device):
    return pltpu.make_async_remote_copy(
        src_ref=source,
        dst_ref=target,
        send_sem=send_sem,
        recv_sem=recv_sem,
        device_id=device,
        device_id_type=MESH,
    )


def phases_of(levels):
    spans, first = [], 0
    for width in PHASES:
        width = min(width, levels - first)
        if width > 0:
            spans.append((first, width))
        first += width
    return spans


def vectors_kernel(rows_ref, order_ref, sorted_ref):
    vector_rows = rows_ref[...]

    def sort_vectors(number, _):
        positions = order_of(order_ref, number)
        block = dot_nn(vector_rows, one_hot(positions & 255))
        high = jnp.broadcast_to(positions >> 8, (OWN, LEAF))
        out = jnp.zeros((OWN, LEAF), F32)
        for source in range(LEAVES):
            out = jnp.where(high == source, block[source * OWN : (source + 1) * OWN], out)
        sorted_ref[number] = out
        return 0

    lax.fori_loop(0, LEAVES, sort_vectors, 0, unroll=4)


def gather_kernel(
    count,
    levels,
    coords_ref,
    sorted_ref,
    order_ref,
    basis_ref,
    transfer_ref,
    top_ref,
    skel_root_ref,
    skel_leaf_ref,
    admissible_ref,
    near_ref,
    count_ref,
    window_ref,
    columns_ref,
    window_vectors_ref,
    t_root_ref,
    times_ref,
    skel_out_ref,
    vectors_ref,
    points_ref,
    got_points_ref,
    kernel_ref,
    sibling_ref,
    *rest,
):
    spans = phases_of(levels)
    gathered_refs = rest[: len(spans)]
    spread_sems = rest[len(spans) : 2 * len(spans)]
    row_sems, column_sems, vector_sems, push_sems = rest[2 * len(spans) :]

    leaf = lax.axis_index("leaf")
    rep = lax.axis_index("rep")
    before = lax.rem(leaf + count - 1, count)
    after = lax.rem(leaf + 1, count)
    others = [lax.rem(rep + step, REPS) for step in range(1, REPS)]
    partners = [(side, other) for side in (before, after) for other in [rep] + others]
    partners += [(leaf, other) for other in others]
    for first, width in spans:
        partners += [(leaf ^ (number << first), rep) for number in range(1, 1 << width)]
    greet_signals(partners)

    def coordinate_slices():
        return [coords_ref[:, high * LEAF : (high + 1) * LEAF] for high in range(LEAVES)]

    at = jnp.broadcast_to(skel_root_ref[...], (8, LANES))
    at_high = at >> 7
    at_low = at & 127
    initial = jnp.zeros((8, LANES), I32)
    for source in range(BLOCKS):
        table = jnp.broadcast_to(order_ref[source : source + 1, :], (8, LANES))
        initial = jnp.where(at_high == source, pick(table, at_low), initial)
    points_ref[0] = choose(coordinate_slices(), initial[:1]).astype(BF16)
    sent = []

    pushes = [[] for _ in spans]

    def push_start(phase):
        if phase >= len(spans):
            return
        first, width = spans[phase]
        for level in range(first, first + width):
            for number in range(1 << (level - first), 2 << (level - first)):
                copy = remote(
                    points_ref.at[first],
                    got_points_ref.at[level],
                    push_sems.at[0, level, number - (1 << (level - first))],
                    push_sems.at[1, level, 0],
                    (leaf ^ (number << first), rep),
                )
                pushes[phase].append((level, copy))
                if level == first:
                    copy.start()
                else:
                    pl.when(lax.rem(leaf // (1 << first), 1 << (level - first)) == 0)(copy.start)

    def push_finish(phase):
        if phase >= len(spans):
            return
        first, width = spans[phase]
        for level in range(first, first + width):
            [copy for at, copy in pushes[phase] if at == level][0].wait_recv()
            if level + 1 < levels:
                on_right = lax.rem(leaf // (1 << level), 2) == 1
                points_ref[level + 1] = jnp.where(
                    on_right, got_points_ref[level].astype(F32), points_ref[level].astype(F32)
                ).astype(BF16)
        push_start(phase + 1)

    def push_wait_send():
        for (first, width), copies in zip(spans, pushes):
            for level, copy in copies:
                if level == first:
                    copy.wait_send()
                else:
                    pl.when(lax.rem(leaf // (1 << first), 1 << (level - first)) == 0)(copy.wait_send)

    def kernels(first, last):
        first, last = min(first, levels), min(last, levels)
        values = []
        for level in range(first, last):
            own = with_norms(points_ref[level].astype(F32), True).astype(BF16)
            rows = with_norms(got_points_ref[level].astype(F32), False).T.astype(BF16)
            values.append(split_two(kernel_values(dot_nn(rows, own))))
        for level, (high, low) in zip(range(first, last), values):
            kernel_ref[level, 0] = high
            kernel_ref[level, 1] = low

    spreads = []

    def spread_start(phase):
        if phase >= len(spans):
            return
        first, width = spans[phase]
        copies = []
        for number in range(1, 1 << width):
            copy = remote(
                gathered_refs[phase].at[0],
                gathered_refs[phase].at[number],
                spread_sems[phase].at[0, number],
                spread_sems[phase].at[1, number],
                (leaf ^ (number << first), rep),
            )
            copy.start()
            copies.append(copy)
            sent.append(copy)
        spreads.append(copies)

    def spread_finish(phase):
        if phase >= len(spans):
            return
        first, width = spans[phase]
        for copy in spreads[phase]:
            copy.wait_recv()
        nodes = [gathered_refs[phase][number] for number in range(1 << width)]
        for level in range(first, first + width):
            sibling_ref[level] = nodes[1]
            if level + 1 == levels:
                return
            on_right = lax.rem(leaf // (1 << level), 2) == 1
            even = jnp.concatenate(nodes[0::2], axis=0)
            odd = jnp.concatenate(nodes[1::2], axis=0)
            parents = dot_wide(jnp.where(on_right, odd, even), top_ref[level, 0]) + dot_wide(
                jnp.where(on_right, even, odd), top_ref[level, 1]
            )
            nodes = [parents[i * OWN : i * OWN + OWN] for i in range(len(nodes) // 2)]
        gathered_refs[phase + 1][0] = nodes[0]
        spread_start(phase + 1)

    def coupling(level):
        rows = stack_two(sibling_ref[level])
        return fold_two(dot_nn(rows, kernel_ref[level, 0])) + fold_two(dot_nn(rows, kernel_ref[level, 1]))

    def up(number, total):
        s_leaf = dot_nn(sorted_ref[number].astype(BF16), basis_ref[number])
        return total + dot_nn(stack_two(s_leaf), transfer_ref[number])

    s_root = fold_two(lax.fori_loop(0, LEAVES, up, jnp.zeros((2 * OWN, RANK), F32), unroll=LEAVES))
    gathered_refs[0][0] = s_root
    greet_wait(partners)
    spread_start(0)
    push_start(0)

    for target in range(REPS):
        for column in range(2):
            top = sorted_ref[column * REPS + target]
            bottom = sorted_ref[(column + 2) * REPS + target]
            vectors_ref[target, :, column * LEAF : (column + 1) * LEAF] = jnp.concatenate(
                [top, bottom], axis=0
            ).astype(BF16)
    window_vectors_ref[1, rep] = vectors_ref[rep]
    vector_moves = [
        (index, side, device, step)
        for index, (side, device) in enumerate(((2, before), (0, after), (1, leaf)))
        for step in range(REPS)
        if side != 1 or step > 0
    ]
    for index, side, device, step in vector_moves:
        target = lax.rem(rep + step, REPS)
        copy = remote(
            vectors_ref.at[target],
            window_vectors_ref.at[side, rep],
            vector_sems.at[0, index, step],
            vector_sems.at[1, index, step],
            (device, target),
        )
        copy.start()
        sent.append(copy)

    row_copies = []

    def sort_points(k):
        number = k * REPS + rep
        points = choose(coordinate_slices(), order_of(order_ref, number))
        columns_ref[rep, k] = points.astype(BF16)
        window_ref[1, k] = with_norms(points, False).T.astype(BF16)

    def send_points(pair):
        span = pl.ds(pair * 2, 2)
        for index, (side, device) in enumerate(((2, before), (0, after))):
            copy = remote(
                window_ref.at[1, span],
                window_ref.at[side, span],
                row_sems.at[0, pair, index],
                row_sems.at[1, pair, index],
                (device, rep),
            )
            copy.start()
            row_copies.append(copy)
            sent.append(copy)
        for step, other in enumerate(others):
            copy = remote(
                columns_ref.at[rep, span],
                columns_ref.at[rep, span],
                column_sems.at[0, pair, step],
                column_sems.at[1, pair, step],
                (leaf, other),
            )
            copy.start()
            sent.append(copy)

    sort_points(0)
    sort_points(1)
    send_points(0)
    push_finish(0)
    spread_finish(0)
    sort_points(2)
    sort_points(3)
    send_points(1)
    push_finish(1)
    spread_finish(1)
    kernels(0, 5)
    push_finish(2)
    kernels(5, 7)

    diagonal = lax.broadcasted_iota(I32, (LEAVES, LEAVES), 0) == lax.broadcasted_iota(
        I32, (LEAVES, LEAVES), 1
    )

    def as_column(row):
        return jnp.sum(jnp.where(diagonal, row, 0.0), axis=1, keepdims=True)

    near = near_ref[...]
    slot = lax.broadcasted_iota(I32, near.shape, 1)
    live = slot.astype(F32) < as_column(count_ref[...].astype(F32))
    admissible = admissible_ref[...]
    lane = lax.broadcasted_iota(I32, (LEAVES, LANES), 1)
    times = jnp.zeros((LEAVES, LANES), F32)
    for entry in range(PARTNERS + QUARTER):
        if entry < PARTNERS:
            named = jnp.where(near == entry * REPS + rep, 1.0, 0.0)
            total = jnp.sum(jnp.where(live, named, 0.0), axis=1, keepdims=True)
        else:
            named = jnp.where(admissible == (entry - PARTNERS) * REPS + rep, 1.0, 0.0)
            total = as_column(jnp.sum(named, axis=0, keepdims=True))
        times = jnp.where(lane == entry, total, times)
    times_ref[...] = times.astype(I32)
    skel_out_ref[...] = skel_leaf_ref[...]

    spread_finish(2)

    running = coupling(levels - 1)
    for level in range(levels - 2, -1, -1):
        side = lax.rem(leaf // (1 << level), 2)
        running = coupling(level) + dot_wide_nt(running, top_ref[level, side])
    t_root_ref[...] = running

    for copy in row_copies:
        copy.wait_recv()
    for pair in range(2):
        span = pl.ds(pair * 2, 2)
        for step, other in enumerate(others):
            source = lax.rem(rep + REPS - 1 - step, REPS)
            remote(
                columns_ref.at[rep, span],
                columns_ref.at[source, span],
                column_sems.at[0, pair, step],
                column_sems.at[1, pair, step],
                (leaf, other),
            ).wait_recv()
    for index, side, device, step in vector_moves:
        source = lax.rem(rep + REPS - step, REPS)
        remote(
            vectors_ref.at[rep],
            window_vectors_ref.at[side, source],
            vector_sems.at[0, index, step],
            vector_sems.at[1, index, step],
            (device, lax.rem(rep + step, REPS)),
        ).wait_recv()
    for copy in sent:
        copy.wait_send()
    push_wait_send()


def near_kernel(
    times_ref,
    columns_ref,
    skel_leaf_ref,
    t_root_ref,
    window_vectors_ref,
    transfer_ref,
    basis_ref,
    window_ref,
    out_ref,
    own_out_ref,
    list_ref,
    own_ref,
    own_skel_ref,
    skel_rows_ref,
    vectors_ref,
    total_ref,
    s_ref,
    t_ref,
    near_shifted_even,
    near_shifted_odd,
    near_even,
    near_odd,
    far_shifted_even,
    far_shifted_odd,
    far_even,
    far_odd,
):
    near_shifted, near_tiles = (near_shifted_even, near_shifted_odd), (near_even, near_odd)
    far_shifted, far_tiles = (far_shifted_even, far_shifted_odd), (far_even, far_odd)
    rep = lax.axis_index("rep")
    root_rows = stack_two(t_root_ref[...])
    t_ref[...] = jnp.zeros_like(t_ref)

    def prepare(leaf, _):
        source = lax.rem(leaf, REPS)
        k = leaf // REPS
        points = columns_ref[source, k].astype(F32)
        columns = with_norms(points, True)
        own_ref[leaf] = columns.astype(BF16)
        marks = one_hot(skel_leaf_ref[pl.ds(leaf, 1), :])
        own_skel_ref[leaf] = with_norms(dot_nn(columns_ref[source, k], marks), True).astype(BF16)
        return 0

    lax.fori_loop(0, LEAVES, prepare, 0, unroll=4)

    def from_root(leaf, _):
        t_ref[leaf, pl.ds(pl.multiple_of(rep * OWN, OWN), OWN), :] = fold_two(
            dot_nt(root_rows, transfer_ref[leaf])
        )
        return 0

    lax.fori_loop(0, LEAVES, from_root, 0, unroll=8)

    for side in range(SIDES):
        for column in range(2):
            span = slice(column * LEAF, (column + 1) * LEAF)
            blocks = [window_vectors_ref[side, source, :, span].astype(F32) for source in range(REPS)]
            vectors_ref[side * QUARTER + column] = jnp.concatenate(
                [block[:OWN] for block in blocks], axis=0
            ).astype(BF16)
            vectors_ref[side * QUARTER + column + 2] = jnp.concatenate(
                [block[OWN:] for block in blocks], axis=0
            ).astype(BF16)
    for k in range(QUARTER):
        leaf = k * REPS + rep
        s_leaf = dot_nn(vectors_ref[QUARTER + k], basis_ref[leaf])
        s_ref[k] = stack_two(s_leaf)
        skel = own_skel_ref[leaf].astype(F32)
        skel_rows_ref[k] = with_norms(skel[:DIM] * -0.5, False).T.astype(BF16)

    total_ref[...] = jnp.zeros_like(total_ref)

    def make_list(first, width):
        def one_leaf(leaf, filled):
            for entry in range(first, first + width):
                list_ref[filled] = leaf * 16 + entry
                filled = filled + jnp.where(times_ref[leaf, entry] > 0, 1, 0)
            return filled

        filled = lax.fori_loop(0, LEAVES, one_leaf, 0, unroll=2)
        for pad in range(4 * WAYS):
            list_ref[filled + pad] = first
        return filled

    def run(filled, product, keep, apply, shifted_refs, tile_refs):
        def start(group, shifted_ref):
            for way in range(WAYS):
                code = list_ref[group * WAYS + way]
                shifted_ref[way] = product(code >> 4, code & 15)

        def middle(shifted_ref, tile_ref):
            for way in range(WAYS):
                keep(tile_ref, way, kernel_values(shifted_ref[way]))

        def finish(group, tile_ref):
            for way in range(WAYS):
                number = group * WAYS + way
                code = list_ref[jnp.maximum(number, 0)]
                leaf, entry = code >> 4, code & 15
                times = jnp.where((number >= 0) & (number < filled), times_ref[leaf, entry], 0)
                apply(leaf, entry, times.astype(F32), tile_ref, way)

        start(0, shifted_refs[0])
        tile_refs[1][...] = jnp.zeros_like(tile_refs[1])

        def step(number, _):
            even = number * 2
            start(even + 1, shifted_refs[1])
            middle(shifted_refs[0], tile_refs[0])
            finish(even - 1, tile_refs[1])
            start(even + 2, shifted_refs[0])
            middle(shifted_refs[1], tile_refs[1])
            finish(even, tile_refs[0])
            return 0

        steps = (filled + 2 * WAYS - 1) // (2 * WAYS)
        lax.fori_loop(0, steps, step, 0)
        finish(2 * steps - 1, tile_refs[1])

    def near_keep(tile_ref, way, values):
        tile_ref[way] = values.astype(BF16)

    def near_apply(leaf, entry, times, tile_ref, way):
        total_ref[leaf] += dot_nn(vectors_ref[entry], tile_ref[way]) * times

    run(
        make_list(0, PARTNERS),
        lambda leaf, entry: dot_nn(window_ref[entry], own_ref[leaf]),
        near_keep,
        near_apply,
        near_shifted,
        near_tiles,
    )

    def far_keep(tile_ref, way, values):
        high, low = split_two(values)
        tile_ref[way, 0] = high
        tile_ref[way, 1] = low

    def far_apply(leaf, entry, times, tile_ref, way):
        rows = s_ref[entry - PARTNERS]
        term = fold_two(dot_nn(rows, tile_ref[way, 0])) + dot_nn(rows[:RHS], tile_ref[way, 1])
        t_ref[leaf] += term * times

    run(
        make_list(PARTNERS, QUARTER),
        lambda leaf, entry: dot_nn(skel_rows_ref[entry - PARTNERS], own_skel_ref[leaf]),
        far_keep,
        far_apply,
        far_shifted,
        far_tiles,
    )

    for leaf in range(LEAVES):
        total_ref[leaf] += dot_wide_nt(t_ref[leaf], basis_ref[leaf])
    mine = pl.ds(pl.multiple_of(rep * OWN, OWN), OWN)
    for leaf in range(LEAVES):
        own_out_ref[:, leaf * LEAF : (leaf + 1) * LEAF] = total_ref[leaf, mine, :]
    for leaf in range(LEAVES // 2):
        top = total_ref[leaf].reshape(REPS, OWN, LEAF)
        bottom = total_ref[leaf + LEAVES // 2].reshape(REPS, OWN, LEAF)
        out_ref[:, :, leaf * LEAF : (leaf + 1) * LEAF] = jnp.concatenate([top, bottom], axis=1).astype(BF16)


def combine_kernel(part_ref, own_ref, order_ref, out_ref, got_ref, sems):
    leaf = lax.axis_index("leaf")
    rep = lax.axis_index("rep")
    half = PTS // 2
    width = half // CHUNKS
    partners = [(leaf, lax.rem(rep + step, REPS)) for step in range(1, REPS)]
    greet_signals(partners)
    greet_wait(partners)
    copies = []
    for chunk in range(CHUNKS):
        span = pl.ds(chunk * width, width)
        for index, partner in enumerate(partners):
            copy = remote(
                part_ref.at[partner[1], :, span],
                got_ref.at[index, :, span],
                sems.at[0, index, chunk],
                sems.at[1, index, chunk],
                partner,
            )
            copy.start()
            copies.append(copy)

    scattered = jnp.zeros((LEAVES * 2 * OWN, LEAF), F32)
    for chunk in range(CHUNKS):
        here = [(number, (number * half + chunk * width) // LANES) for number in range(2)]
        positions = jnp.concatenate(
            [
                order_ref[first + at : first + at + 1, :]
                for _, first in here
                for at in range(width // LANES)
            ],
            axis=1,
        )
        marks = one_hot(positions & 255)
        high = jnp.broadcast_to(positions >> 8, (2 * OWN, 2 * width))
        for copy in copies[chunk * len(partners) : (chunk + 1) * len(partners)]:
            copy.wait_recv()
        totals = []
        for number, first in here:
            rows = slice(number * OWN, (number + 1) * OWN)
            total = -own_ref[:, first * LANES : first * LANES + width]
            for index in range(REPS - 1):
                total = total - got_ref[index, :, chunk * width : (chunk + 1) * width].astype(F32)[rows]
            totals.append(total)
        total = jnp.concatenate(totals, axis=1)
        rounded = total.astype(BF16).astype(F32)
        terms = jnp.concatenate([rounded, total - rounded], axis=0)
        rows = jnp.concatenate(
            [jnp.where(high == source, terms, 0.0).astype(BF16) for source in range(LEAVES)], axis=0
        )
        scattered = scattered + dot_nt(rows, marks)
    for source in range(LEAVES):
        first = source * 2 * OWN
        out_ref[:, source * LEAF : (source + 1) * LEAF] = (
            scattered[first : first + OWN] + scattered[first + OWN : first + 2 * OWN]
        )
    for copy in copies:
        copy.wait_send()


def vmem(count):
    return [pl.BlockSpec(memory_space=pltpu.VMEM)] * count


def shape(dims, dtype):
    return jax.ShapeDtypeStruct(dims, dtype)


def params(collective_id=None):
    if collective_id is None:
        return pltpu.CompilerParams(vmem_limit_bytes=VMEM_LIMIT)
    return pltpu.CompilerParams(
        collective_id=collective_id, has_side_effects=True, vmem_limit_bytes=VMEM_LIMIT
    )


def on_device(
    count,
    coords,
    right_sides,
    leaf_order,
    leaf_basis,
    leaf_transfer,
    top_transfer,
    skel_leaf,
    skel_root,
    admissible,
    near_leaves,
    near_count,
):
    levels = count.bit_length() - 1
    spans = phases_of(levels)
    order = leaf_order.reshape(BLOCKS, LANES)
    dma = pltpu.SemaphoreType.DMA
    sorted_vectors = pl.pallas_call(
        vectors_kernel,
        out_shape=shape((LEAVES, OWN, LEAF), F32),
        in_specs=vmem(2),
        out_specs=pl.BlockSpec(memory_space=pltpu.VMEM),
        compiler_params=params(),
        cost_estimate=pl.CostEstimate(flops=10**9, bytes_accessed=10**6, transcendentals=0),
        name="vectors",
    )(
        right_sides.reshape(OWN, LEAVES, LEAF).transpose(1, 0, 2).reshape(LEAVES * OWN, LEAF),
        order,
    )
    window, columns, window_vectors, t_root, times, skel_here = pl.pallas_call(
        functools.partial(gather_kernel, count, levels),
        out_shape=(
            shape((SIDES, QUARTER, LEAF, LANES), BF16),
            shape((REPS, QUARTER, DIM, LEAF), BF16),
            shape((SIDES, REPS, 2 * OWN, 2 * LEAF), BF16),
            shape((OWN, RANK), F32),
            shape((LEAVES, LANES), I32),
            shape((LEAVES, RANK), I32),
        ),
        in_specs=vmem(11),
        out_specs=tuple(vmem(6)),
        scratch_shapes=[
            pltpu.VMEM((REPS, 2 * OWN, 2 * LEAF), BF16),
            pltpu.VMEM((levels, DIM, RANK), BF16),
            pltpu.VMEM((levels, DIM, RANK), BF16),
            pltpu.VMEM((levels, 2, RANK, RANK), BF16),
            pltpu.VMEM((levels, OWN, RANK), F32),
        ]
        + [pltpu.VMEM((1 << width, OWN, RANK), F32) for _, width in spans]
        + [dma((2, 1 << width)) for _, width in spans]
        + [
            dma((2, 2, 2)),
            dma((2, 2, REPS - 1)),
            dma((2, SIDES, REPS)),
            dma((2, levels, 1 << (max(PHASES) - 1))),
        ],
        compiler_params=params(0),
        name="gather",
    )(
        coords,
        sorted_vectors,
        order,
        leaf_basis,
        leaf_transfer,
        top_transfer[: levels - 1],
        skel_root,
        skel_leaf,
        admissible.T,
        near_leaves,
        near_count.reshape(1, LEAVES),
    )

    part, own_part = pl.pallas_call(
        near_kernel,
        out_shape=(shape((REPS, 2 * OWN, PTS // 2), BF16), shape((OWN, PTS), F32)),
        in_specs=[pl.BlockSpec(memory_space=pltpu.SMEM)] + vmem(7),
        out_specs=tuple(vmem(2)),
        scratch_shapes=[
            pltpu.SMEM((LEAVES * PARTNERS + 4 * WAYS + 8,), I32),
            pltpu.VMEM((LEAVES, LANES, LEAF), BF16),
            pltpu.VMEM((LEAVES, LANES, RANK), BF16),
            pltpu.VMEM((QUARTER, RANK, LANES), BF16),
            pltpu.VMEM((PARTNERS, RHS, LEAF), BF16),
            pltpu.VMEM((LEAVES, RHS, LEAF), F32),
            pltpu.VMEM((QUARTER, 2 * RHS, RANK), BF16),
            pltpu.VMEM((LEAVES, RHS, RANK), F32),
        ]
        + [pltpu.VMEM((WAYS, LEAF, LEAF), F32)] * 2
        + [pltpu.VMEM((WAYS, LEAF, LEAF), BF16)] * 2
        + [pltpu.VMEM((WAYS, RANK, RANK), F32)] * 2
        + [pltpu.VMEM((WAYS, 2, RANK, RANK), BF16)] * 2,
        compiler_params=params(),
        name="near",
    )(
        times,
        columns,
        skel_here,
        t_root,
        window_vectors,
        leaf_transfer,
        leaf_basis,
        window.reshape(PARTNERS, LEAF, LANES),
    )

    negative = pl.pallas_call(
        combine_kernel,
        out_shape=shape((OWN, PTS), F32),
        in_specs=vmem(3),
        out_specs=pl.BlockSpec(memory_space=pltpu.VMEM),
        scratch_shapes=[
            pltpu.VMEM((REPS - 1, 2 * OWN, PTS // 2), BF16),
            dma((2, REPS - 1, CHUNKS)),
        ],
        compiler_params=params(1),
        name="combine",
    )(part, own_part, order)
    return -negative


def solution(mesh):
    placed = (
        P(None, "leaf"),
        P("rep", "leaf"),
        P("leaf"),
        P("leaf", None, None),
        P("leaf", None, None),
        P(),
        P("leaf", None),
        P("leaf", None),
        P("leaf", None),
        P("leaf", None),
        P("leaf"),
    )
    return jax.shard_map(
        functools.partial(on_device, mesh.shape["leaf"]),
        mesh=mesh,
        in_specs=placed,
        out_specs=P("rep", "leaf"),
        check_vma=False,
    )
```

```python
import functools

import jax
import jax.numpy as jnp
from jax import lax
from jax.experimental import pallas as pl
from jax.experimental.pallas import tpu as pltpu
from jax.sharding import PartitionSpec as P

MESH = pl.DeviceIdType.MESH
F32 = jnp.float32
BF16 = jnp.bfloat16
I32 = jnp.int32

DIM = 64
RANK = 128
LEAF = 256
LEAVES = 16
PTS = 4096
LANES = 128
BLOCKS = PTS // LANES
REPS = 4
QUARTER = LEAVES // REPS
OWN = 8
RHS = 32
SIDES = 3
PARTNERS = SIDES * QUARTER
PHASES = (3, 4)
WAYS = 2
CHUNKS = 4
VMEM_LIMIT = 24 * 1024 * 1024


def dot_nn(a, b):
    return lax.dot_general(a, b, (((1,), (0,)), ((), ())), preferred_element_type=F32)


def dot_nt(a, b):
    return lax.dot_general(a, b, (((1,), (1,)), ((), ())), preferred_element_type=F32)


def kernel_values(shifted):
    shifted = jnp.maximum(shifted, 1.0)
    return jnp.exp((shifted * -0.5) * lax.rsqrt(shifted))


def split_two(x):
    high = x.astype(BF16)
    return high, (x - high.astype(F32)).astype(BF16)


def stack_two(x):
    high = x.astype(BF16).astype(F32)
    return jnp.concatenate([high, x - high], axis=0).astype(BF16)


def fold_two(x):
    half = x.shape[0] // 2
    return x[:half] + x[half:]


def dot_wide(x, matrix):
    return fold_two(dot_nn(stack_two(x), matrix))


def dot_wide_nt(x, matrix):
    return fold_two(dot_nt(stack_two(x), matrix))


def dot_both_wide(x, matrix):
    rows = stack_two(x)
    high, low = split_two(matrix)
    return fold_two(dot_nn(rows, high)) + fold_two(dot_nn(rows, low))


def with_norms(points, own):
    count = points.shape[1]
    norm = jnp.sum(points * points, axis=0, keepdims=True)
    if own:
        norm = norm + 1.0
    high = norm.astype(BF16).astype(F32)
    rest = norm - high
    mid = rest.astype(BF16).astype(F32)
    low = rest - mid
    row = lax.broadcasted_iota(I32, (16, count), 0)
    if not own:
        row = row - 3
    tail = jnp.where(row == 0, high, jnp.where(row == 1, mid, jnp.where(row == 2, low, 0.0)))
    ones = lax.broadcasted_iota(I32, (16, count), 0) - (3 if own else 0)
    tail = jnp.where((ones >= 0) & (ones < 3), 1.0, tail)
    head = points * -2.0 if own else points
    return jnp.concatenate([head, tail, jnp.zeros((LANES - DIM - 16, count), F32)], axis=0)


def one_hot(low):
    row = lax.broadcasted_iota(I32, (LEAF, low.shape[1]), 0)
    return jnp.where(row == low, 1.0, 0.0).astype(BF16)


def choose(slices, positions):
    marks = one_hot(positions & 255)
    rows = slices[0].shape[0]
    high = jnp.broadcast_to(positions >> 8, (rows, positions.shape[1]))
    out = jnp.zeros((rows, positions.shape[1]), F32)
    together = min(len(slices), 512 // rows)
    for first in range(0, len(slices), together):
        block = dot_nn(jnp.concatenate(slices[first : first + together], axis=0), marks)
        for number in range(together):
            out = jnp.where(high == first + number, block[number * rows : (number + 1) * rows], out)
    return out


def order_of(order_ref, leaf):
    return jnp.concatenate([order_ref[pl.ds(leaf * 2 + half, 1), :] for half in range(2)], axis=1)


def pick(table, lanes):
    return jnp.take_along_axis(table, lanes, axis=1, mode="promise_in_bounds")


def greet_signals(devices):
    barrier = pltpu.get_barrier_semaphore()
    for device in devices:
        pl.semaphore_signal(barrier, inc=1, device_id=device, device_id_type=MESH)


def greet_wait(devices):
    pl.semaphore_wait(pltpu.get_barrier_semaphore(), len(devices))


def remote(source, target, send_sem, recv_sem, device):
    return pltpu.make_async_remote_copy(
        src_ref=source,
        dst_ref=target,
        send_sem=send_sem,
        recv_sem=recv_sem,
        device_id=device,
        device_id_type=MESH,
    )


def phases_of(levels):
    spans, first = [], 0
    for width in PHASES:
        width = min(width, levels - first)
        if width > 0:
            spans.append((first, width))
        first += width
    return spans


def vectors_kernel(rows_ref, order_ref, sorted_ref):
    vector_rows = rows_ref[...]

    def sort_vectors(number, _):
        positions = order_of(order_ref, number)
        block = dot_nn(vector_rows, one_hot(positions & 255))
        high = jnp.broadcast_to(positions >> 8, (OWN, LEAF))
        out = jnp.zeros((OWN, LEAF), F32)
        for source in range(LEAVES):
            out = jnp.where(high == source, block[source * OWN : (source + 1) * OWN], out)
        sorted_ref[number] = out
        return 0

    lax.fori_loop(0, LEAVES, sort_vectors, 0, unroll=4)


def gather_kernel(
    count,
    levels,
    coords_ref,
    sorted_ref,
    order_ref,
    basis_ref,
    transfer_ref,
    top_ref,
    skel_root_ref,
    skel_leaf_ref,
    admissible_ref,
    near_ref,
    count_ref,
    window_ref,
    columns_ref,
    window_vectors_ref,
    t_root_ref,
    times_ref,
    skel_out_ref,
    vectors_ref,
    points_ref,
    got_points_ref,
    kernel_ref,
    sibling_ref,
    *rest,
):
    spans = phases_of(levels)
    gathered_refs = rest[: len(spans)]
    spread_sems = rest[len(spans) : 2 * len(spans)]
    row_sems, column_sems, vector_sems, push_sems = rest[2 * len(spans) :]

    leaf = lax.axis_index("leaf")
    rep = lax.axis_index("rep")
    before = lax.rem(leaf + count - 1, count)
    after = lax.rem(leaf + 1, count)
    others = [lax.rem(rep + step, REPS) for step in range(1, REPS)]
    partners = [(side, other) for side in (before, after) for other in [rep] + others]
    partners += [(leaf, other) for other in others]
    for first, width in spans:
        partners += [(leaf ^ (number << first), rep) for number in range(1, 1 << width)]
    greet_signals(partners)

    def coordinate_slices():
        return [coords_ref[:, high * LEAF : (high + 1) * LEAF] for high in range(LEAVES)]

    at = jnp.broadcast_to(skel_root_ref[...], (8, LANES))
    at_high = at >> 7
    at_low = at & 127
    initial = jnp.zeros((8, LANES), I32)
    for source in range(BLOCKS):
        table = jnp.broadcast_to(order_ref[source : source + 1, :], (8, LANES))
        initial = jnp.where(at_high == source, pick(table, at_low), initial)
    points_ref[0] = choose(coordinate_slices(), initial[:1]).astype(BF16)
    sent = []

    pushes = [[] for _ in spans]

    def push_start(phase):
        if phase >= len(spans):
            return
        first, width = spans[phase]
        for level in range(first, first + width):
            for number in range(1 << (level - first), 2 << (level - first)):
                copy = remote(
                    points_ref.at[first],
                    got_points_ref.at[level],
                    push_sems.at[0, level, number - (1 << (level - first))],
                    push_sems.at[1, level, 0],
                    (leaf ^ (number << first), rep),
                )
                pushes[phase].append((level, copy))
                if level == first:
                    copy.start()
                else:
                    pl.when(lax.rem(leaf // (1 << first), 1 << (level - first)) == 0)(copy.start)

    def push_finish(phase):
        if phase >= len(spans):
            return
        first, width = spans[phase]
        for level in range(first, first + width):
            [copy for at, copy in pushes[phase] if at == level][0].wait_recv()
            if level + 1 < levels:
                on_right = lax.rem(leaf // (1 << level), 2) == 1
                points_ref[level + 1] = jnp.where(
                    on_right, got_points_ref[level].astype(F32), points_ref[level].astype(F32)
                ).astype(BF16)
        push_start(phase + 1)

    def push_wait_send():
        for (first, width), copies in zip(spans, pushes):
            for level, copy in copies:
                if level == first:
                    copy.wait_send()
                else:
                    pl.when(lax.rem(leaf // (1 << first), 1 << (level - first)) == 0)(copy.wait_send)

    def kernels(first, last):
        first, last = min(first, levels), min(last, levels)
        values = []
        for level in range(first, last):
            own = with_norms(points_ref[level].astype(F32), True).astype(BF16)
            rows = with_norms(got_points_ref[level].astype(F32), False).T.astype(BF16)
            values.append(split_two(kernel_values(dot_nn(rows, own))))
        for level, (high, low) in zip(range(first, last), values):
            kernel_ref[level, 0] = high
            kernel_ref[level, 1] = low

    spreads = []

    def spread_start(phase):
        if phase >= len(spans):
            return
        first, width = spans[phase]
        copies = []
        for number in range(1, 1 << width):
            copy = remote(
                gathered_refs[phase].at[0],
                gathered_refs[phase].at[number],
                spread_sems[phase].at[0, number],
                spread_sems[phase].at[1, number],
                (leaf ^ (number << first), rep),
            )
            copy.start()
            copies.append(copy)
            sent.append(copy)
        spreads.append(copies)

    def spread_finish(phase):
        if phase >= len(spans):
            return
        first, width = spans[phase]
        for copy in spreads[phase]:
            copy.wait_recv()
        nodes = [gathered_refs[phase][number] for number in range(1 << width)]
        for level in range(first, first + width):
            sibling_ref[level] = nodes[1]
            if level + 1 == levels:
                return
            on_right = lax.rem(leaf // (1 << level), 2) == 1
            even = jnp.concatenate(nodes[0::2], axis=0)
            odd = jnp.concatenate(nodes[1::2], axis=0)
            parents = dot_wide(jnp.where(on_right, odd, even), top_ref[level, 0]) + dot_wide(
                jnp.where(on_right, even, odd), top_ref[level, 1]
            )
            nodes = [parents[i * OWN : i * OWN + OWN] for i in range(len(nodes) // 2)]
        gathered_refs[phase + 1][0] = nodes[0]
        spread_start(phase + 1)

    def coupling(level):
        rows = stack_two(sibling_ref[level])
        return fold_two(dot_nn(rows, kernel_ref[level, 0])) + fold_two(dot_nn(rows, kernel_ref[level, 1]))

    def up(number, total):
        s_leaf = dot_nn(sorted_ref[number].astype(BF16), basis_ref[number])
        return total + dot_nn(stack_two(s_leaf), transfer_ref[number])

    s_root = fold_two(lax.fori_loop(0, LEAVES, up, jnp.zeros((2 * OWN, RANK), F32), unroll=LEAVES))
    gathered_refs[0][0] = s_root
    greet_wait(partners)
    spread_start(0)
    push_start(0)

    for target in range(REPS):
        for column in range(2):
            top = sorted_ref[column * REPS + target]
            bottom = sorted_ref[(column + 2) * REPS + target]
            vectors_ref[target, :, column * LEAF : (column + 1) * LEAF] = jnp.concatenate(
                [top, bottom], axis=0
            ).astype(BF16)
    window_vectors_ref[1, rep] = vectors_ref[rep]
    vector_moves = [
        (index, side, device, step)
        for index, (side, device) in enumerate(((2, before), (0, after), (1, leaf)))
        for step in range(REPS)
        if side != 1 or step > 0
    ]
    for index, side, device, step in vector_moves:
        target = lax.rem(rep + step, REPS)
        copy = remote(
            vectors_ref.at[target],
            window_vectors_ref.at[side, rep],
            vector_sems.at[0, index, step],
            vector_sems.at[1, index, step],
            (device, target),
        )
        copy.start()
        sent.append(copy)

    row_copies = []

    def sort_points(k):
        number = k * REPS + rep
        points = choose(coordinate_slices(), order_of(order_ref, number))
        columns_ref[rep, k] = points.astype(BF16)
        window_ref[1, k] = with_norms(points, False).T.astype(BF16)

    def send_points(pair):
        span = pl.ds(pair * 2, 2)
        for index, (side, device) in enumerate(((2, before), (0, after))):
            copy = remote(
                window_ref.at[1, span],
                window_ref.at[side, span],
                row_sems.at[0, pair, index],
                row_sems.at[1, pair, index],
                (device, rep),
            )
            copy.start()
            row_copies.append(copy)
            sent.append(copy)
        for step, other in enumerate(others):
            copy = remote(
                columns_ref.at[rep, span],
                columns_ref.at[rep, span],
                column_sems.at[0, pair, step],
                column_sems.at[1, pair, step],
                (leaf, other),
            )
            copy.start()
            sent.append(copy)

    sort_points(0)
    sort_points(1)
    send_points(0)
    push_finish(0)
    spread_finish(0)
    sort_points(2)
    sort_points(3)
    send_points(1)
    push_finish(1)
    spread_finish(1)
    kernels(0, 5)
    push_finish(2)
    kernels(5, 7)

    diagonal = lax.broadcasted_iota(I32, (LEAVES, LEAVES), 0) == lax.broadcasted_iota(
        I32, (LEAVES, LEAVES), 1
    )

    def as_column(row):
        return jnp.sum(jnp.where(diagonal, row, 0.0), axis=1, keepdims=True)

    near = near_ref[...]
    slot = lax.broadcasted_iota(I32, near.shape, 1)
    live = slot.astype(F32) < as_column(count_ref[...].astype(F32))
    admissible = admissible_ref[...]
    lane = lax.broadcasted_iota(I32, (LEAVES, LANES), 1)
    times = jnp.zeros((LEAVES, LANES), F32)
    for entry in range(PARTNERS + QUARTER):
        if entry < PARTNERS:
            named = jnp.where(near == entry * REPS + rep, 1.0, 0.0)
            total = jnp.sum(jnp.where(live, named, 0.0), axis=1, keepdims=True)
        else:
            named = jnp.where(admissible == (entry - PARTNERS) * REPS + rep, 1.0, 0.0)
            total = as_column(jnp.sum(named, axis=0, keepdims=True))
        times = jnp.where(lane == entry, total, times)
    times_ref[...] = times.astype(I32)
    skel_out_ref[...] = skel_leaf_ref[...]

    spread_finish(2)

    running = coupling(levels - 1)
    for level in range(levels - 2, -1, -1):
        side = lax.rem(leaf // (1 << level), 2)
        running = coupling(level) + dot_wide_nt(running, top_ref[level, side])
    t_root_ref[...] = running

    for copy in row_copies:
        copy.wait_recv()
    for pair in range(2):
        span = pl.ds(pair * 2, 2)
        for step, other in enumerate(others):
            source = lax.rem(rep + REPS - 1 - step, REPS)
            remote(
                columns_ref.at[rep, span],
                columns_ref.at[source, span],
                column_sems.at[0, pair, step],
                column_sems.at[1, pair, step],
                (leaf, other),
            ).wait_recv()
    for index, side, device, step in vector_moves:
        source = lax.rem(rep + REPS - step, REPS)
        remote(
            vectors_ref.at[rep],
            window_vectors_ref.at[side, source],
            vector_sems.at[0, index, step],
            vector_sems.at[1, index, step],
            (device, lax.rem(rep + step, REPS)),
        ).wait_recv()
    for copy in sent:
        copy.wait_send()
    push_wait_send()


def near_kernel(
    times_ref,
    columns_ref,
    skel_leaf_ref,
    t_root_ref,
    window_vectors_ref,
    transfer_ref,
    basis_ref,
    window_ref,
    out_ref,
    own_out_ref,
    list_ref,
    own_ref,
    own_skel_ref,
    skel_rows_ref,
    vectors_ref,
    total_ref,
    s_ref,
    t_ref,
    near_shifted_even,
    near_shifted_odd,
    near_even,
    near_odd,
    far_shifted_even,
    far_shifted_odd,
    far_even,
    far_odd,
):
    near_shifted, near_tiles = (near_shifted_even, near_shifted_odd), (near_even, near_odd)
    far_shifted, far_tiles = (far_shifted_even, far_shifted_odd), (far_even, far_odd)
    rep = lax.axis_index("rep")
    root_rows = stack_two(t_root_ref[...])
    t_ref[...] = jnp.zeros_like(t_ref)

    def prepare(leaf, _):
        source = lax.rem(leaf, REPS)
        k = leaf // REPS
        points = columns_ref[source, k].astype(F32)
        columns = with_norms(points, True)
        own_ref[leaf] = columns.astype(BF16)
        marks = one_hot(skel_leaf_ref[pl.ds(leaf, 1), :])
        own_skel_ref[leaf] = with_norms(dot_nn(columns_ref[source, k], marks), True).astype(BF16)
        return 0

    lax.fori_loop(0, LEAVES, prepare, 0, unroll=4)

    def from_root(leaf, _):
        t_ref[leaf, pl.ds(pl.multiple_of(rep * OWN, OWN), OWN), :] = fold_two(
            dot_nt(root_rows, transfer_ref[leaf])
        )
        return 0

    lax.fori_loop(0, LEAVES, from_root, 0, unroll=8)

    for side in range(SIDES):
        for column in range(2):
            span = slice(column * LEAF, (column + 1) * LEAF)
            blocks = [window_vectors_ref[side, source, :, span].astype(F32) for source in range(REPS)]
            vectors_ref[side * QUARTER + column] = jnp.concatenate(
                [block[:OWN] for block in blocks], axis=0
            ).astype(BF16)
            vectors_ref[side * QUARTER + column + 2] = jnp.concatenate(
                [block[OWN:] for block in blocks], axis=0
            ).astype(BF16)
    for k in range(QUARTER):
        leaf = k * REPS + rep
        s_leaf = dot_nn(vectors_ref[QUARTER + k], basis_ref[leaf])
        s_ref[k] = stack_two(s_leaf)
        skel = own_skel_ref[leaf].astype(F32)
        skel_rows_ref[k] = with_norms(skel[:DIM] * -0.5, False).T.astype(BF16)

    total_ref[...] = jnp.zeros_like(total_ref)

    def make_list(first, width):
        def one_leaf(leaf, filled):
            for entry in range(first, first + width):
                list_ref[filled] = leaf * 16 + entry
                filled = filled + jnp.where(times_ref[leaf, entry] > 0, 1, 0)
            return filled

        filled = lax.fori_loop(0, LEAVES, one_leaf, 0, unroll=2)
        for pad in range(4 * WAYS):
            list_ref[filled + pad] = first
        return filled

    def run(filled, product, keep, apply, shifted_refs, tile_refs):
        def start(group, shifted_ref):
            for way in range(WAYS):
                code = list_ref[group * WAYS + way]
                shifted_ref[way] = product(code >> 4, code & 15)

        def middle(shifted_ref, tile_ref):
            for way in range(WAYS):
                keep(tile_ref, way, kernel_values(shifted_ref[way]))

        def finish(group, tile_ref):
            for way in range(WAYS):
                number = group * WAYS + way
                code = list_ref[jnp.maximum(number, 0)]
                leaf, entry = code >> 4, code & 15
                times = jnp.where((number >= 0) & (number < filled), times_ref[leaf, entry], 0)
                apply(leaf, entry, times.astype(F32), tile_ref, way)

        start(0, shifted_refs[0])
        tile_refs[1][...] = jnp.zeros_like(tile_refs[1])

        def step(number, _):
            even = number * 2
            start(even + 1, shifted_refs[1])
            middle(shifted_refs[0], tile_refs[0])
            finish(even - 1, tile_refs[1])
            start(even + 2, shifted_refs[0])
            middle(shifted_refs[1], tile_refs[1])
            finish(even, tile_refs[0])
            return 0

        steps = (filled + 2 * WAYS - 1) // (2 * WAYS)
        lax.fori_loop(0, steps, step, 0)
        finish(2 * steps - 1, tile_refs[1])

    def near_keep(tile_ref, way, values):
        tile_ref[way] = values.astype(BF16)

    def near_apply(leaf, entry, times, tile_ref, way):
        total_ref[leaf] += dot_nn(vectors_ref[entry], tile_ref[way]) * times

    run(
        make_list(0, PARTNERS),
        lambda leaf, entry: dot_nn(window_ref[entry], own_ref[leaf]),
        near_keep,
        near_apply,
        near_shifted,
        near_tiles,
    )

    def far_keep(tile_ref, way, values):
        high, low = split_two(values)
        tile_ref[way, 0] = high
        tile_ref[way, 1] = low

    def far_apply(leaf, entry, times, tile_ref, way):
        rows = s_ref[entry - PARTNERS]
        term = fold_two(dot_nn(rows, tile_ref[way, 0])) + dot_nn(rows[:RHS], tile_ref[way, 1])
        t_ref[leaf] += term * times

    run(
        make_list(PARTNERS, QUARTER),
        lambda leaf, entry: dot_nn(skel_rows_ref[entry - PARTNERS], own_skel_ref[leaf]),
        far_keep,
        far_apply,
        far_shifted,
        far_tiles,
    )

    for leaf in range(LEAVES):
        total_ref[leaf] += dot_wide_nt(t_ref[leaf], basis_ref[leaf])
    mine = pl.ds(pl.multiple_of(rep * OWN, OWN), OWN)
    for leaf in range(LEAVES):
        own_out_ref[:, leaf * LEAF : (leaf + 1) * LEAF] = total_ref[leaf, mine, :]
    for leaf in range(LEAVES // 2):
        top = total_ref[leaf].reshape(REPS, OWN, LEAF)
        bottom = total_ref[leaf + LEAVES // 2].reshape(REPS, OWN, LEAF)
        out_ref[:, :, leaf * LEAF : (leaf + 1) * LEAF] = jnp.concatenate([top, bottom], axis=1).astype(BF16)


def combine_kernel(part_ref, own_ref, order_ref, out_ref, got_ref, sems):
    leaf = lax.axis_index("leaf")
    rep = lax.axis_index("rep")
    half = PTS // 2
    width = half // CHUNKS
    partners = [(leaf, lax.rem(rep + step, REPS)) for step in range(1, REPS)]
    greet_signals(partners)
    greet_wait(partners)
    copies = []
    for chunk in range(CHUNKS):
        span = pl.ds(chunk * width, width)
        for index, partner in enumerate(partners):
            copy = remote(
                part_ref.at[partner[1], :, span],
                got_ref.at[index, :, span],
                sems.at[0, index, chunk],
                sems.at[1, index, chunk],
                partner,
            )
            copy.start()
            copies.append(copy)

    scattered = jnp.zeros((LEAVES * 2 * OWN, LEAF), F32)
    for chunk in range(CHUNKS):
        here = [(number, (number * half + chunk * width) // LANES) for number in range(2)]
        positions = jnp.concatenate(
            [
                order_ref[first + at : first + at + 1, :]
                for _, first in here
                for at in range(width // LANES)
            ],
            axis=1,
        )
        marks = one_hot(positions & 255)
        high = jnp.broadcast_to(positions >> 8, (2 * OWN, 2 * width))
        for copy in copies[chunk * len(partners) : (chunk + 1) * len(partners)]:
            copy.wait_recv()
        totals = []
        for number, first in here:
            rows = slice(number * OWN, (number + 1) * OWN)
            total = -own_ref[:, first * LANES : first * LANES + width]
            for index in range(REPS - 1):
                total = total - got_ref[index, :, chunk * width : (chunk + 1) * width].astype(F32)[rows]
            totals.append(total)
        total = jnp.concatenate(totals, axis=1)
        rounded = total.astype(BF16).astype(F32)
        terms = jnp.concatenate([rounded, total - rounded], axis=0)
        rows = jnp.concatenate(
            [jnp.where(high == source, terms, 0.0).astype(BF16) for source in range(LEAVES)], axis=0
        )
        scattered = scattered + dot_nt(rows, marks)
    for source in range(LEAVES):
        first = source * 2 * OWN
        out_ref[:, source * LEAF : (source + 1) * LEAF] = (
            scattered[first : first + OWN] + scattered[first + OWN : first + 2 * OWN]
        )
    for copy in copies:
        copy.wait_send()


def vmem(count):
    return [pl.BlockSpec(memory_space=pltpu.VMEM)] * count


def shape(dims, dtype):
    return jax.ShapeDtypeStruct(dims, dtype)


def params(collective_id=None):
    if collective_id is None:
        return pltpu.CompilerParams(vmem_limit_bytes=VMEM_LIMIT)
    return pltpu.CompilerParams(
        collective_id=collective_id, has_side_effects=True, vmem_limit_bytes=VMEM_LIMIT
    )


def on_device(
    count,
    coords,
    right_sides,
    leaf_order,
    leaf_basis,
    leaf_transfer,
    top_transfer,
    skel_leaf,
    skel_root,
    admissible,
    near_leaves,
    near_count,
):
    levels = count.bit_length() - 1
    spans = phases_of(levels)
    order = leaf_order.reshape(BLOCKS, LANES)
    dma = pltpu.SemaphoreType.DMA
    sorted_vectors = pl.pallas_call(
        vectors_kernel,
        out_shape=shape((LEAVES, OWN, LEAF), F32),
        in_specs=vmem(2),
        out_specs=pl.BlockSpec(memory_space=pltpu.VMEM),
        compiler_params=params(),
        cost_estimate=pl.CostEstimate(flops=10**9, bytes_accessed=10**6, transcendentals=0),
        name="vectors",
    )(
        right_sides.reshape(OWN, LEAVES, LEAF).transpose(1, 0, 2).reshape(LEAVES * OWN, LEAF),
        order,
    )
    window, columns, window_vectors, t_root, times, skel_here = pl.pallas_call(
        functools.partial(gather_kernel, count, levels),
        out_shape=(
            shape((SIDES, QUARTER, LEAF, LANES), BF16),
            shape((REPS, QUARTER, DIM, LEAF), BF16),
            shape((SIDES, REPS, 2 * OWN, 2 * LEAF), BF16),
            shape((OWN, RANK), F32),
            shape((LEAVES, LANES), I32),
            shape((LEAVES, RANK), I32),
        ),
        in_specs=vmem(11),
        out_specs=tuple(vmem(6)),
        scratch_shapes=[
            pltpu.VMEM((REPS, 2 * OWN, 2 * LEAF), BF16),
            pltpu.VMEM((levels, DIM, RANK), BF16),
            pltpu.VMEM((levels, DIM, RANK), BF16),
            pltpu.VMEM((levels, 2, RANK, RANK), BF16),
            pltpu.VMEM((levels, OWN, RANK), F32),
        ]
        + [pltpu.VMEM((1 << width, OWN, RANK), F32) for _, width in spans]
        + [dma((2, 1 << width)) for _, width in spans]
        + [
            dma((2, 2, 2)),
            dma((2, 2, REPS - 1)),
            dma((2, SIDES, REPS)),
            dma((2, levels, 1 << (max(PHASES) - 1))),
        ],
        compiler_params=params(0),
        name="gather",
    )(
        coords,
        sorted_vectors,
        order,
        leaf_basis,
        leaf_transfer,
        top_transfer[: levels - 1],
        skel_root,
        skel_leaf,
        admissible.T,
        near_leaves,
        near_count.reshape(1, LEAVES),
    )

    part, own_part = pl.pallas_call(
        near_kernel,
        out_shape=(shape((REPS, 2 * OWN, PTS // 2), BF16), shape((OWN, PTS), F32)),
        in_specs=[pl.BlockSpec(memory_space=pltpu.SMEM)] + vmem(7),
        out_specs=tuple(vmem(2)),
        scratch_shapes=[
            pltpu.SMEM((LEAVES * PARTNERS + 4 * WAYS + 8,), I32),
            pltpu.VMEM((LEAVES, LANES, LEAF), BF16),
            pltpu.VMEM((LEAVES, LANES, RANK), BF16),
            pltpu.VMEM((QUARTER, RANK, LANES), BF16),
            pltpu.VMEM((PARTNERS, RHS, LEAF), BF16),
            pltpu.VMEM((LEAVES, RHS, LEAF), F32),
            pltpu.VMEM((QUARTER, 2 * RHS, RANK), BF16),
            pltpu.VMEM((LEAVES, RHS, RANK), F32),
        ]
        + [pltpu.VMEM((WAYS, LEAF, LEAF), F32)] * 2
        + [pltpu.VMEM((WAYS, LEAF, LEAF), BF16)] * 2
        + [pltpu.VMEM((WAYS, RANK, RANK), F32)] * 2
        + [pltpu.VMEM((WAYS, 2, RANK, RANK), BF16)] * 2,
        compiler_params=params(),
        name="near",
    )(
        times,
        columns,
        skel_here,
        t_root,
        window_vectors,
        leaf_transfer,
        leaf_basis,
        window.reshape(PARTNERS, LEAF, LANES),
    )

    negative = pl.pallas_call(
        combine_kernel,
        out_shape=shape((OWN, PTS), F32),
        in_specs=vmem(3),
        out_specs=pl.BlockSpec(memory_space=pltpu.VMEM),
        scratch_shapes=[
            pltpu.VMEM((REPS - 1, 2 * OWN, PTS // 2), BF16),
            dma((2, REPS - 1, CHUNKS)),
        ],
        compiler_params=params(1),
        name="combine",
    )(part, own_part, order)
    return -negative


def solution(mesh):
    placed = (
        P(None, "leaf"),
        P("rep", "leaf"),
        P("leaf"),
        P("leaf", None, None),
        P("leaf", None, None),
        P(),
        P("leaf", None),
        P("leaf", None),
        P("leaf", None),
        P("leaf", None),
        P("leaf"),
    )
    return jax.shard_map(
        functools.partial(on_device, mesh.shape["leaf"]),
        mesh=mesh,
        in_specs=placed,
        out_specs=P("rep", "leaf"),
        check_vma=False,
    )
```

```python
import functools

import jax
import jax.numpy as jnp
from jax import lax
from jax.experimental import pallas as pl
from jax.experimental.pallas import tpu as pltpu
from jax.sharding import PartitionSpec as P

MESH = pl.DeviceIdType.MESH
F32 = jnp.float32
BF16 = jnp.bfloat16
I32 = jnp.int32

DIM = 64
RANK = 128
LEAF = 256
LEAVES = 16
PTS = 4096
LANES = 128
BLOCKS = PTS // LANES
REPS = 4
QUARTER = LEAVES // REPS
OWN = 8
RHS = 32
SIDES = 3
PARTNERS = SIDES * QUARTER
PHASES = (3, 2, 2)
WAYS = 2
CHUNKS = 4
VMEM_LIMIT = 24 * 1024 * 1024


def dot_nn(a, b):
    return lax.dot_general(a, b, (((1,), (0,)), ((), ())), preferred_element_type=F32)


def dot_nt(a, b):
    return lax.dot_general(a, b, (((1,), (1,)), ((), ())), preferred_element_type=F32)


def kernel_values(shifted):
    shifted = jnp.maximum(shifted, 1.0)
    return jnp.exp((shifted * -0.5) * lax.rsqrt(shifted))


def split_two(x):
    high = x.astype(BF16)
    return high, (x - high.astype(F32)).astype(BF16)


def stack_two(x):
    high = x.astype(BF16).astype(F32)
    return jnp.concatenate([high, x - high], axis=0).astype(BF16)


def fold_two(x):
    half = x.shape[0] // 2
    return x[:half] + x[half:]


def dot_wide(x, matrix):
    return fold_two(dot_nn(stack_two(x), matrix))


def dot_wide_nt(x, matrix):
    return fold_two(dot_nt(stack_two(x), matrix))


def dot_both_wide(x, matrix):
    rows = stack_two(x)
    high, low = split_two(matrix)
    return fold_two(dot_nn(rows, high)) + fold_two(dot_nn(rows, low))


def with_norms(points, own):
    count = points.shape[1]
    norm = jnp.sum(points * points, axis=0, keepdims=True)
    if own:
        norm = norm + 1.0
    high = norm.astype(BF16).astype(F32)
    rest = norm - high
    mid = rest.astype(BF16).astype(F32)
    low = rest - mid
    row = lax.broadcasted_iota(I32, (16, count), 0)
    if not own:
        row = row - 3
    tail = jnp.where(row == 0, high, jnp.where(row == 1, mid, jnp.where(row == 2, low, 0.0)))
    ones = lax.broadcasted_iota(I32, (16, count), 0) - (3 if own else 0)
    tail = jnp.where((ones >= 0) & (ones < 3), 1.0, tail)
    head = points * -2.0 if own else points
    return jnp.concatenate([head, tail, jnp.zeros((LANES - DIM - 16, count), F32)], axis=0)


def one_hot(low):
    row = lax.broadcasted_iota(I32, (LEAF, low.shape[1]), 0)
    return jnp.where(row == low, 1.0, 0.0).astype(BF16)


def choose(slices, positions):
    marks = one_hot(positions & 255)
    rows = slices[0].shape[0]
    high = jnp.broadcast_to(positions >> 8, (rows, positions.shape[1]))
    out = jnp.zeros((rows, positions.shape[1]), F32)
    together = min(len(slices), 512 // rows)
    for first in range(0, len(slices), together):
        block = dot_nn(jnp.concatenate(slices[first : first + together], axis=0), marks)
        for number in range(together):
            out = jnp.where(high == first + number, block[number * rows : (number + 1) * rows], out)
    return out


def order_of(order_ref, leaf):
    return jnp.concatenate([order_ref[pl.ds(leaf * 2 + half, 1), :] for half in range(2)], axis=1)


def pick(table, lanes):
    return jnp.take_along_axis(table, lanes, axis=1, mode="promise_in_bounds")


def greet_signals(devices):
    barrier = pltpu.get_barrier_semaphore()
    for device in devices:
        pl.semaphore_signal(barrier, inc=1, device_id=device, device_id_type=MESH)


def greet_wait(devices):
    pl.semaphore_wait(pltpu.get_barrier_semaphore(), len(devices))


def remote(source, target, send_sem, recv_sem, device):
    return pltpu.make_async_remote_copy(
        src_ref=source,
        dst_ref=target,
        send_sem=send_sem,
        recv_sem=recv_sem,
        device_id=device,
        device_id_type=MESH,
    )


def phases_of(levels):
    spans, first = [], 0
    for width in PHASES:
        width = min(width, levels - first)
        if width > 0:
            spans.append((first, width))
        first += width
    return spans


def vectors_kernel(rows_ref, order_ref, sorted_ref):
    vector_rows = rows_ref[...]

    def sort_vectors(number, _):
        positions = order_of(order_ref, number)
        block = dot_nn(vector_rows, one_hot(positions & 255))
        high = jnp.broadcast_to(positions >> 8, (OWN, LEAF))
        out = jnp.zeros((OWN, LEAF), F32)
        for source in range(LEAVES):
            out = jnp.where(high == source, block[source * OWN : (source + 1) * OWN], out)
        sorted_ref[number] = out
        return 0

    lax.fori_loop(0, LEAVES, sort_vectors, 0, unroll=4)


def gather_kernel(
    count,
    levels,
    coords_ref,
    sorted_ref,
    order_ref,
    basis_ref,
    transfer_ref,
    top_ref,
    skel_root_ref,
    skel_leaf_ref,
    admissible_ref,
    near_ref,
    count_ref,
    halo_ref,
    columns_ref,
    window_vectors_ref,
    t_root_ref,
    times_ref,
    skel_out_ref,
    vectors_ref,
    points_ref,
    got_points_ref,
    kernel_ref,
    sibling_ref,
    *rest,
):
    spans = phases_of(levels)
    gathered_refs = rest[: len(spans)]
    spread_sems = rest[len(spans) : 2 * len(spans)]
    row_sems, column_sems, vector_sems, push_sems, swap_sems = rest[2 * len(spans) :]

    leaf = lax.axis_index("leaf")
    rep = lax.axis_index("rep")
    before = lax.rem(leaf + count - 1, count)
    after = lax.rem(leaf + 1, count)
    others = [lax.rem(rep + step, REPS) for step in range(1, REPS)]
    partners = [(side, other) for side in (before, after) for other in [rep] + others]
    partners += [(leaf, other) for other in others]
    for first, width in spans:
        partners += [(leaf ^ (number << first), rep) for number in range(1, 1 << width)]
    greet_signals(partners)

    def coordinate_slices():
        return [coords_ref[:, high * LEAF : (high + 1) * LEAF] for high in range(LEAVES)]

    at = jnp.broadcast_to(skel_root_ref[...], (8, LANES))
    at_high = at >> 7
    at_low = at & 127
    initial = jnp.zeros((8, LANES), I32)
    for source in range(BLOCKS):
        table = jnp.broadcast_to(order_ref[source : source + 1, :], (8, LANES))
        initial = jnp.where(at_high == source, pick(table, at_low), initial)
    points_ref[0] = choose(coordinate_slices(), initial[:1]).astype(BF16)
    sent = []

    pushes = [[] for _ in spans]
    core = lax.rem(leaf, 2)

    def rows_of(half):
        return pl.ds(pl.multiple_of(half * (DIM // 2), DIM // 2), DIM // 2)

    def push_start(phase):
        if phase >= len(spans):
            return
        first, width = spans[phase]
        for level in range(first, first + width):
            for number in range(1 << (level - first), 2 << (level - first)):
                device = leaf ^ (number << first)
                span = pl.ds(0, DIM) if level == 0 else rows_of(lax.rem(device, 2))
                copy = remote(
                    points_ref.at[first, span],
                    got_points_ref.at[level, span],
                    push_sems.at[0, level, number - (1 << (level - first))],
                    push_sems.at[1, level, 0],
                    (device, rep),
                )
                pushes[phase].append((level, copy))
                if level == first:
                    copy.start()
                else:
                    pl.when(lax.rem(leaf // (1 << first), 1 << (level - first)) == 0)(copy.start)

    def push_finish(phase):
        if phase >= len(spans):
            return
        first, width = spans[phase]
        for level in range(first, first + width):
            span = pl.ds(0, DIM) if level == 0 else rows_of(core)
            remote(
                points_ref.at[first, span],
                got_points_ref.at[level, span],
                push_sems.at[0, level, 0],
                push_sems.at[1, level, 0],
                (leaf ^ (1 << level), rep),
            ).wait_recv()
            if level > 0:
                copy = remote(
                    got_points_ref.at[level, span],
                    got_points_ref.at[level, span],
                    swap_sems.at[0, level],
                    swap_sems.at[1, level],
                    (leaf ^ 1, rep),
                )
                copy.start()
                sent.append(copy)
        for level in range(first, first + width):
            if level > 0:
                span = rows_of(1 - core)
                remote(
                    got_points_ref.at[level, span],
                    got_points_ref.at[level, span],
                    swap_sems.at[0, level],
                    swap_sems.at[1, level],
                    (leaf ^ 1, rep),
                ).wait_recv()
            if level + 1 < levels:
                on_right = lax.rem(leaf // (1 << level), 2) == 1
                points_ref[level + 1] = jnp.where(
                    on_right, got_points_ref[level].astype(F32), points_ref[level].astype(F32)
                ).astype(BF16)
        push_start(phase + 1)

    def push_wait_send():
        for (first, width), copies in zip(spans, pushes):
            for level, copy in copies:
                if level == first:
                    copy.wait_send()
                else:
                    pl.when(lax.rem(leaf // (1 << first), 1 << (level - first)) == 0)(copy.wait_send)

    def kernels(first, last):
        first, last = min(first, levels), min(last, levels)
        values = []
        for level in range(first, last):
            own = with_norms(points_ref[level].astype(F32), True).astype(BF16)
            rows = with_norms(got_points_ref[level].astype(F32), False).T.astype(BF16)
            values.append(split_two(kernel_values(dot_nn(rows, own))))
        for level, (high, low) in zip(range(first, last), values):
            kernel_ref[level, 0] = high
            kernel_ref[level, 1] = low

    spreads = []

    def spread_start(phase):
        if phase >= len(spans):
            return
        first, width = spans[phase]
        copies = []
        for number in range(1, 1 << width):
            copy = remote(
                gathered_refs[phase].at[0],
                gathered_refs[phase].at[number],
                spread_sems[phase].at[0, number],
                spread_sems[phase].at[1, number],
                (leaf ^ (number << first), rep),
            )
            copy.start()
            copies.append(copy)
            sent.append(copy)
        spreads.append(copies)

    def spread_finish(phase):
        if phase >= len(spans):
            return
        first, width = spans[phase]
        for copy in spreads[phase]:
            copy.wait_recv()
        nodes = [gathered_refs[phase][number] for number in range(1 << width)]
        for level in range(first, first + width):
            sibling_ref[level] = nodes[1]
            if level + 1 == levels:
                return
            on_right = lax.rem(leaf // (1 << level), 2) == 1
            even = jnp.concatenate(nodes[0::2], axis=0)
            odd = jnp.concatenate(nodes[1::2], axis=0)
            parents = dot_wide(jnp.where(on_right, odd, even), top_ref[level, 0]) + dot_wide(
                jnp.where(on_right, even, odd), top_ref[level, 1]
            )
            nodes = [parents[i * OWN : i * OWN + OWN] for i in range(len(nodes) // 2)]
        gathered_refs[phase + 1][0] = nodes[0]
        spread_start(phase + 1)

    def coupling(level):
        rows = stack_two(sibling_ref[level])
        return fold_two(dot_nn(rows, kernel_ref[level, 0])) + fold_two(dot_nn(rows, kernel_ref[level, 1]))

    def up(number, total):
        s_leaf = dot_nn(sorted_ref[number].astype(BF16), basis_ref[number])
        return total + dot_nn(stack_two(s_leaf), transfer_ref[number])

    s_root = fold_two(lax.fori_loop(0, LEAVES, up, jnp.zeros((2 * OWN, RANK), F32), unroll=LEAVES))
    gathered_refs[0][0] = s_root
    greet_wait(partners)
    spread_start(0)
    push_start(0)

    for target in range(REPS):
        for column in range(2):
            top = sorted_ref[column * REPS + target]
            bottom = sorted_ref[(column + 2) * REPS + target]
            vectors_ref[target, :, column * LEAF : (column + 1) * LEAF] = jnp.concatenate(
                [top, bottom], axis=0
            ).astype(BF16)
    window_vectors_ref[1, rep] = vectors_ref[rep]
    vector_moves = [
        (index, side, device, step)
        for index, (side, device) in enumerate(((2, before), (0, after), (1, leaf)))
        for step in range(REPS)
        if side != 1 or step > 0
    ]
    for index, side, device, step in vector_moves:
        target = lax.rem(rep + step, REPS)
        copy = remote(
            vectors_ref.at[target],
            window_vectors_ref.at[side, rep],
            vector_sems.at[0, index, step],
            vector_sems.at[1, index, step],
            (device, target),
        )
        copy.start()
        sent.append(copy)

    row_copies = []

    def sort_points(k):
        number = k * REPS + rep
        points = choose(coordinate_slices(), order_of(order_ref, number))
        columns_ref[rep, k] = points.astype(BF16)

    def send_points(pair):
        span = pl.ds(pair * 2, 2)
        for index, (side, device) in enumerate(((1, before), (0, after))):
            copy = remote(
                columns_ref.at[rep, span],
                halo_ref.at[side, span],
                row_sems.at[0, pair, index],
                row_sems.at[1, pair, index],
                (device, rep),
            )
            copy.start()
            row_copies.append(copy)
            sent.append(copy)
        for step in (0, 2):
            copy = remote(
                columns_ref.at[rep, span],
                columns_ref.at[rep, span],
                column_sems.at[0, pair, step],
                column_sems.at[1, pair, step],
                (leaf, others[step]),
            )
            copy.start()
            sent.append(copy)

    def got_columns(pair, step):
        span = pl.ds(pair * 2, 2)
        source = lax.rem(rep + REPS - 1 - step, REPS)
        remote(
            columns_ref.at[rep, span],
            columns_ref.at[source, span],
            column_sems.at[0, pair, step],
            column_sems.at[1, pair, step],
            (leaf, others[step]),
        ).wait_recv()

    def pass_columns(pair, step):
        got_columns(pair, step)
        span = pl.ds(pair * 2, 2)
        source = lax.rem(rep + REPS - 1 - step, REPS)
        copy = remote(
            columns_ref.at[source, span],
            columns_ref.at[source, span],
            column_sems.at[0, pair, 1],
            column_sems.at[1, pair, 1],
            (leaf, others[step]),
        )
        copy.start()
        sent.append(copy)

    sort_points(0)
    sort_points(1)
    send_points(0)
    push_finish(0)
    spread_finish(0)
    sort_points(2)
    sort_points(3)
    send_points(1)
    pass_columns(0, 0)
    push_finish(1)
    spread_finish(1)
    pass_columns(1, 2)
    kernels(0, 5)
    push_finish(2)
    kernels(5, 7)

    diagonal = lax.broadcasted_iota(I32, (LEAVES, LEAVES), 0) == lax.broadcasted_iota(
        I32, (LEAVES, LEAVES), 1
    )

    def as_column(row):
        return jnp.sum(jnp.where(diagonal, row, 0.0), axis=1, keepdims=True)

    near = near_ref[...]
    slot = lax.broadcasted_iota(I32, near.shape, 1)
    live = slot.astype(F32) < as_column(count_ref[...].astype(F32))
    admissible = admissible_ref[...]
    lane = lax.broadcasted_iota(I32, (LEAVES, LANES), 1)
    times = jnp.zeros((LEAVES, LANES), F32)
    for entry in range(PARTNERS + QUARTER):
        if entry < PARTNERS:
            named = jnp.where(near == entry * REPS + rep, 1.0, 0.0)
            total = jnp.sum(jnp.where(live, named, 0.0), axis=1, keepdims=True)
        else:
            named = jnp.where(admissible == (entry - PARTNERS) * REPS + rep, 1.0, 0.0)
            total = as_column(jnp.sum(named, axis=0, keepdims=True))
        times = jnp.where(lane == entry, total, times)
    times_ref[...] = times.astype(I32)
    skel_out_ref[...] = skel_leaf_ref[...]

    spread_finish(2)

    running = coupling(levels - 1)
    for level in range(levels - 2, -1, -1):
        side = lax.rem(leaf // (1 << level), 2)
        running = coupling(level) + dot_wide_nt(running, top_ref[level, side])
    t_root_ref[...] = running

    for copy in row_copies:
        copy.wait_recv()
    got_columns(0, 2)
    got_columns(1, 0)
    for pair in range(2):
        span = pl.ds(pair * 2, 2)
        remote(
            columns_ref.at[rep, span],
            columns_ref.at[lax.rem(rep + 2, REPS), span],
            column_sems.at[0, pair, 1],
            column_sems.at[1, pair, 1],
            (leaf, others[0]),
        ).wait_recv()
    for index, side, device, step in vector_moves:
        source = lax.rem(rep + REPS - step, REPS)
        remote(
            vectors_ref.at[rep],
            window_vectors_ref.at[side, source],
            vector_sems.at[0, index, step],
            vector_sems.at[1, index, step],
            (device, lax.rem(rep + step, REPS)),
        ).wait_recv()
    for copy in sent:
        copy.wait_send()
    push_wait_send()


def near_kernel(
    times_ref,
    columns_ref,
    skel_leaf_ref,
    t_root_ref,
    window_vectors_ref,
    transfer_ref,
    basis_ref,
    halo_ref,
    out_ref,
    own_out_ref,
    list_ref,
    window_ref,
    own_ref,
    own_skel_ref,
    skel_rows_ref,
    vectors_ref,
    total_ref,
    s_ref,
    t_ref,
    near_shifted_even,
    near_shifted_odd,
    near_even,
    near_odd,
    far_shifted_even,
    far_shifted_odd,
    far_even,
    far_odd,
):
    near_shifted, near_tiles = (near_shifted_even, near_shifted_odd), (near_even, near_odd)
    far_shifted, far_tiles = (far_shifted_even, far_shifted_odd), (far_even, far_odd)
    rep = lax.axis_index("rep")
    root_rows = stack_two(t_root_ref[...])
    t_ref[...] = jnp.zeros_like(t_ref)

    def prepare(leaf, _):
        source = lax.rem(leaf, REPS)
        k = leaf // REPS
        points = columns_ref[source, k].astype(F32)
        columns = with_norms(points, True)
        own_ref[leaf] = columns.astype(BF16)
        marks = one_hot(skel_leaf_ref[pl.ds(leaf, 1), :])
        own_skel_ref[leaf] = with_norms(dot_nn(columns_ref[source, k], marks), True).astype(BF16)
        return 0

    lax.fori_loop(0, LEAVES, prepare, 0, unroll=4)

    def partner_rows(k, _):
        for side, points in enumerate((halo_ref[0, k], columns_ref[rep, k], halo_ref[1, k])):
            window_ref[side * QUARTER + k] = with_norms(points.astype(F32), False).T.astype(BF16)
        return 0

    lax.fori_loop(0, QUARTER, partner_rows, 0, unroll=2)

    def from_root(leaf, _):
        t_ref[leaf, pl.ds(pl.multiple_of(rep * OWN, OWN), OWN), :] = fold_two(
            dot_nt(root_rows, transfer_ref[leaf])
        )
        return 0

    lax.fori_loop(0, LEAVES, from_root, 0, unroll=8)

    for side in range(SIDES):
        for column in range(2):
            span = slice(column * LEAF, (column + 1) * LEAF)
            blocks = [window_vectors_ref[side, source, :, span].astype(F32) for source in range(REPS)]
            vectors_ref[side * QUARTER + column] = jnp.concatenate(
                [block[:OWN] for block in blocks], axis=0
            ).astype(BF16)
            vectors_ref[side * QUARTER + column + 2] = jnp.concatenate(
                [block[OWN:] for block in blocks], axis=0
            ).astype(BF16)
    for k in range(QUARTER):
        leaf = k * REPS + rep
        s_leaf = dot_nn(vectors_ref[QUARTER + k], basis_ref[leaf])
        s_ref[k] = stack_two(s_leaf)
        skel = own_skel_ref[leaf].astype(F32)
        skel_rows_ref[k] = with_norms(skel[:DIM] * -0.5, False).T.astype(BF16)

    total_ref[...] = jnp.zeros_like(total_ref)

    def make_list(first, width):
        def one_leaf(leaf, filled):
            for entry in range(first, first + width):
                list_ref[filled] = leaf * 16 + entry
                filled = filled + jnp.where(times_ref[leaf, entry] > 0, 1, 0)
            return filled

        filled = lax.fori_loop(0, LEAVES, one_leaf, 0, unroll=2)
        for pad in range(4 * WAYS):
            list_ref[filled + pad] = first
        return filled

    def run(filled, product, keep, apply, shifted_refs, tile_refs):
        def start(group, shifted_ref):
            for way in range(WAYS):
                code = list_ref[group * WAYS + way]
                shifted_ref[way] = product(code >> 4, code & 15)

        def middle(shifted_ref, tile_ref):
            for way in range(WAYS):
                keep(tile_ref, way, kernel_values(shifted_ref[way]))

        def finish(group, tile_ref):
            for way in range(WAYS):
                number = group * WAYS + way
                code = list_ref[jnp.maximum(number, 0)]
                leaf, entry = code >> 4, code & 15
                times = jnp.where((number >= 0) & (number < filled), times_ref[leaf, entry], 0)
                apply(leaf, entry, times.astype(F32), tile_ref, way)

        start(0, shifted_refs[0])
        tile_refs[1][...] = jnp.zeros_like(tile_refs[1])

        def step(number, _):
            even = number * 2
            start(even + 1, shifted_refs[1])
            middle(shifted_refs[0], tile_refs[0])
            finish(even - 1, tile_refs[1])
            start(even + 2, shifted_refs[0])
            middle(shifted_refs[1], tile_refs[1])
            finish(even, tile_refs[0])
            return 0

        steps = (filled + 2 * WAYS - 1) // (2 * WAYS)
        lax.fori_loop(0, steps, step, 0)
        finish(2 * steps - 1, tile_refs[1])

    def near_keep(tile_ref, way, values):
        tile_ref[way] = values.astype(BF16)

    def near_apply(leaf, entry, times, tile_ref, way):
        total_ref[leaf] += dot_nn(vectors_ref[entry], tile_ref[way]) * times

    run(
        make_list(0, PARTNERS),
        lambda leaf, entry: dot_nn(window_ref[entry], own_ref[leaf]),
        near_keep,
        near_apply,
        near_shifted,
        near_tiles,
    )

    def far_keep(tile_ref, way, values):
        high, low = split_two(values)
        tile_ref[way, 0] = high
        tile_ref[way, 1] = low

    def far_apply(leaf, entry, times, tile_ref, way):
        rows = s_ref[entry - PARTNERS]
        term = fold_two(dot_nn(rows, tile_ref[way, 0])) + dot_nn(rows[:RHS], tile_ref[way, 1])
        t_ref[leaf] += term * times

    run(
        make_list(PARTNERS, QUARTER),
        lambda leaf, entry: dot_nn(skel_rows_ref[entry - PARTNERS], own_skel_ref[leaf]),
        far_keep,
        far_apply,
        far_shifted,
        far_tiles,
    )

    for leaf in range(LEAVES):
        total_ref[leaf] += dot_wide_nt(t_ref[leaf], basis_ref[leaf])
    mine = pl.ds(pl.multiple_of(rep * OWN, OWN), OWN)
    for leaf in range(LEAVES):
        own_out_ref[:, leaf * LEAF : (leaf + 1) * LEAF] = total_ref[leaf, mine, :]
    for leaf in range(LEAVES // 2):
        top = total_ref[leaf].reshape(REPS, OWN, LEAF)
        bottom = total_ref[leaf + LEAVES // 2].reshape(REPS, OWN, LEAF)
        out_ref[:, :, leaf * LEAF : (leaf + 1) * LEAF] = jnp.concatenate([top, bottom], axis=1).astype(BF16)


def combine_kernel(part_ref, own_ref, order_ref, out_ref, got_ref, sems):
    leaf = lax.axis_index("leaf")
    rep = lax.axis_index("rep")
    half = PTS // 2
    width = half // CHUNKS
    partners = [(leaf, lax.rem(rep + step, REPS)) for step in range(1, REPS)]
    greet_signals(partners)
    greet_wait(partners)
    copies = []
    for chunk in range(CHUNKS):
        span = pl.ds(chunk * width, width)
        for index, partner in enumerate(partners):
            copy = remote(
                part_ref.at[partner[1], :, span],
                got_ref.at[index, :, span],
                sems.at[0, index, chunk],
                sems.at[1, index, chunk],
                partner,
            )
            copy.start()
            copies.append(copy)

    scattered = jnp.zeros((LEAVES * 2 * OWN, LEAF), F32)
    for chunk in range(CHUNKS):
        here = [(number, (number * half + chunk * width) // LANES) for number in range(2)]
        positions = jnp.concatenate(
            [
                order_ref[first + at : first + at + 1, :]
                for _, first in here
                for at in range(width // LANES)
            ],
            axis=1,
        )
        marks = one_hot(positions & 255)
        high = jnp.broadcast_to(positions >> 8, (2 * OWN, 2 * width))
        for copy in copies[chunk * len(partners) : (chunk + 1) * len(partners)]:
            copy.wait_recv()
        totals = []
        for number, first in here:
            rows = slice(number * OWN, (number + 1) * OWN)
            total = -own_ref[:, first * LANES : first * LANES + width]
            for index in range(REPS - 1):
                total = total - got_ref[index, :, chunk * width : (chunk + 1) * width].astype(F32)[rows]
            totals.append(total)
        total = jnp.concatenate(totals, axis=1)
        rounded = total.astype(BF16).astype(F32)
        terms = jnp.concatenate([rounded, total - rounded], axis=0)
        rows = jnp.concatenate(
            [jnp.where(high == source, terms, 0.0).astype(BF16) for source in range(LEAVES)], axis=0
        )
        scattered = scattered + dot_nt(rows, marks)
    for source in range(LEAVES):
        first = source * 2 * OWN
        out_ref[:, source * LEAF : (source + 1) * LEAF] = (
            scattered[first : first + OWN] + scattered[first + OWN : first + 2 * OWN]
        )
    for copy in copies:
        copy.wait_send()


def vmem(count):
    return [pl.BlockSpec(memory_space=pltpu.VMEM)] * count


def shape(dims, dtype):
    return jax.ShapeDtypeStruct(dims, dtype)


def params(collective_id=None):
    if collective_id is None:
        return pltpu.CompilerParams(vmem_limit_bytes=VMEM_LIMIT)
    return pltpu.CompilerParams(
        collective_id=collective_id, has_side_effects=True, vmem_limit_bytes=VMEM_LIMIT
    )


def on_device(
    count,
    coords,
    right_sides,
    leaf_order,
    leaf_basis,
    leaf_transfer,
    top_transfer,
    skel_leaf,
    skel_root,
    admissible,
    near_leaves,
    near_count,
):
    levels = count.bit_length() - 1
    spans = phases_of(levels)
    order = leaf_order.reshape(BLOCKS, LANES)
    dma = pltpu.SemaphoreType.DMA
    sorted_vectors = pl.pallas_call(
        vectors_kernel,
        out_shape=shape((LEAVES, OWN, LEAF), F32),
        in_specs=vmem(2),
        out_specs=pl.BlockSpec(memory_space=pltpu.VMEM),
        compiler_params=params(),
        cost_estimate=pl.CostEstimate(flops=10**9, bytes_accessed=10**6, transcendentals=0),
        name="vectors",
    )(
        right_sides.reshape(OWN, LEAVES, LEAF).transpose(1, 0, 2).reshape(LEAVES * OWN, LEAF),
        order,
    )
    halo, columns, window_vectors, t_root, times, skel_here = pl.pallas_call(
        functools.partial(gather_kernel, count, levels),
        out_shape=(
            shape((2, QUARTER, DIM, LEAF), BF16),
            shape((REPS, QUARTER, DIM, LEAF), BF16),
            shape((SIDES, REPS, 2 * OWN, 2 * LEAF), BF16),
            shape((OWN, RANK), F32),
            shape((LEAVES, LANES), I32),
            shape((LEAVES, RANK), I32),
        ),
        in_specs=vmem(11),
        out_specs=tuple(vmem(6)),
        scratch_shapes=[
            pltpu.VMEM((REPS, 2 * OWN, 2 * LEAF), BF16),
            pltpu.VMEM((levels, DIM, RANK), BF16),
            pltpu.VMEM((levels, DIM, RANK), BF16),
            pltpu.VMEM((levels, 2, RANK, RANK), BF16),
            pltpu.VMEM((levels, OWN, RANK), F32),
        ]
        + [pltpu.VMEM((1 << width, OWN, RANK), F32) for _, width in spans]
        + [dma((2, 1 << width)) for _, width in spans]
        + [
            dma((2, 2, 2)),
            dma((2, 2, REPS - 1)),
            dma((2, SIDES, REPS)),
            dma((2, levels, 1 << (max(PHASES) - 1))),
            dma((2, levels)),
        ],
        compiler_params=params(0),
        name="gather",
    )(
        coords,
        sorted_vectors,
        order,
        leaf_basis,
        leaf_transfer,
        top_transfer[: levels - 1],
        skel_root,
        skel_leaf,
        admissible.T,
        near_leaves,
        near_count.reshape(1, LEAVES),
    )

    part, own_part = pl.pallas_call(
        near_kernel,
        out_shape=(shape((REPS, 2 * OWN, PTS // 2), BF16), shape((OWN, PTS), F32)),
        in_specs=[pl.BlockSpec(memory_space=pltpu.SMEM)] + vmem(7),
        out_specs=tuple(vmem(2)),
        scratch_shapes=[
            pltpu.SMEM((LEAVES * PARTNERS + 4 * WAYS + 8,), I32),
            pltpu.VMEM((PARTNERS, LEAF, LANES), BF16),
            pltpu.VMEM((LEAVES, LANES, LEAF), BF16),
            pltpu.VMEM((LEAVES, LANES, RANK), BF16),
            pltpu.VMEM((QUARTER, RANK, LANES), BF16),
            pltpu.VMEM((PARTNERS, RHS, LEAF), BF16),
            pltpu.VMEM((LEAVES, RHS, LEAF), F32),
            pltpu.VMEM((QUARTER, 2 * RHS, RANK), BF16),
            pltpu.VMEM((LEAVES, RHS, RANK), F32),
        ]
        + [pltpu.VMEM((WAYS, LEAF, LEAF), F32)] * 2
        + [pltpu.VMEM((WAYS, LEAF, LEAF), BF16)] * 2
        + [pltpu.VMEM((WAYS, RANK, RANK), F32)] * 2
        + [pltpu.VMEM((WAYS, 2, RANK, RANK), BF16)] * 2,
        compiler_params=params(),
        name="near",
    )(
        times,
        columns,
        skel_here,
        t_root,
        window_vectors,
        leaf_transfer,
        leaf_basis,
        halo,
    )

    negative = pl.pallas_call(
        combine_kernel,
        out_shape=shape((OWN, PTS), F32),
        in_specs=vmem(3),
        out_specs=pl.BlockSpec(memory_space=pltpu.VMEM),
        scratch_shapes=[
            pltpu.VMEM((REPS - 1, 2 * OWN, PTS // 2), BF16),
            dma((2, REPS - 1, CHUNKS)),
        ],
        compiler_params=params(1),
        name="combine",
    )(part, own_part, order)
    return -negative


def solution(mesh):
    placed = (
        P(None, "leaf"),
        P("rep", "leaf"),
        P("leaf"),
        P("leaf", None, None),
        P("leaf", None, None),
        P(),
        P("leaf", None),
        P("leaf", None),
        P("leaf", None),
        P("leaf", None),
        P("leaf"),
    )
    return jax.shard_map(
        functools.partial(on_device, mesh.shape["leaf"]),
        mesh=mesh,
        in_specs=placed,
        out_specs=P("rep", "leaf"),
        check_vma=False,
    )
```

```python
import functools

import jax
import jax.numpy as jnp
from jax import lax
from jax.experimental import pallas as pl
from jax.experimental.pallas import tpu as pltpu
from jax.sharding import PartitionSpec as P

MESH = pl.DeviceIdType.MESH
F32 = jnp.float32
BF16 = jnp.bfloat16
I32 = jnp.int32

DIM = 64
RANK = 128
LEAF = 256
LEAVES = 16
PTS = 4096
LANES = 128
BLOCKS = PTS // LANES
REPS = 4
QUARTER = LEAVES // REPS
OWN = 8
RHS = 32
SIDES = 3
PARTNERS = SIDES * QUARTER
PHASES = (3, 2, 2)
WAYS = 2
CHUNKS = 4
VMEM_LIMIT = 24 * 1024 * 1024


def dot_nn(a, b):
    return lax.dot_general(a, b, (((1,), (0,)), ((), ())), preferred_element_type=F32)


def dot_nt(a, b):
    return lax.dot_general(a, b, (((1,), (1,)), ((), ())), preferred_element_type=F32)


def kernel_values(shifted):
    shifted = jnp.maximum(shifted, 1.0)
    return jnp.exp((shifted * -0.5) * lax.rsqrt(shifted))


def split_two(x):
    high = x.astype(BF16)
    return high, (x - high.astype(F32)).astype(BF16)


def stack_two(x):
    high = x.astype(BF16).astype(F32)
    return jnp.concatenate([high, x - high], axis=0).astype(BF16)


def fold_two(x):
    half = x.shape[0] // 2
    return x[:half] + x[half:]


def dot_wide(x, matrix):
    return fold_two(dot_nn(stack_two(x), matrix))


def dot_wide_nt(x, matrix):
    return fold_two(dot_nt(stack_two(x), matrix))


def dot_both_wide(x, matrix):
    rows = stack_two(x)
    high, low = split_two(matrix)
    return fold_two(dot_nn(rows, high)) + fold_two(dot_nn(rows, low))


def with_norms(points, own):
    count = points.shape[1]
    norm = jnp.sum(points * points, axis=0, keepdims=True)
    if own:
        norm = norm + 1.0
    high = norm.astype(BF16).astype(F32)
    rest = norm - high
    mid = rest.astype(BF16).astype(F32)
    low = rest - mid
    row = lax.broadcasted_iota(I32, (16, count), 0)
    if not own:
        row = row - 3
    tail = jnp.where(row == 0, high, jnp.where(row == 1, mid, jnp.where(row == 2, low, 0.0)))
    ones = lax.broadcasted_iota(I32, (16, count), 0) - (3 if own else 0)
    tail = jnp.where((ones >= 0) & (ones < 3), 1.0, tail)
    head = points * -2.0 if own else points
    return jnp.concatenate([head, tail, jnp.zeros((LANES - DIM - 16, count), F32)], axis=0)


def one_hot(low):
    row = lax.broadcasted_iota(I32, (LEAF, low.shape[1]), 0)
    return jnp.where(row == low, 1.0, 0.0).astype(BF16)


def choose(slices, positions):
    marks = one_hot(positions & 255)
    rows = slices[0].shape[0]
    high = jnp.broadcast_to(positions >> 8, (rows, positions.shape[1]))
    out = jnp.zeros((rows, positions.shape[1]), F32)
    together = min(len(slices), 512 // rows)
    for first in range(0, len(slices), together):
        block = dot_nn(jnp.concatenate(slices[first : first + together], axis=0), marks)
        for number in range(together):
            out = jnp.where(high == first + number, block[number * rows : (number + 1) * rows], out)
    return out


def order_of(order_ref, leaf):
    return jnp.concatenate([order_ref[pl.ds(leaf * 2 + half, 1), :] for half in range(2)], axis=1)


def pick(table, lanes):
    return jnp.take_along_axis(table, lanes, axis=1, mode="promise_in_bounds")


def greet_signals(devices):
    barrier = pltpu.get_barrier_semaphore()
    for device in devices:
        pl.semaphore_signal(barrier, inc=1, device_id=device, device_id_type=MESH)


def greet_wait(devices):
    pl.semaphore_wait(pltpu.get_barrier_semaphore(), len(devices))


def remote(source, target, send_sem, recv_sem, device):
    return pltpu.make_async_remote_copy(
        src_ref=source,
        dst_ref=target,
        send_sem=send_sem,
        recv_sem=recv_sem,
        device_id=device,
        device_id_type=MESH,
    )


def phases_of(levels):
    spans, first = [], 0
    for width in PHASES:
        width = min(width, levels - first)
        if width > 0:
            spans.append((first, width))
        first += width
    return spans


def vectors_kernel(rows_ref, order_ref, sorted_ref):
    vector_rows = rows_ref[...]

    def sort_vectors(number, _):
        positions = order_of(order_ref, number)
        block = dot_nn(vector_rows, one_hot(positions & 255))
        high = jnp.broadcast_to(positions >> 8, (OWN, LEAF))
        out = jnp.zeros((OWN, LEAF), F32)
        for source in range(LEAVES):
            out = jnp.where(high == source, block[source * OWN : (source + 1) * OWN], out)
        sorted_ref[number] = out
        return 0

    lax.fori_loop(0, LEAVES, sort_vectors, 0, unroll=4)


def gather_kernel(
    count,
    levels,
    coords_ref,
    sorted_ref,
    order_ref,
    basis_ref,
    transfer_ref,
    top_ref,
    skel_root_ref,
    skel_leaf_ref,
    admissible_ref,
    near_ref,
    count_ref,
    halo_ref,
    columns_ref,
    window_vectors_ref,
    t_root_ref,
    times_ref,
    skel_out_ref,
    vectors_ref,
    points_ref,
    got_points_ref,
    kernel_ref,
    sibling_ref,
    *rest,
):
    spans = phases_of(levels)
    gathered_refs = rest[: len(spans)]
    spread_sems = rest[len(spans) : 2 * len(spans)]
    row_sems, column_sems, vector_sems, push_sems = rest[2 * len(spans) :]

    leaf = lax.axis_index("leaf")
    rep = lax.axis_index("rep")
    before = lax.rem(leaf + count - 1, count)
    after = lax.rem(leaf + 1, count)
    others = [lax.rem(rep + step, REPS) for step in range(1, REPS)]
    partners = [(jnp.where(lax.rem(leaf, 2) == 0, before, after), rep)]
    partners += [(leaf, other) for other in others]
    for first, width in spans:
        partners += [(leaf ^ (number << first), rep) for number in range(1, 1 << width)]
    greet_signals(partners)

    def coordinate_slices():
        return [coords_ref[:, high * LEAF : (high + 1) * LEAF] for high in range(LEAVES)]

    at = jnp.broadcast_to(skel_root_ref[...], (8, LANES))
    at_high = at >> 7
    at_low = at & 127
    initial = jnp.zeros((8, LANES), I32)
    for source in range(BLOCKS):
        table = jnp.broadcast_to(order_ref[source : source + 1, :], (8, LANES))
        initial = jnp.where(at_high == source, pick(table, at_low), initial)
    points_ref[0] = choose(coordinate_slices(), initial[:1]).astype(BF16)
    sent = []

    pushes = [[] for _ in spans]

    def push_start(phase):
        if phase >= len(spans):
            return
        first, width = spans[phase]
        for level in range(first, first + width):
            for number in range(1 << (level - first), 2 << (level - first)):
                copy = remote(
                    points_ref.at[first],
                    got_points_ref.at[level],
                    push_sems.at[0, level, number - (1 << (level - first))],
                    push_sems.at[1, level, 0],
                    (leaf ^ (number << first), rep),
                )
                pushes[phase].append((level, copy))
                if level == first:
                    copy.start()
                else:
                    pl.when(lax.rem(leaf // (1 << first), 1 << (level - first)) == 0)(copy.start)

    def push_finish(phase):
        if phase >= len(spans):
            return
        first, width = spans[phase]
        for level in range(first, first + width):
            [copy for at, copy in pushes[phase] if at == level][0].wait_recv()
            if level + 1 < levels:
                on_right = lax.rem(leaf // (1 << level), 2) == 1
                points_ref[level + 1] = jnp.where(
                    on_right, got_points_ref[level].astype(F32), points_ref[level].astype(F32)
                ).astype(BF16)
        push_start(phase + 1)

    def push_wait_send():
        for (first, width), copies in zip(spans, pushes):
            for level, copy in copies:
                if level == first:
                    copy.wait_send()
                else:
                    pl.when(lax.rem(leaf // (1 << first), 1 << (level - first)) == 0)(copy.wait_send)

    def kernels(first, last):
        first, last = min(first, levels), min(last, levels)
        values = []
        for level in range(first, last):
            own = with_norms(points_ref[level].astype(F32), True).astype(BF16)
            rows = with_norms(got_points_ref[level].astype(F32), False).T.astype(BF16)
            values.append(split_two(kernel_values(dot_nn(rows, own))))
        for level, (high, low) in zip(range(first, last), values):
            kernel_ref[level, 0] = high
            kernel_ref[level, 1] = low

    spreads = []

    def spread_start(phase):
        if phase >= len(spans):
            return
        first, width = spans[phase]
        copies = []
        for number in range(1, 1 << width):
            copy = remote(
                gathered_refs[phase].at[0],
                gathered_refs[phase].at[number],
                spread_sems[phase].at[0, number],
                spread_sems[phase].at[1, number],
                (leaf ^ (number << first), rep),
            )
            copy.start()
            copies.append(copy)
            sent.append(copy)
        spreads.append(copies)

    def spread_finish(phase):
        if phase >= len(spans):
            return
        first, width = spans[phase]
        for copy in spreads[phase]:
            copy.wait_recv()
        nodes = [gathered_refs[phase][number] for number in range(1 << width)]
        for level in range(first, first + width):
            sibling_ref[level] = nodes[1]
            if level + 1 == levels:
                return
            on_right = lax.rem(leaf // (1 << level), 2) == 1
            even = jnp.concatenate(nodes[0::2], axis=0)
            odd = jnp.concatenate(nodes[1::2], axis=0)
            parents = dot_wide(jnp.where(on_right, odd, even), top_ref[level, 0]) + dot_wide(
                jnp.where(on_right, even, odd), top_ref[level, 1]
            )
            nodes = [parents[i * OWN : i * OWN + OWN] for i in range(len(nodes) // 2)]
        gathered_refs[phase + 1][0] = nodes[0]
        spread_start(phase + 1)

    def coupling(level):
        rows = stack_two(sibling_ref[level])
        return fold_two(dot_nn(rows, kernel_ref[level, 0])) + fold_two(dot_nn(rows, kernel_ref[level, 1]))

    def up(number, total):
        s_leaf = dot_nn(sorted_ref[number].astype(BF16), basis_ref[number])
        return total + dot_nn(stack_two(s_leaf), transfer_ref[number])

    s_root = fold_two(lax.fori_loop(0, LEAVES, up, jnp.zeros((2 * OWN, RANK), F32), unroll=LEAVES))
    gathered_refs[0][0] = s_root
    greet_wait(partners)
    spread_start(0)
    push_start(0)

    for target in range(REPS):
        for column in range(2):
            top = sorted_ref[column * REPS + target]
            bottom = sorted_ref[(column + 2) * REPS + target]
            vectors_ref[target, :, column * LEAF : (column + 1) * LEAF] = jnp.concatenate(
                [top, bottom], axis=0
            ).astype(BF16)
    window_vectors_ref[1, rep] = vectors_ref[rep]
    for step, other in enumerate(others):
        copy = remote(
            vectors_ref.at[other],
            window_vectors_ref.at[1, rep],
            vector_sems.at[0, step],
            vector_sems.at[1, step],
            (leaf, other),
        )
        copy.start()
        sent.append(copy)

    side_copies = []

    def pass_vectors():
        for step, other in enumerate(others):
            source = lax.rem(rep + REPS - 1 - step, REPS)
            remote(
                vectors_ref.at[rep],
                window_vectors_ref.at[1, source],
                vector_sems.at[0, step],
                vector_sems.at[1, step],
                (leaf, other),
            ).wait_recv()
        for index, (side, device) in enumerate(((2, before), (0, after))):
            copy = remote(
                window_vectors_ref.at[1],
                window_vectors_ref.at[side],
                vector_sems.at[0, REPS - 1 + index],
                vector_sems.at[1, REPS - 1 + index],
                (device, rep),
            )
            copy.start()
            side_copies.append(copy)
            sent.append(copy)


    def sort_points(k):
        number = k * REPS + rep
        points = choose(coordinate_slices(), order_of(order_ref, number))
        columns_ref[rep, k] = points.astype(BF16)

    def send_points():
        for index, (side, device) in enumerate(((1, before), (0, after))):
            copy = remote(
                columns_ref.at[rep],
                halo_ref.at[side],
                row_sems.at[0, index],
                row_sems.at[1, index],
                (device, rep),
            )
            copy.start()
            side_copies.append(copy)
            sent.append(copy)
        for step, other in enumerate(others):
            copy = remote(
                columns_ref.at[rep],
                columns_ref.at[rep],
                column_sems.at[0, step],
                column_sems.at[1, step],
                (leaf, other),
            )
            copy.start()
            sent.append(copy)

    for k in range(QUARTER):
        sort_points(k)
    send_points()
    push_finish(0)
    spread_finish(0)
    pass_vectors()
    push_finish(1)
    spread_finish(1)
    kernels(0, 5)
    push_finish(2)
    kernels(5, 7)

    diagonal = lax.broadcasted_iota(I32, (LEAVES, LEAVES), 0) == lax.broadcasted_iota(
        I32, (LEAVES, LEAVES), 1
    )

    def as_column(row):
        return jnp.sum(jnp.where(diagonal, row, 0.0), axis=1, keepdims=True)

    near = near_ref[...]
    slot = lax.broadcasted_iota(I32, near.shape, 1)
    live = slot.astype(F32) < as_column(count_ref[...].astype(F32))
    admissible = admissible_ref[...]
    lane = lax.broadcasted_iota(I32, (LEAVES, LANES), 1)
    times = jnp.zeros((LEAVES, LANES), F32)
    for entry in range(PARTNERS + QUARTER):
        if entry < PARTNERS:
            named = jnp.where(near == entry * REPS + rep, 1.0, 0.0)
            total = jnp.sum(jnp.where(live, named, 0.0), axis=1, keepdims=True)
        else:
            named = jnp.where(admissible == (entry - PARTNERS) * REPS + rep, 1.0, 0.0)
            total = as_column(jnp.sum(named, axis=0, keepdims=True))
        times = jnp.where(lane == entry, total, times)
    times_ref[...] = times.astype(I32)
    skel_out_ref[...] = skel_leaf_ref[...]

    spread_finish(2)

    running = coupling(levels - 1)
    for level in range(levels - 2, -1, -1):
        side = lax.rem(leaf // (1 << level), 2)
        running = coupling(level) + dot_wide_nt(running, top_ref[level, side])
    t_root_ref[...] = running

    for copy in side_copies:
        copy.wait_recv()
    for step, other in enumerate(others):
        source = lax.rem(rep + REPS - 1 - step, REPS)
        remote(
            columns_ref.at[rep],
            columns_ref.at[source],
            column_sems.at[0, step],
            column_sems.at[1, step],
            (leaf, other),
        ).wait_recv()
    for copy in sent:
        copy.wait_send()
    push_wait_send()


def near_kernel(
    times_ref,
    columns_ref,
    skel_leaf_ref,
    t_root_ref,
    window_vectors_ref,
    transfer_ref,
    basis_ref,
    halo_ref,
    out_ref,
    own_out_ref,
    list_ref,
    window_ref,
    own_ref,
    own_skel_ref,
    skel_rows_ref,
    vectors_ref,
    total_ref,
    s_ref,
    t_ref,
    near_shifted_even,
    near_shifted_odd,
    near_even,
    near_odd,
    far_shifted_even,
    far_shifted_odd,
    far_even,
    far_odd,
):
    near_shifted, near_tiles = (near_shifted_even, near_shifted_odd), (near_even, near_odd)
    far_shifted, far_tiles = (far_shifted_even, far_shifted_odd), (far_even, far_odd)
    rep = lax.axis_index("rep")
    root_rows = stack_two(t_root_ref[...])
    t_ref[...] = jnp.zeros_like(t_ref)

    def prepare(leaf, _):
        source = lax.rem(leaf, REPS)
        k = leaf // REPS
        points = columns_ref[source, k].astype(F32)
        columns = with_norms(points, True)
        own_ref[leaf] = columns.astype(BF16)
        marks = one_hot(skel_leaf_ref[pl.ds(leaf, 1), :])
        own_skel_ref[leaf] = with_norms(dot_nn(columns_ref[source, k], marks), True).astype(BF16)
        return 0

    lax.fori_loop(0, LEAVES, prepare, 0, unroll=4)

    def partner_rows(k, _):
        for side, points in enumerate((halo_ref[0, k], columns_ref[rep, k], halo_ref[1, k])):
            window_ref[side * QUARTER + k] = with_norms(points.astype(F32), False).T.astype(BF16)
        return 0

    lax.fori_loop(0, QUARTER, partner_rows, 0, unroll=2)

    def from_root(leaf, _):
        t_ref[leaf, pl.ds(pl.multiple_of(rep * OWN, OWN), OWN), :] = fold_two(
            dot_nt(root_rows, transfer_ref[leaf])
        )
        return 0

    lax.fori_loop(0, LEAVES, from_root, 0, unroll=8)

    for side in range(SIDES):
        for column in range(2):
            span = slice(column * LEAF, (column + 1) * LEAF)
            blocks = [window_vectors_ref[side, source, :, span].astype(F32) for source in range(REPS)]
            vectors_ref[side * QUARTER + column] = jnp.concatenate(
                [block[:OWN] for block in blocks], axis=0
            ).astype(BF16)
            vectors_ref[side * QUARTER + column + 2] = jnp.concatenate(
                [block[OWN:] for block in blocks], axis=0
            ).astype(BF16)
    for k in range(QUARTER):
        leaf = k * REPS + rep
        s_leaf = dot_nn(vectors_ref[QUARTER + k], basis_ref[leaf])
        s_ref[k] = stack_two(s_leaf)
        skel = own_skel_ref[leaf].astype(F32)
        skel_rows_ref[k] = with_norms(skel[:DIM] * -0.5, False).T.astype(BF16)

    total_ref[...] = jnp.zeros_like(total_ref)

    def make_list(first, width):
        def one_leaf(leaf, filled):
            for entry in range(first, first + width):
                list_ref[filled] = leaf * 16 + entry
                filled = filled + jnp.where(times_ref[leaf, entry] > 0, 1, 0)
            return filled

        filled = lax.fori_loop(0, LEAVES, one_leaf, 0, unroll=2)
        for pad in range(4 * WAYS):
            list_ref[filled + pad] = first
        return filled

    def run(filled, product, keep, apply, shifted_refs, tile_refs):
        def start(group, shifted_ref):
            for way in range(WAYS):
                code = list_ref[group * WAYS + way]
                shifted_ref[way] = product(code >> 4, code & 15)

        def middle(shifted_ref, tile_ref):
            for way in range(WAYS):
                keep(tile_ref, way, kernel_values(shifted_ref[way]))

        def finish(group, tile_ref):
            for way in range(WAYS):
                number = group * WAYS + way
                code = list_ref[jnp.maximum(number, 0)]
                leaf, entry = code >> 4, code & 15
                times = jnp.where((number >= 0) & (number < filled), times_ref[leaf, entry], 0)
                apply(leaf, entry, times.astype(F32), tile_ref, way)

        start(0, shifted_refs[0])
        tile_refs[1][...] = jnp.zeros_like(tile_refs[1])

        def step(number, _):
            even = number * 2
            start(even + 1, shifted_refs[1])
            middle(shifted_refs[0], tile_refs[0])
            finish(even - 1, tile_refs[1])
            start(even + 2, shifted_refs[0])
            middle(shifted_refs[1], tile_refs[1])
            finish(even, tile_refs[0])
            return 0

        steps = (filled + 2 * WAYS - 1) // (2 * WAYS)
        lax.fori_loop(0, steps, step, 0)
        finish(2 * steps - 1, tile_refs[1])

    def near_keep(tile_ref, way, values):
        tile_ref[way] = values.astype(BF16)

    def near_apply(leaf, entry, times, tile_ref, way):
        total_ref[leaf] += dot_nn(vectors_ref[entry], tile_ref[way]) * times

    run(
        make_list(0, PARTNERS),
        lambda leaf, entry: dot_nn(window_ref[entry], own_ref[leaf]),
        near_keep,
        near_apply,
        near_shifted,
        near_tiles,
    )

    def far_keep(tile_ref, way, values):
        high, low = split_two(values)
        tile_ref[way, 0] = high
        tile_ref[way, 1] = low

    def far_apply(leaf, entry, times, tile_ref, way):
        rows = s_ref[entry - PARTNERS]
        term = fold_two(dot_nn(rows, tile_ref[way, 0])) + dot_nn(rows[:RHS], tile_ref[way, 1])
        t_ref[leaf] += term * times

    run(
        make_list(PARTNERS, QUARTER),
        lambda leaf, entry: dot_nn(skel_rows_ref[entry - PARTNERS], own_skel_ref[leaf]),
        far_keep,
        far_apply,
        far_shifted,
        far_tiles,
    )

    for leaf in range(LEAVES):
        total_ref[leaf] += dot_wide_nt(t_ref[leaf], basis_ref[leaf])
    mine = pl.ds(pl.multiple_of(rep * OWN, OWN), OWN)
    for leaf in range(LEAVES):
        own_out_ref[:, leaf * LEAF : (leaf + 1) * LEAF] = total_ref[leaf, mine, :]
    for leaf in range(LEAVES // 2):
        top = total_ref[leaf].reshape(REPS, OWN, LEAF)
        bottom = total_ref[leaf + LEAVES // 2].reshape(REPS, OWN, LEAF)
        out_ref[:, :, leaf * LEAF : (leaf + 1) * LEAF] = jnp.concatenate([top, bottom], axis=1).astype(BF16)


def combine_kernel(part_ref, own_ref, order_ref, out_ref, got_ref, marks_ref, sems):
    leaf = lax.axis_index("leaf")
    rep = lax.axis_index("rep")
    half = PTS // 2
    width = half // CHUNKS
    partners = [(leaf, lax.rem(rep + step, REPS)) for step in range(1, REPS)]
    greet_signals(partners)
    greet_wait(partners)
    copies = []
    for index, partner in enumerate(partners):
        copy = remote(
            part_ref.at[partner[1]], got_ref.at[index], sems.at[0, index], sems.at[1, index], partner
        )
        copy.start()
        copies.append(copy)

    scattered = jnp.zeros((LEAVES * 2 * OWN, LEAF), F32)
    highs = []
    for chunk in range(CHUNKS):
        here = [(number, (number * half + chunk * width) // LANES) for number in range(2)]
        positions = jnp.concatenate(
            [
                order_ref[first + at : first + at + 1, :]
                for _, first in here
                for at in range(width // LANES)
            ],
            axis=1,
        )
        marks_ref[chunk] = one_hot(positions & 255)
        highs.append(positions >> 8)
    for copy in copies:
        copy.wait()
    for chunk in range(CHUNKS):
        here = [(number, (number * half + chunk * width) // LANES) for number in range(2)]
        high = jnp.broadcast_to(highs[chunk], (2 * OWN, 2 * width))
        totals = []
        for number, first in here:
            rows = slice(number * OWN, (number + 1) * OWN)
            total = -own_ref[:, first * LANES : first * LANES + width]
            for index in range(REPS - 1):
                total = total - got_ref[index, :, chunk * width : (chunk + 1) * width].astype(F32)[rows]
            totals.append(total)
        total = jnp.concatenate(totals, axis=1)
        rounded = total.astype(BF16).astype(F32)
        terms = jnp.concatenate([rounded, total - rounded], axis=0)
        rows = jnp.concatenate(
            [jnp.where(high == source, terms, 0.0).astype(BF16) for source in range(LEAVES)], axis=0
        )
        scattered = scattered + dot_nt(rows, marks_ref[chunk])
    for source in range(LEAVES):
        first = source * 2 * OWN
        out_ref[:, source * LEAF : (source + 1) * LEAF] = (
            scattered[first : first + OWN] + scattered[first + OWN : first + 2 * OWN]
        )


def vmem(count):
    return [pl.BlockSpec(memory_space=pltpu.VMEM)] * count


def shape(dims, dtype):
    return jax.ShapeDtypeStruct(dims, dtype)


def params(collective_id=None):
    if collective_id is None:
        return pltpu.CompilerParams(vmem_limit_bytes=VMEM_LIMIT)
    return pltpu.CompilerParams(
        collective_id=collective_id, has_side_effects=True, vmem_limit_bytes=VMEM_LIMIT
    )


def on_device(
    count,
    coords,
    right_sides,
    leaf_order,
    leaf_basis,
    leaf_transfer,
    top_transfer,
    skel_leaf,
    skel_root,
    admissible,
    near_leaves,
    near_count,
):
    levels = count.bit_length() - 1
    spans = phases_of(levels)
    order = leaf_order.reshape(BLOCKS, LANES)
    dma = pltpu.SemaphoreType.DMA
    sorted_vectors = pl.pallas_call(
        vectors_kernel,
        out_shape=shape((LEAVES, OWN, LEAF), F32),
        in_specs=vmem(2),
        out_specs=pl.BlockSpec(memory_space=pltpu.VMEM),
        compiler_params=params(),
        cost_estimate=pl.CostEstimate(flops=10**9, bytes_accessed=10**6, transcendentals=0),
        name="vectors",
    )(
        right_sides.reshape(OWN, LEAVES, LEAF).transpose(1, 0, 2).reshape(LEAVES * OWN, LEAF),
        order,
    )
    halo, columns, window_vectors, t_root, times, skel_here = pl.pallas_call(
        functools.partial(gather_kernel, count, levels),
        out_shape=(
            shape((2, QUARTER, DIM, LEAF), BF16),
            shape((REPS, QUARTER, DIM, LEAF), BF16),
            shape((SIDES, REPS, 2 * OWN, 2 * LEAF), BF16),
            shape((OWN, RANK), F32),
            shape((LEAVES, LANES), I32),
            shape((LEAVES, RANK), I32),
        ),
        in_specs=vmem(11),
        out_specs=tuple(vmem(6)),
        scratch_shapes=[
            pltpu.VMEM((REPS, 2 * OWN, 2 * LEAF), BF16),
            pltpu.VMEM((levels, DIM, RANK), BF16),
            pltpu.VMEM((levels, DIM, RANK), BF16),
            pltpu.VMEM((levels, 2, RANK, RANK), BF16),
            pltpu.VMEM((levels, OWN, RANK), F32),
        ]
        + [pltpu.VMEM((1 << width, OWN, RANK), F32) for _, width in spans]
        + [dma((2, 1 << width)) for _, width in spans]
        + [
            dma((2, 2)),
            dma((2, REPS - 1)),
            dma((2, REPS + 1)),
            dma((2, levels, 1 << (max(PHASES) - 1))),
        ],
        compiler_params=params(0),
        name="gather",
    )(
        coords,
        sorted_vectors,
        order,
        leaf_basis,
        leaf_transfer,
        top_transfer[: levels - 1],
        skel_root,
        skel_leaf,
        admissible.T,
        near_leaves,
        near_count.reshape(1, LEAVES),
    )

    part, own_part = pl.pallas_call(
        near_kernel,
        out_shape=(shape((REPS, 2 * OWN, PTS // 2), BF16), shape((OWN, PTS), F32)),
        in_specs=[pl.BlockSpec(memory_space=pltpu.SMEM)] + vmem(7),
        out_specs=tuple(vmem(2)),
        scratch_shapes=[
            pltpu.SMEM((LEAVES * PARTNERS + 4 * WAYS + 8,), I32),
            pltpu.VMEM((PARTNERS, LEAF, LANES), BF16),
            pltpu.VMEM((LEAVES, LANES, LEAF), BF16),
            pltpu.VMEM((LEAVES, LANES, RANK), BF16),
            pltpu.VMEM((QUARTER, RANK, LANES), BF16),
            pltpu.VMEM((PARTNERS, RHS, LEAF), BF16),
            pltpu.VMEM((LEAVES, RHS, LEAF), F32),
            pltpu.VMEM((QUARTER, 2 * RHS, RANK), BF16),
            pltpu.VMEM((LEAVES, RHS, RANK), F32),
        ]
        + [pltpu.VMEM((WAYS, LEAF, LEAF), F32)] * 2
        + [pltpu.VMEM((WAYS, LEAF, LEAF), BF16)] * 2
        + [pltpu.VMEM((WAYS, RANK, RANK), F32)] * 2
        + [pltpu.VMEM((WAYS, 2, RANK, RANK), BF16)] * 2,
        compiler_params=params(),
        name="near",
    )(
        times,
        columns,
        skel_here,
        t_root,
        window_vectors,
        leaf_transfer,
        leaf_basis,
        halo,
    )

    negative = pl.pallas_call(
        combine_kernel,
        out_shape=shape((OWN, PTS), F32),
        in_specs=vmem(3),
        out_specs=pl.BlockSpec(memory_space=pltpu.VMEM),
        scratch_shapes=[
            pltpu.VMEM((REPS - 1, 2 * OWN, PTS // 2), BF16),
            pltpu.VMEM((CHUNKS, LEAF, PTS // CHUNKS), BF16),
            dma((2, REPS - 1)),
        ],
        compiler_params=params(1),
        name="combine",
    )(part, own_part, order)
    return -negative


def solution(mesh):
    placed = (
        P(None, "leaf"),
        P("rep", "leaf"),
        P("leaf"),
        P("leaf", None, None),
        P("leaf", None, None),
        P(),
        P("leaf", None),
        P("leaf", None),
        P("leaf", None),
        P("leaf", None),
        P("leaf"),
    )
    return jax.shard_map(
        functools.partial(on_device, mesh.shape["leaf"]),
        mesh=mesh,
        in_specs=placed,
        out_specs=P("rep", "leaf"),
        check_vma=False,
    )
```

```python
import functools

import jax
import jax.numpy as jnp
from jax import lax
from jax.experimental import pallas as pl
from jax.experimental.pallas import tpu as pltpu
from jax.sharding import PartitionSpec as P

MESH = pl.DeviceIdType.MESH
F32 = jnp.float32
BF16 = jnp.bfloat16
I32 = jnp.int32

DIM = 64
RANK = 128
LEAF = 256
LEAVES = 16
PTS = 4096
LANES = 128
BLOCKS = PTS // LANES
REPS = 4
QUARTER = LEAVES // REPS
OWN = 8
RHS = 32
SIDES = 3
PARTNERS = SIDES * QUARTER
PHASES = (3, 2, 2)
WAYS = 2
CHUNKS = 4
VMEM_LIMIT = 24 * 1024 * 1024


def dot_nn(a, b):
    return lax.dot_general(a, b, (((1,), (0,)), ((), ())), preferred_element_type=F32)


def dot_nt(a, b):
    return lax.dot_general(a, b, (((1,), (1,)), ((), ())), preferred_element_type=F32)


def kernel_values(shifted):
    shifted = jnp.maximum(shifted, 1.0)
    return jnp.exp((shifted * -0.5) * lax.rsqrt(shifted))


def split_two(x):
    high = x.astype(BF16)
    return high, (x - high.astype(F32)).astype(BF16)


def stack_two(x):
    high = x.astype(BF16).astype(F32)
    return jnp.concatenate([high, x - high], axis=0).astype(BF16)


def fold_two(x):
    half = x.shape[0] // 2
    return x[:half] + x[half:]


def dot_wide(x, matrix):
    return fold_two(dot_nn(stack_two(x), matrix))


def dot_wide_nt(x, matrix):
    return fold_two(dot_nt(stack_two(x), matrix))


def dot_both_wide(x, matrix):
    rows = stack_two(x)
    high, low = split_two(matrix)
    return fold_two(dot_nn(rows, high)) + fold_two(dot_nn(rows, low))


def with_norms(points, own):
    count = points.shape[1]
    norm = jnp.sum(points * points, axis=0, keepdims=True)
    if own:
        norm = norm + 1.0
    high = norm.astype(BF16).astype(F32)
    rest = norm - high
    mid = rest.astype(BF16).astype(F32)
    low = rest - mid
    row = lax.broadcasted_iota(I32, (16, count), 0)
    if not own:
        row = row - 3
    tail = jnp.where(row == 0, high, jnp.where(row == 1, mid, jnp.where(row == 2, low, 0.0)))
    ones = lax.broadcasted_iota(I32, (16, count), 0) - (3 if own else 0)
    tail = jnp.where((ones >= 0) & (ones < 3), 1.0, tail)
    head = points * -2.0 if own else points
    return jnp.concatenate([head, tail, jnp.zeros((LANES - DIM - 16, count), F32)], axis=0)


def one_hot(low):
    row = lax.broadcasted_iota(I32, (LEAF, low.shape[1]), 0)
    return jnp.where(row == low, 1.0, 0.0).astype(BF16)


def choose(slices, positions):
    marks = one_hot(positions & 255)
    rows = slices[0].shape[0]
    high = jnp.broadcast_to(positions >> 8, (rows, positions.shape[1]))
    out = jnp.zeros((rows, positions.shape[1]), F32)
    together = min(len(slices), 512 // rows)
    for first in range(0, len(slices), together):
        block = dot_nn(jnp.concatenate(slices[first : first + together], axis=0), marks)
        for number in range(together):
            out = jnp.where(high == first + number, block[number * rows : (number + 1) * rows], out)
    return out


def order_of(order_ref, leaf):
    return jnp.concatenate([order_ref[pl.ds(leaf * 2 + half, 1), :] for half in range(2)], axis=1)


def pick(table, lanes):
    return jnp.take_along_axis(table, lanes, axis=1, mode="promise_in_bounds")


def greet_signals(devices):
    barrier = pltpu.get_barrier_semaphore()
    for device in devices:
        pl.semaphore_signal(barrier, inc=1, device_id=device, device_id_type=MESH)


def greet_wait(devices):
    pl.semaphore_wait(pltpu.get_barrier_semaphore(), len(devices))


def remote(source, target, send_sem, recv_sem, device):
    return pltpu.make_async_remote_copy(
        src_ref=source,
        dst_ref=target,
        send_sem=send_sem,
        recv_sem=recv_sem,
        device_id=device,
        device_id_type=MESH,
    )


def phases_of(levels):
    spans, first = [], 0
    for width in PHASES:
        width = min(width, levels - first)
        if width > 0:
            spans.append((first, width))
        first += width
    return spans


def vectors_kernel(rows_ref, order_ref, sorted_ref):
    vector_rows = rows_ref[...]

    def sort_vectors(number, _):
        positions = order_of(order_ref, number)
        block = dot_nn(vector_rows, one_hot(positions & 255))
        high = jnp.broadcast_to(positions >> 8, (OWN, LEAF))
        out = jnp.zeros((OWN, LEAF), F32)
        for source in range(LEAVES):
            out = jnp.where(high == source, block[source * OWN : (source + 1) * OWN], out)
        sorted_ref[number] = out
        return 0

    lax.fori_loop(0, LEAVES, sort_vectors, 0, unroll=4)


def gather_kernel(
    count,
    levels,
    coords_ref,
    sorted_ref,
    order_ref,
    basis_ref,
    transfer_ref,
    top_ref,
    skel_root_ref,
    skel_leaf_ref,
    admissible_ref,
    near_ref,
    count_ref,
    halo_ref,
    columns_ref,
    window_vectors_ref,
    t_root_ref,
    times_ref,
    skel_out_ref,
    vectors_ref,
    points_ref,
    got_points_ref,
    kernel_ref,
    sibling_ref,
    *rest,
):
    spans = phases_of(levels)
    gathered_refs = rest[: len(spans)]
    spread_sems = rest[len(spans) : 2 * len(spans)]
    row_sems, column_sems, vector_sems, push_sems = rest[2 * len(spans) :]

    leaf = lax.axis_index("leaf")
    rep = lax.axis_index("rep")
    before = lax.rem(leaf + count - 1, count)
    after = lax.rem(leaf + 1, count)
    others = [lax.rem(rep + step, REPS) for step in range(1, REPS)]
    partners = [(jnp.where(lax.rem(leaf, 2) == 0, before, after), rep)]
    partners += [(leaf, other) for other in others]
    for first, width in spans:
        partners += [(leaf ^ (number << first), rep) for number in range(1, 1 << width)]
    greet_signals(partners)

    def coordinate_slices():
        return [coords_ref[:, high * LEAF : (high + 1) * LEAF] for high in range(LEAVES)]

    at = jnp.broadcast_to(skel_root_ref[...], (8, LANES))
    at_high = at >> 7
    at_low = at & 127
    initial = jnp.zeros((8, LANES), I32)
    for source in range(BLOCKS):
        table = jnp.broadcast_to(order_ref[source : source + 1, :], (8, LANES))
        initial = jnp.where(at_high == source, pick(table, at_low), initial)
    points_ref[0] = choose(coordinate_slices(), initial[:1]).astype(BF16)
    sent = []

    pushes = [[] for _ in spans]

    def push_start(phase):
        if phase >= len(spans):
            return
        first, width = spans[phase]
        for level in range(first, first + width):
            for number in range(1 << (level - first), 2 << (level - first)):
                copy = remote(
                    points_ref.at[first],
                    got_points_ref.at[level],
                    push_sems.at[0, level, number - (1 << (level - first))],
                    push_sems.at[1, level, 0],
                    (leaf ^ (number << first), rep),
                )
                pushes[phase].append((level, copy))
                if level == first:
                    copy.start()
                else:
                    pl.when(lax.rem(leaf // (1 << first), 1 << (level - first)) == 0)(copy.start)

    def push_finish(phase):
        if phase >= len(spans):
            return
        first, width = spans[phase]
        for level in range(first, first + width):
            [copy for at, copy in pushes[phase] if at == level][0].wait_recv()
            if level + 1 < levels:
                on_right = lax.rem(leaf // (1 << level), 2) == 1
                points_ref[level + 1] = jnp.where(
                    on_right, got_points_ref[level].astype(F32), points_ref[level].astype(F32)
                ).astype(BF16)
        push_start(phase + 1)

    def push_wait_send():
        for (first, width), copies in zip(spans, pushes):
            for level, copy in copies:
                if level == first:
                    copy.wait_send()
                else:
                    pl.when(lax.rem(leaf // (1 << first), 1 << (level - first)) == 0)(copy.wait_send)

    def kernels(first, last):
        first, last = min(first, levels), min(last, levels)
        values = []
        for level in range(first, last):
            own = with_norms(points_ref[level].astype(F32), True).astype(BF16)
            rows = with_norms(got_points_ref[level].astype(F32), False).T.astype(BF16)
            values.append(split_two(kernel_values(dot_nn(rows, own))))
        for level, (high, low) in zip(range(first, last), values):
            kernel_ref[level, 0] = high
            kernel_ref[level, 1] = low

    spreads = []

    def spread_start(phase):
        if phase >= len(spans):
            return
        first, width = spans[phase]
        copies = []
        for number in range(1, 1 << width):
            copy = remote(
                gathered_refs[phase].at[0],
                gathered_refs[phase].at[number],
                spread_sems[phase].at[0, number],
                spread_sems[phase].at[1, number],
                (leaf ^ (number << first), rep),
            )
            copy.start()
            copies.append(copy)
            sent.append(copy)
        spreads.append(copies)

    def spread_finish(phase):
        if phase >= len(spans):
            return
        first, width = spans[phase]
        for copy in spreads[phase]:
            copy.wait_recv()
        nodes = [gathered_refs[phase][number] for number in range(1 << width)]
        for level in range(first, first + width):
            sibling_ref[level] = nodes[1]
            if level + 1 == levels:
                return
            on_right = lax.rem(leaf // (1 << level), 2) == 1
            even = jnp.concatenate(nodes[0::2], axis=0)
            odd = jnp.concatenate(nodes[1::2], axis=0)
            parents = dot_wide(jnp.where(on_right, odd, even), top_ref[level, 0]) + dot_wide(
                jnp.where(on_right, even, odd), top_ref[level, 1]
            )
            nodes = [parents[i * OWN : i * OWN + OWN] for i in range(len(nodes) // 2)]
        gathered_refs[phase + 1][0] = nodes[0]
        spread_start(phase + 1)

    def coupling(level):
        rows = stack_two(sibling_ref[level])
        return fold_two(dot_nn(rows, kernel_ref[level, 0])) + fold_two(dot_nn(rows, kernel_ref[level, 1]))

    def up(number, total):
        s_leaf = dot_nn(sorted_ref[number].astype(BF16), basis_ref[number])
        return total + dot_nn(stack_two(s_leaf), transfer_ref[number])

    s_root = fold_two(lax.fori_loop(0, LEAVES, up, jnp.zeros((2 * OWN, RANK), F32), unroll=LEAVES))
    gathered_refs[0][0] = s_root
    greet_wait(partners)
    spread_start(0)
    push_start(0)

    for target in range(REPS):
        for column in range(2):
            top = sorted_ref[column * REPS + target]
            bottom = sorted_ref[(column + 2) * REPS + target]
            vectors_ref[target, :, column * LEAF : (column + 1) * LEAF] = jnp.concatenate(
                [top, bottom], axis=0
            ).astype(BF16)
    window_vectors_ref[1, rep] = vectors_ref[rep]
    for step, other in enumerate(others):
        copy = remote(
            vectors_ref.at[other],
            window_vectors_ref.at[1, rep],
            vector_sems.at[0, step],
            vector_sems.at[1, step],
            (leaf, other),
        )
        copy.start()
        sent.append(copy)

    side_copies = []

    def pass_vectors():
        for step, other in enumerate(others):
            source = lax.rem(rep + REPS - 1 - step, REPS)
            remote(
                vectors_ref.at[rep],
                window_vectors_ref.at[1, source],
                vector_sems.at[0, step],
                vector_sems.at[1, step],
                (leaf, other),
            ).wait_recv()
        for index, (side, device) in enumerate(((2, before), (0, after))):
            copy = remote(
                window_vectors_ref.at[1],
                window_vectors_ref.at[side],
                vector_sems.at[0, REPS - 1 + index],
                vector_sems.at[1, REPS - 1 + index],
                (device, rep),
            )
            copy.start()
            side_copies.append(copy)
            sent.append(copy)


    def sort_points(k):
        number = k * REPS + rep
        points = choose(coordinate_slices(), order_of(order_ref, number))
        columns_ref[rep, k] = points.astype(BF16)

    def send_sides():
        for index, (side, device) in enumerate(((1, before), (0, after))):
            copy = remote(
                columns_ref.at[rep],
                halo_ref.at[side],
                row_sems.at[0, index],
                row_sems.at[1, index],
                (device, rep),
            )
            copy.start()
            side_copies.append(copy)
            sent.append(copy)

    def send_columns():
        for step, other in enumerate(others):
            copy = remote(
                columns_ref.at[rep],
                columns_ref.at[rep],
                column_sems.at[0, step],
                column_sems.at[1, step],
                (leaf, other),
            )
            copy.start()
            sent.append(copy)

    for k in range(QUARTER):
        sort_points(k)
    send_columns()
    push_finish(0)
    spread_finish(0)
    push_finish(1)
    spread_finish(1)
    send_sides()
    pass_vectors()
    kernels(0, 5)
    push_finish(2)
    kernels(5, 7)

    diagonal = lax.broadcasted_iota(I32, (LEAVES, LEAVES), 0) == lax.broadcasted_iota(
        I32, (LEAVES, LEAVES), 1
    )

    def as_column(row):
        return jnp.sum(jnp.where(diagonal, row, 0.0), axis=1, keepdims=True)

    near = near_ref[...]
    slot = lax.broadcasted_iota(I32, near.shape, 1)
    live = slot.astype(F32) < as_column(count_ref[...].astype(F32))
    admissible = admissible_ref[...]
    lane = lax.broadcasted_iota(I32, (LEAVES, LANES), 1)
    times = jnp.zeros((LEAVES, LANES), F32)
    for entry in range(PARTNERS + QUARTER):
        if entry < PARTNERS:
            named = jnp.where(near == entry * REPS + rep, 1.0, 0.0)
            total = jnp.sum(jnp.where(live, named, 0.0), axis=1, keepdims=True)
        else:
            named = jnp.where(admissible == (entry - PARTNERS) * REPS + rep, 1.0, 0.0)
            total = as_column(jnp.sum(named, axis=0, keepdims=True))
        times = jnp.where(lane == entry, total, times)
    times_ref[...] = times.astype(I32)
    skel_out_ref[...] = skel_leaf_ref[...]

    split = spans[-1][0]
    sides = [lax.rem(leaf // (1 << level), 2) for level in range(levels)]
    lower = coupling(split - 1)
    for level in range(split - 2, -1, -1):
        lower = coupling(level) + dot_wide_nt(lower, top_ref[level, sides[level]])
    product = top_ref[0, sides[0]].astype(F32)
    for level in range(1, split):
        product = dot_wide(product, top_ref[level, sides[level]])
    product_high, product_low = split_two(product)

    spread_finish(2)
    running = coupling(levels - 1)
    for level in range(levels - 2, split - 1, -1):
        running = coupling(level) + dot_wide_nt(running, top_ref[level, sides[level]])
    rows = stack_two(running)
    running = lower + (fold_two(dot_nt(rows, product_high)) + fold_two(dot_nt(rows, product_low)))
    t_root_ref[...] = running

    for copy in side_copies:
        copy.wait_recv()
    for step, other in enumerate(others):
        source = lax.rem(rep + REPS - 1 - step, REPS)
        remote(
            columns_ref.at[rep],
            columns_ref.at[source],
            column_sems.at[0, step],
            column_sems.at[1, step],
            (leaf, other),
        ).wait_recv()
    for copy in sent:
        copy.wait_send()
    push_wait_send()


def near_kernel(
    times_ref,
    columns_ref,
    skel_leaf_ref,
    t_root_ref,
    window_vectors_ref,
    transfer_ref,
    basis_ref,
    halo_ref,
    out_ref,
    own_out_ref,
    list_ref,
    window_ref,
    own_ref,
    own_skel_ref,
    skel_rows_ref,
    vectors_ref,
    total_ref,
    s_ref,
    t_ref,
    near_shifted_even,
    near_shifted_odd,
    near_even,
    near_odd,
    far_shifted_even,
    far_shifted_odd,
    far_even,
    far_odd,
):
    near_shifted, near_tiles = (near_shifted_even, near_shifted_odd), (near_even, near_odd)
    far_shifted, far_tiles = (far_shifted_even, far_shifted_odd), (far_even, far_odd)
    rep = lax.axis_index("rep")
    root_rows = stack_two(t_root_ref[...])
    t_ref[...] = jnp.zeros_like(t_ref)

    def prepare(leaf, _):
        source = lax.rem(leaf, REPS)
        k = leaf // REPS
        points = columns_ref[source, k].astype(F32)
        columns = with_norms(points, True)
        own_ref[leaf] = columns.astype(BF16)
        marks = one_hot(skel_leaf_ref[pl.ds(leaf, 1), :])
        own_skel_ref[leaf] = with_norms(dot_nn(columns_ref[source, k], marks), True).astype(BF16)
        return 0

    lax.fori_loop(0, LEAVES, prepare, 0, unroll=4)

    def partner_rows(k, _):
        for side, points in enumerate((halo_ref[0, k], columns_ref[rep, k], halo_ref[1, k])):
            window_ref[side * QUARTER + k] = with_norms(points.astype(F32), False).T.astype(BF16)
        return 0

    lax.fori_loop(0, QUARTER, partner_rows, 0, unroll=2)

    def from_root(leaf, _):
        t_ref[leaf, pl.ds(pl.multiple_of(rep * OWN, OWN), OWN), :] = fold_two(
            dot_nt(root_rows, transfer_ref[leaf])
        )
        return 0

    lax.fori_loop(0, LEAVES, from_root, 0, unroll=8)

    for side in range(SIDES):
        for column in range(2):
            span = slice(column * LEAF, (column + 1) * LEAF)
            blocks = [window_vectors_ref[side, source, :, span].astype(F32) for source in range(REPS)]
            vectors_ref[side * QUARTER + column] = jnp.concatenate(
                [block[:OWN] for block in blocks], axis=0
            ).astype(BF16)
            vectors_ref[side * QUARTER + column + 2] = jnp.concatenate(
                [block[OWN:] for block in blocks], axis=0
            ).astype(BF16)
    for k in range(QUARTER):
        leaf = k * REPS + rep
        s_leaf = dot_nn(vectors_ref[QUARTER + k], basis_ref[leaf])
        s_ref[k] = stack_two(s_leaf)
        skel = own_skel_ref[leaf].astype(F32)
        skel_rows_ref[k] = with_norms(skel[:DIM] * -0.5, False).T.astype(BF16)

    total_ref[...] = jnp.zeros_like(total_ref)

    def make_list(first, width):
        def one_leaf(leaf, filled):
            for entry in range(first, first + width):
                list_ref[filled] = leaf * 16 + entry
                filled = filled + jnp.where(times_ref[leaf, entry] > 0, 1, 0)
            return filled

        filled = lax.fori_loop(0, LEAVES, one_leaf, 0, unroll=2)
        for pad in range(4 * WAYS):
            list_ref[filled + pad] = first
        return filled

    def run(filled, product, keep, apply, shifted_refs, tile_refs):
        def start(group, shifted_ref):
            for way in range(WAYS):
                code = list_ref[group * WAYS + way]
                shifted_ref[way] = product(code >> 4, code & 15)

        def middle(shifted_ref, tile_ref):
            for way in range(WAYS):
                keep(tile_ref, way, kernel_values(shifted_ref[way]))

        def finish(group, tile_ref):
            for way in range(WAYS):
                number = group * WAYS + way
                code = list_ref[jnp.maximum(number, 0)]
                leaf, entry = code >> 4, code & 15
                times = jnp.where((number >= 0) & (number < filled), times_ref[leaf, entry], 0)
                apply(leaf, entry, times.astype(F32), tile_ref, way)

        start(0, shifted_refs[0])
        tile_refs[1][...] = jnp.zeros_like(tile_refs[1])

        def step(number, _):
            even = number * 2
            start(even + 1, shifted_refs[1])
            middle(shifted_refs[0], tile_refs[0])
            finish(even - 1, tile_refs[1])
            start(even + 2, shifted_refs[0])
            middle(shifted_refs[1], tile_refs[1])
            finish(even, tile_refs[0])
            return 0

        steps = (filled + 2 * WAYS - 1) // (2 * WAYS)
        lax.fori_loop(0, steps, step, 0)
        finish(2 * steps - 1, tile_refs[1])

    def near_keep(tile_ref, way, values):
        tile_ref[way] = values.astype(BF16)

    def near_apply(leaf, entry, times, tile_ref, way):
        total_ref[leaf] += dot_nn(vectors_ref[entry], tile_ref[way]) * times

    run(
        make_list(0, PARTNERS),
        lambda leaf, entry: dot_nn(window_ref[entry], own_ref[leaf]),
        near_keep,
        near_apply,
        near_shifted,
        near_tiles,
    )

    def far_keep(tile_ref, way, values):
        high, low = split_two(values)
        tile_ref[way, 0] = high
        tile_ref[way, 1] = low

    def far_apply(leaf, entry, times, tile_ref, way):
        rows = s_ref[entry - PARTNERS]
        term = fold_two(dot_nn(rows, tile_ref[way, 0])) + dot_nn(rows[:RHS], tile_ref[way, 1])
        t_ref[leaf] += term * times

    run(
        make_list(PARTNERS, QUARTER),
        lambda leaf, entry: dot_nn(skel_rows_ref[entry - PARTNERS], own_skel_ref[leaf]),
        far_keep,
        far_apply,
        far_shifted,
        far_tiles,
    )

    for leaf in range(LEAVES):
        total_ref[leaf] += dot_wide_nt(t_ref[leaf], basis_ref[leaf])
    mine = pl.ds(pl.multiple_of(rep * OWN, OWN), OWN)
    for leaf in range(LEAVES):
        own_out_ref[:, leaf * LEAF : (leaf + 1) * LEAF] = total_ref[leaf, mine, :]
    for leaf in range(LEAVES // 2):
        top = total_ref[leaf].reshape(REPS, OWN, LEAF)
        bottom = total_ref[leaf + LEAVES // 2].reshape(REPS, OWN, LEAF)
        out_ref[:, :, leaf * LEAF : (leaf + 1) * LEAF] = jnp.concatenate([top, bottom], axis=1).astype(BF16)


def combine_kernel(part_ref, own_ref, order_ref, out_ref, got_ref, marks_ref, sems):
    leaf = lax.axis_index("leaf")
    rep = lax.axis_index("rep")
    half = PTS // 2
    width = half // CHUNKS
    partners = [(leaf, lax.rem(rep + step, REPS)) for step in range(1, REPS)]
    greet_signals(partners)
    greet_wait(partners)
    copies = []
    for index, partner in enumerate(partners):
        copy = remote(
            part_ref.at[partner[1]], got_ref.at[index], sems.at[0, index], sems.at[1, index], partner
        )
        copy.start()
        copies.append(copy)

    scattered = jnp.zeros((LEAVES * 2 * OWN, LEAF), F32)
    highs = []
    for chunk in range(CHUNKS):
        here = [(number, (number * half + chunk * width) // LANES) for number in range(2)]
        positions = jnp.concatenate(
            [
                order_ref[first + at : first + at + 1, :]
                for _, first in here
                for at in range(width // LANES)
            ],
            axis=1,
        )
        marks_ref[chunk] = one_hot(positions & 255)
        highs.append(positions >> 8)
    for copy in copies:
        copy.wait()
    for chunk in range(CHUNKS):
        here = [(number, (number * half + chunk * width) // LANES) for number in range(2)]
        high = jnp.broadcast_to(highs[chunk], (2 * OWN, 2 * width))
        totals = []
        for number, first in here:
            rows = slice(number * OWN, (number + 1) * OWN)
            total = -own_ref[:, first * LANES : first * LANES + width]
            for index in range(REPS - 1):
                total = total - got_ref[index, :, chunk * width : (chunk + 1) * width].astype(F32)[rows]
            totals.append(total)
        total = jnp.concatenate(totals, axis=1)
        rounded = total.astype(BF16).astype(F32)
        terms = jnp.concatenate([rounded, total - rounded], axis=0)
        rows = jnp.concatenate(
            [jnp.where(high == source, terms, 0.0).astype(BF16) for source in range(LEAVES)], axis=0
        )
        scattered = scattered + dot_nt(rows, marks_ref[chunk])
    for source in range(LEAVES):
        first = source * 2 * OWN
        out_ref[:, source * LEAF : (source + 1) * LEAF] = (
            scattered[first : first + OWN] + scattered[first + OWN : first + 2 * OWN]
        )


def vmem(count):
    return [pl.BlockSpec(memory_space=pltpu.VMEM)] * count


def shape(dims, dtype):
    return jax.ShapeDtypeStruct(dims, dtype)


def params(collective_id=None):
    if collective_id is None:
        return pltpu.CompilerParams(vmem_limit_bytes=VMEM_LIMIT)
    return pltpu.CompilerParams(
        collective_id=collective_id, has_side_effects=True, vmem_limit_bytes=VMEM_LIMIT
    )


def on_device(
    count,
    coords,
    right_sides,
    leaf_order,
    leaf_basis,
    leaf_transfer,
    top_transfer,
    skel_leaf,
    skel_root,
    admissible,
    near_leaves,
    near_count,
):
    levels = count.bit_length() - 1
    spans = phases_of(levels)
    order = leaf_order.reshape(BLOCKS, LANES)
    dma = pltpu.SemaphoreType.DMA
    sorted_vectors = pl.pallas_call(
        vectors_kernel,
        out_shape=shape((LEAVES, OWN, LEAF), F32),
        in_specs=vmem(2),
        out_specs=pl.BlockSpec(memory_space=pltpu.VMEM),
        compiler_params=params(),
        cost_estimate=pl.CostEstimate(flops=10**9, bytes_accessed=10**6, transcendentals=0),
        name="vectors",
    )(
        right_sides.reshape(OWN, LEAVES, LEAF).transpose(1, 0, 2).reshape(LEAVES * OWN, LEAF),
        order,
    )
    halo, columns, window_vectors, t_root, times, skel_here = pl.pallas_call(
        functools.partial(gather_kernel, count, levels),
        out_shape=(
            shape((2, QUARTER, DIM, LEAF), BF16),
            shape((REPS, QUARTER, DIM, LEAF), BF16),
            shape((SIDES, REPS, 2 * OWN, 2 * LEAF), BF16),
            shape((OWN, RANK), F32),
            shape((LEAVES, LANES), I32),
            shape((LEAVES, RANK), I32),
        ),
        in_specs=vmem(11),
        out_specs=tuple(vmem(6)),
        scratch_shapes=[
            pltpu.VMEM((REPS, 2 * OWN, 2 * LEAF), BF16),
            pltpu.VMEM((levels, DIM, RANK), BF16),
            pltpu.VMEM((levels, DIM, RANK), BF16),
            pltpu.VMEM((levels, 2, RANK, RANK), BF16),
            pltpu.VMEM((levels, OWN, RANK), F32),
        ]
        + [pltpu.VMEM((1 << width, OWN, RANK), F32) for _, width in spans]
        + [dma((2, 1 << width)) for _, width in spans]
        + [
            dma((2, 2)),
            dma((2, REPS - 1)),
            dma((2, REPS + 1)),
            dma((2, levels, 1 << (max(PHASES) - 1))),
        ],
        compiler_params=params(0),
        name="gather",
    )(
        coords,
        sorted_vectors,
        order,
        leaf_basis,
        leaf_transfer,
        top_transfer[: levels - 1],
        skel_root,
        skel_leaf,
        admissible.T,
        near_leaves,
        near_count.reshape(1, LEAVES),
    )

    part, own_part = pl.pallas_call(
        near_kernel,
        out_shape=(shape((REPS, 2 * OWN, PTS // 2), BF16), shape((OWN, PTS), F32)),
        in_specs=[pl.BlockSpec(memory_space=pltpu.SMEM)] + vmem(7),
        out_specs=tuple(vmem(2)),
        scratch_shapes=[
            pltpu.SMEM((LEAVES * PARTNERS + 4 * WAYS + 8,), I32),
            pltpu.VMEM((PARTNERS, LEAF, LANES), BF16),
            pltpu.VMEM((LEAVES, LANES, LEAF), BF16),
            pltpu.VMEM((LEAVES, LANES, RANK), BF16),
            pltpu.VMEM((QUARTER, RANK, LANES), BF16),
            pltpu.VMEM((PARTNERS, RHS, LEAF), BF16),
            pltpu.VMEM((LEAVES, RHS, LEAF), F32),
            pltpu.VMEM((QUARTER, 2 * RHS, RANK), BF16),
            pltpu.VMEM((LEAVES, RHS, RANK), F32),
        ]
        + [pltpu.VMEM((WAYS, LEAF, LEAF), F32)] * 2
        + [pltpu.VMEM((WAYS, LEAF, LEAF), BF16)] * 2
        + [pltpu.VMEM((WAYS, RANK, RANK), F32)] * 2
        + [pltpu.VMEM((WAYS, 2, RANK, RANK), BF16)] * 2,
        compiler_params=params(),
        name="near",
    )(
        times,
        columns,
        skel_here,
        t_root,
        window_vectors,
        leaf_transfer,
        leaf_basis,
        halo,
    )

    negative = pl.pallas_call(
        combine_kernel,
        out_shape=shape((OWN, PTS), F32),
        in_specs=vmem(3),
        out_specs=pl.BlockSpec(memory_space=pltpu.VMEM),
        scratch_shapes=[
            pltpu.VMEM((REPS - 1, 2 * OWN, PTS // 2), BF16),
            pltpu.VMEM((CHUNKS, LEAF, PTS // CHUNKS), BF16),
            dma((2, REPS - 1)),
        ],
        compiler_params=params(1),
        name="combine",
    )(part, own_part, order)
    return -negative


def solution(mesh):
    placed = (
        P(None, "leaf"),
        P("rep", "leaf"),
        P("leaf"),
        P("leaf", None, None),
        P("leaf", None, None),
        P(),
        P("leaf", None),
        P("leaf", None),
        P("leaf", None),
        P("leaf", None),
        P("leaf"),
    )
    return jax.shard_map(
        functools.partial(on_device, mesh.shape["leaf"]),
        mesh=mesh,
        in_specs=placed,
        out_specs=P("rep", "leaf"),
        check_vma=False,
    )
```

```python
import functools

import jax
import jax.numpy as jnp
from jax import lax
from jax.experimental import pallas as pl
from jax.experimental.pallas import tpu as pltpu
from jax.sharding import PartitionSpec as P

MESH = pl.DeviceIdType.MESH
F32 = jnp.float32
BF16 = jnp.bfloat16
I32 = jnp.int32

DIM = 64
RANK = 128
LEAF = 256
LEAVES = 16
PTS = 4096
LANES = 128
BLOCKS = PTS // LANES
REPS = 4
QUARTER = LEAVES // REPS
OWN = 8
RHS = 32
SIDES = 3
PARTNERS = SIDES * QUARTER
PHASES = (3, 2, 2)
WAYS = 2
CHUNKS = 4
VMEM_LIMIT = 24 * 1024 * 1024


def dot_nn(a, b):
    return lax.dot_general(a, b, (((1,), (0,)), ((), ())), preferred_element_type=F32)


def dot_nt(a, b):
    return lax.dot_general(a, b, (((1,), (1,)), ((), ())), preferred_element_type=F32)


def kernel_values(shifted):
    shifted = jnp.maximum(shifted, 1.0)
    return jnp.exp((shifted * -0.5) * lax.rsqrt(shifted))


def split_two(x):
    high = x.astype(BF16)
    return high, (x - high.astype(F32)).astype(BF16)


def stack_two(x):
    high = x.astype(BF16).astype(F32)
    return jnp.concatenate([high, x - high], axis=0).astype(BF16)


def fold_two(x):
    half = x.shape[0] // 2
    return x[:half] + x[half:]


def dot_wide(x, matrix):
    return fold_two(dot_nn(stack_two(x), matrix))


def dot_wide_nt(x, matrix):
    return fold_two(dot_nt(stack_two(x), matrix))


def dot_both_wide(x, matrix):
    rows = stack_two(x)
    high, low = split_two(matrix)
    return fold_two(dot_nn(rows, high)) + fold_two(dot_nn(rows, low))


def with_norms(points, own):
    count = points.shape[1]
    norm = jnp.sum(points * points, axis=0, keepdims=True)
    if own:
        norm = norm + 1.0
    high = norm.astype(BF16).astype(F32)
    rest = norm - high
    mid = rest.astype(BF16).astype(F32)
    low = rest - mid
    row = lax.broadcasted_iota(I32, (16, count), 0)
    if not own:
        row = row - 3
    tail = jnp.where(row == 0, high, jnp.where(row == 1, mid, jnp.where(row == 2, low, 0.0)))
    ones = lax.broadcasted_iota(I32, (16, count), 0) - (3 if own else 0)
    tail = jnp.where((ones >= 0) & (ones < 3), 1.0, tail)
    head = points * -2.0 if own else points
    return jnp.concatenate([head, tail, jnp.zeros((LANES - DIM - 16, count), F32)], axis=0)


def one_hot(low):
    row = lax.broadcasted_iota(I32, (LEAF, low.shape[1]), 0)
    return jnp.where(row == low, 1.0, 0.0).astype(BF16)


def choose(slices, positions):
    marks = one_hot(positions & 255)
    rows = slices[0].shape[0]
    high = jnp.broadcast_to(positions >> 8, (rows, positions.shape[1]))
    out = jnp.zeros((rows, positions.shape[1]), F32)
    together = min(len(slices), 512 // rows)
    for first in range(0, len(slices), together):
        block = dot_nn(jnp.concatenate(slices[first : first + together], axis=0), marks)
        for number in range(together):
            out = jnp.where(high == first + number, block[number * rows : (number + 1) * rows], out)
    return out


def order_of(order_ref, leaf):
    return jnp.concatenate([order_ref[pl.ds(leaf * 2 + half, 1), :] for half in range(2)], axis=1)


def pick(table, lanes):
    return jnp.take_along_axis(table, lanes, axis=1, mode="promise_in_bounds")


def greet_signals(devices):
    barrier = pltpu.get_barrier_semaphore()
    for device in devices:
        pl.semaphore_signal(barrier, inc=1, device_id=device, device_id_type=MESH)


def greet_wait(devices):
    pl.semaphore_wait(pltpu.get_barrier_semaphore(), len(devices))


def remote(source, target, send_sem, recv_sem, device):
    return pltpu.make_async_remote_copy(
        src_ref=source,
        dst_ref=target,
        send_sem=send_sem,
        recv_sem=recv_sem,
        device_id=device,
        device_id_type=MESH,
    )


def phases_of(levels):
    spans, first = [], 0
    for width in PHASES:
        width = min(width, levels - first)
        if width > 0:
            spans.append((first, width))
        first += width
    return spans


def vectors_kernel(rows_ref, order_ref, sorted_ref):
    vector_rows = rows_ref[...]

    def sort_vectors(number, _):
        positions = order_of(order_ref, number)
        block = dot_nn(vector_rows, one_hot(positions & 255))
        high = jnp.broadcast_to(positions >> 8, (OWN, LEAF))
        out = jnp.zeros((OWN, LEAF), F32)
        for source in range(LEAVES):
            out = jnp.where(high == source, block[source * OWN : (source + 1) * OWN], out)
        sorted_ref[number] = out
        return 0

    lax.fori_loop(0, LEAVES, sort_vectors, 0, unroll=4)


def gather_kernel(
    count,
    levels,
    coords_ref,
    sorted_ref,
    order_ref,
    basis_ref,
    transfer_ref,
    top_ref,
    skel_root_ref,
    skel_leaf_ref,
    admissible_ref,
    near_ref,
    count_ref,
    halo_ref,
    columns_ref,
    window_vectors_ref,
    t_root_ref,
    times_ref,
    skel_out_ref,
    vectors_ref,
    points_ref,
    got_points_ref,
    kernel_ref,
    sibling_ref,
    *rest,
):
    spans = phases_of(levels)
    gathered_refs = rest[: len(spans)]
    spread_sems = rest[len(spans) : 2 * len(spans)]
    row_sems, column_sems, vector_sems, push_sems = rest[2 * len(spans) :]

    leaf = lax.axis_index("leaf")
    rep = lax.axis_index("rep")
    before = lax.rem(leaf + count - 1, count)
    after = lax.rem(leaf + 1, count)
    others = [lax.rem(rep + step, REPS) for step in range(1, REPS)]
    partners = [(jnp.where(lax.rem(leaf, 2) == 0, before, after), rep)]
    partners += [(leaf, other) for other in others]
    for first, width in spans:
        partners += [(leaf ^ (number << first), rep) for number in range(1, 1 << width)]
    greet_signals(partners)

    def coordinate_slices():
        return [coords_ref[:, high * LEAF : (high + 1) * LEAF] for high in range(LEAVES)]

    at = jnp.broadcast_to(skel_root_ref[...], (8, LANES))
    at_high = at >> 7
    at_low = at & 127
    initial = jnp.zeros((8, LANES), I32)
    for source in range(BLOCKS):
        table = jnp.broadcast_to(order_ref[source : source + 1, :], (8, LANES))
        initial = jnp.where(at_high == source, pick(table, at_low), initial)
    points_ref[0] = choose(coordinate_slices(), initial[:1]).astype(BF16)
    sent = []

    pushes = [[] for _ in spans]

    def push_start(phase):
        if phase >= len(spans):
            return
        first, width = spans[phase]
        for level in range(first, first + width):
            for number in range(1 << (level - first), 2 << (level - first)):
                copy = remote(
                    points_ref.at[first],
                    got_points_ref.at[level],
                    push_sems.at[0, level, number - (1 << (level - first))],
                    push_sems.at[1, level, 0],
                    (leaf ^ (number << first), rep),
                )
                pushes[phase].append((level, copy))
                if level == first:
                    copy.start()
                else:
                    pl.when(lax.rem(leaf // (1 << first), 1 << (level - first)) == 0)(copy.start)

    def push_finish(phase):
        if phase >= len(spans):
            return
        first, width = spans[phase]
        for level in range(first, first + width):
            [copy for at, copy in pushes[phase] if at == level][0].wait_recv()
            if level + 1 < levels:
                on_right = lax.rem(leaf // (1 << level), 2) == 1
                points_ref[level + 1] = jnp.where(
                    on_right, got_points_ref[level].astype(F32), points_ref[level].astype(F32)
                ).astype(BF16)
        push_start(phase + 1)

    def push_wait_send():
        for (first, width), copies in zip(spans, pushes):
            for level, copy in copies:
                if level == first:
                    copy.wait_send()
                else:
                    pl.when(lax.rem(leaf // (1 << first), 1 << (level - first)) == 0)(copy.wait_send)

    def kernels(first, last):
        first, last = min(first, levels), min(last, levels)
        values = []
        for level in range(first, last):
            own = with_norms(points_ref[level].astype(F32), True).astype(BF16)
            rows = with_norms(got_points_ref[level].astype(F32), False).T.astype(BF16)
            values.append(split_two(kernel_values(dot_nn(rows, own))))
        for level, (high, low) in zip(range(first, last), values):
            kernel_ref[level, 0] = high
            kernel_ref[level, 1] = low

    spreads = []

    def spread_start(phase):
        if phase >= len(spans):
            return
        first, width = spans[phase]
        copies = []
        for number in range(1, 1 << width):
            copy = remote(
                gathered_refs[phase].at[0],
                gathered_refs[phase].at[number],
                spread_sems[phase].at[0, number],
                spread_sems[phase].at[1, number],
                (leaf ^ (number << first), rep),
            )
            copy.start()
            copies.append(copy)
            sent.append(copy)
        spreads.append(copies)

    def spread_finish(phase):
        if phase >= len(spans):
            return
        first, width = spans[phase]
        for copy in spreads[phase]:
            copy.wait_recv()
        nodes = [gathered_refs[phase][number] for number in range(1 << width)]
        for level in range(first, first + width):
            sibling_ref[level] = nodes[1]
            if level + 1 == levels:
                return
            on_right = lax.rem(leaf // (1 << level), 2) == 1
            even = jnp.concatenate(nodes[0::2], axis=0)
            odd = jnp.concatenate(nodes[1::2], axis=0)
            parents = dot_wide(jnp.where(on_right, odd, even), top_ref[level, 0]) + dot_wide(
                jnp.where(on_right, even, odd), top_ref[level, 1]
            )
            nodes = [parents[i * OWN : i * OWN + OWN] for i in range(len(nodes) // 2)]
        gathered_refs[phase + 1][0] = nodes[0]
        spread_start(phase + 1)

    def coupling(level):
        rows = stack_two(sibling_ref[level])
        return fold_two(dot_nn(rows, kernel_ref[level, 0])) + fold_two(dot_nn(rows, kernel_ref[level, 1]))

    def up(number, total):
        s_leaf = dot_nn(sorted_ref[number].astype(BF16), basis_ref[number])
        return total + dot_nn(stack_two(s_leaf), transfer_ref[number])

    s_root = fold_two(lax.fori_loop(0, LEAVES, up, jnp.zeros((2 * OWN, RANK), F32), unroll=LEAVES))
    gathered_refs[0][0] = s_root
    greet_wait(partners)
    spread_start(0)
    push_start(0)

    for target in range(REPS):
        for column in range(2):
            top = sorted_ref[column * REPS + target]
            bottom = sorted_ref[(column + 2) * REPS + target]
            vectors_ref[target, :, column * LEAF : (column + 1) * LEAF] = jnp.concatenate(
                [top, bottom], axis=0
            ).astype(BF16)
    window_vectors_ref[1, rep] = vectors_ref[rep]
    for step, other in enumerate(others):
        copy = remote(
            vectors_ref.at[other],
            window_vectors_ref.at[1, rep],
            vector_sems.at[0, step],
            vector_sems.at[1, step],
            (leaf, other),
        )
        copy.start()
        sent.append(copy)

    side_copies = []

    def pass_vectors():
        for step, other in enumerate(others):
            source = lax.rem(rep + REPS - 1 - step, REPS)
            remote(
                vectors_ref.at[rep],
                window_vectors_ref.at[1, source],
                vector_sems.at[0, step],
                vector_sems.at[1, step],
                (leaf, other),
            ).wait_recv()
        for index, (side, device) in enumerate(((2, before), (0, after))):
            copy = remote(
                window_vectors_ref.at[1],
                window_vectors_ref.at[side],
                vector_sems.at[0, REPS - 1 + index],
                vector_sems.at[1, REPS - 1 + index],
                (device, rep),
            )
            copy.start()
            side_copies.append(copy)
            sent.append(copy)


    def sort_points(k):
        number = k * REPS + rep
        points = choose(coordinate_slices(), order_of(order_ref, number))
        columns_ref[rep, k] = points.astype(BF16)

    def send_sides():
        for index, (side, device) in enumerate(((1, before), (0, after))):
            copy = remote(
                columns_ref.at[rep],
                halo_ref.at[side],
                row_sems.at[0, index],
                row_sems.at[1, index],
                (device, rep),
            )
            copy.start()
            side_copies.append(copy)
            sent.append(copy)

    def send_columns():
        for step, other in enumerate(others):
            copy = remote(
                columns_ref.at[rep],
                columns_ref.at[rep],
                column_sems.at[0, step],
                column_sems.at[1, step],
                (leaf, other),
            )
            copy.start()
            sent.append(copy)

    for k in range(QUARTER):
        sort_points(k)
    send_sides()
    send_columns()
    push_finish(0)
    spread_finish(0)
    pass_vectors()
    push_finish(1)
    spread_finish(1)
    kernels(0, 5)
    push_finish(2)
    kernels(5, 7)

    diagonal = lax.broadcasted_iota(I32, (LEAVES, LEAVES), 0) == lax.broadcasted_iota(
        I32, (LEAVES, LEAVES), 1
    )

    def as_column(row):
        return jnp.sum(jnp.where(diagonal, row, 0.0), axis=1, keepdims=True)

    near = near_ref[...]
    slot = lax.broadcasted_iota(I32, near.shape, 1)
    live = slot.astype(F32) < as_column(count_ref[...].astype(F32))
    admissible = admissible_ref[...]
    lane = lax.broadcasted_iota(I32, (LEAVES, LANES), 1)
    times = jnp.zeros((LEAVES, LANES), F32)
    for entry in range(PARTNERS + QUARTER):
        if entry < PARTNERS:
            named = jnp.where(near == entry * REPS + rep, 1.0, 0.0)
            total = jnp.sum(jnp.where(live, named, 0.0), axis=1, keepdims=True)
        else:
            named = jnp.where(admissible == (entry - PARTNERS) * REPS + rep, 1.0, 0.0)
            total = as_column(jnp.sum(named, axis=0, keepdims=True))
        times = jnp.where(lane == entry, total, times)
    times_ref[...] = times.astype(I32)
    skel_out_ref[...] = skel_leaf_ref[...]

    split = spans[-1][0]
    sides = [lax.rem(leaf // (1 << level), 2) for level in range(levels)]
    lower = coupling(split - 1)
    for level in range(split - 2, -1, -1):
        lower = coupling(level) + dot_wide_nt(lower, top_ref[level, sides[level]])
    product = top_ref[0, sides[0]].astype(F32)
    for level in range(1, split):
        product = dot_wide(product, top_ref[level, sides[level]])
    product_high, product_low = split_two(product)

    spread_finish(2)
    running = coupling(levels - 1)
    for level in range(levels - 2, split - 1, -1):
        running = coupling(level) + dot_wide_nt(running, top_ref[level, sides[level]])
    rows = stack_two(running)
    running = lower + (fold_two(dot_nt(rows, product_high)) + fold_two(dot_nt(rows, product_low)))
    t_root_ref[...] = running

    for copy in side_copies:
        copy.wait_recv()
    for step, other in enumerate(others):
        source = lax.rem(rep + REPS - 1 - step, REPS)
        remote(
            columns_ref.at[rep],
            columns_ref.at[source],
            column_sems.at[0, step],
            column_sems.at[1, step],
            (leaf, other),
        ).wait_recv()
    for copy in sent:
        copy.wait_send()
    push_wait_send()


def near_kernel(
    times_ref,
    columns_ref,
    skel_leaf_ref,
    t_root_ref,
    window_vectors_ref,
    transfer_ref,
    basis_ref,
    halo_ref,
    out_ref,
    own_out_ref,
    list_ref,
    window_ref,
    own_ref,
    own_skel_ref,
    skel_rows_ref,
    vectors_ref,
    total_ref,
    s_ref,
    t_ref,
    near_shifted_even,
    near_shifted_odd,
    near_even,
    near_odd,
    far_shifted_even,
    far_shifted_odd,
    far_even,
    far_odd,
):
    near_shifted, near_tiles = (near_shifted_even, near_shifted_odd), (near_even, near_odd)
    far_shifted, far_tiles = (far_shifted_even, far_shifted_odd), (far_even, far_odd)
    rep = lax.axis_index("rep")
    root_rows = stack_two(t_root_ref[...])
    t_ref[...] = jnp.zeros_like(t_ref)

    def prepare(leaf, _):
        source = lax.rem(leaf, REPS)
        k = leaf // REPS
        points = columns_ref[source, k].astype(F32)
        columns = with_norms(points, True)
        own_ref[leaf] = columns.astype(BF16)
        marks = one_hot(skel_leaf_ref[pl.ds(leaf, 1), :])
        own_skel_ref[leaf] = with_norms(dot_nn(columns_ref[source, k], marks), True).astype(BF16)
        return 0

    lax.fori_loop(0, LEAVES, prepare, 0, unroll=4)

    def partner_rows(k, _):
        for side, points in enumerate((halo_ref[0, k], columns_ref[rep, k], halo_ref[1, k])):
            window_ref[side * QUARTER + k] = with_norms(points.astype(F32), False).T.astype(BF16)
        return 0

    lax.fori_loop(0, QUARTER, partner_rows, 0, unroll=2)

    def from_root(leaf, _):
        t_ref[leaf, pl.ds(pl.multiple_of(rep * OWN, OWN), OWN), :] = fold_two(
            dot_nt(root_rows, transfer_ref[leaf])
        )
        return 0

    lax.fori_loop(0, LEAVES, from_root, 0, unroll=8)

    for side in range(SIDES):
        for column in range(2):
            span = slice(column * LEAF, (column + 1) * LEAF)
            blocks = [window_vectors_ref[side, source, :, span].astype(F32) for source in range(REPS)]
            vectors_ref[side * QUARTER + column] = jnp.concatenate(
                [block[:OWN] for block in blocks], axis=0
            ).astype(BF16)
            vectors_ref[side * QUARTER + column + 2] = jnp.concatenate(
                [block[OWN:] for block in blocks], axis=0
            ).astype(BF16)
    for k in range(QUARTER):
        leaf = k * REPS + rep
        s_leaf = dot_nn(vectors_ref[QUARTER + k], basis_ref[leaf])
        s_ref[k] = stack_two(s_leaf)
        skel = own_skel_ref[leaf].astype(F32)
        skel_rows_ref[k] = with_norms(skel[:DIM] * -0.5, False).T.astype(BF16)

    total_ref[...] = jnp.zeros_like(total_ref)

    def make_list(first, width):
        def one_leaf(leaf, filled):
            for entry in range(first, first + width):
                list_ref[filled] = leaf * 16 + entry
                filled = filled + jnp.where(times_ref[leaf, entry] > 0, 1, 0)
            return filled

        filled = lax.fori_loop(0, LEAVES, one_leaf, 0, unroll=2)
        for pad in range(4 * WAYS):
            list_ref[filled + pad] = first
        return filled

    def run(filled, product, keep, apply, shifted_refs, tile_refs):
        def start(group, shifted_ref):
            for way in range(WAYS):
                code = list_ref[group * WAYS + way]
                shifted_ref[way] = product(code >> 4, code & 15)

        def middle(shifted_ref, tile_ref):
            for way in range(WAYS):
                keep(tile_ref, way, kernel_values(shifted_ref[way]))

        def finish(group, tile_ref):
            for way in range(WAYS):
                number = group * WAYS + way
                code = list_ref[jnp.maximum(number, 0)]
                leaf, entry = code >> 4, code & 15
                times = jnp.where((number >= 0) & (number < filled), times_ref[leaf, entry], 0)
                apply(leaf, entry, times.astype(F32), tile_ref, way)

        start(0, shifted_refs[0])
        tile_refs[1][...] = jnp.zeros_like(tile_refs[1])

        def step(number, _):
            even = number * 2
            start(even + 1, shifted_refs[1])
            middle(shifted_refs[0], tile_refs[0])
            finish(even - 1, tile_refs[1])
            start(even + 2, shifted_refs[0])
            middle(shifted_refs[1], tile_refs[1])
            finish(even, tile_refs[0])
            return 0

        steps = (filled + 2 * WAYS - 1) // (2 * WAYS)
        lax.fori_loop(0, steps, step, 0)
        finish(2 * steps - 1, tile_refs[1])

    def near_keep(tile_ref, way, values):
        tile_ref[way] = values.astype(BF16)

    def near_apply(leaf, entry, times, tile_ref, way):
        total_ref[leaf] += dot_nn(vectors_ref[entry], tile_ref[way]) * times

    run(
        make_list(0, PARTNERS),
        lambda leaf, entry: dot_nn(window_ref[entry], own_ref[leaf]),
        near_keep,
        near_apply,
        near_shifted,
        near_tiles,
    )

    def far_keep(tile_ref, way, values):
        high, low = split_two(values)
        tile_ref[way, 0] = high
        tile_ref[way, 1] = low

    def far_apply(leaf, entry, times, tile_ref, way):
        rows = s_ref[entry - PARTNERS]
        term = fold_two(dot_nn(rows, tile_ref[way, 0])) + dot_nn(rows[:RHS], tile_ref[way, 1])
        t_ref[leaf] += term * times

    run(
        make_list(PARTNERS, QUARTER),
        lambda leaf, entry: dot_nn(skel_rows_ref[entry - PARTNERS], own_skel_ref[leaf]),
        far_keep,
        far_apply,
        far_shifted,
        far_tiles,
    )

    for leaf in range(LEAVES):
        total_ref[leaf] += dot_wide_nt(t_ref[leaf], basis_ref[leaf])
    mine = pl.ds(pl.multiple_of(rep * OWN, OWN), OWN)
    for leaf in range(LEAVES):
        own_out_ref[:, leaf * LEAF : (leaf + 1) * LEAF] = total_ref[leaf, mine, :]
    for leaf in range(LEAVES // 2):
        top = total_ref[leaf].reshape(REPS, OWN, LEAF)
        bottom = total_ref[leaf + LEAVES // 2].reshape(REPS, OWN, LEAF)
        out_ref[:, :, leaf * LEAF : (leaf + 1) * LEAF] = jnp.concatenate([top, bottom], axis=1).astype(BF16)


def combine_kernel(part_ref, own_ref, order_ref, out_ref, got_ref, marks_ref, sems):
    leaf = lax.axis_index("leaf")
    rep = lax.axis_index("rep")
    half = PTS // 2
    width = half // CHUNKS
    partners = [(leaf, lax.rem(rep + step, REPS)) for step in range(1, REPS)]
    greet_signals(partners)
    greet_wait(partners)
    copies = []
    for index, partner in enumerate(partners):
        copy = remote(
            part_ref.at[partner[1]], got_ref.at[index], sems.at[0, index], sems.at[1, index], partner
        )
        copy.start()
        copies.append(copy)

    scattered = jnp.zeros((LEAVES * 2 * OWN, LEAF), F32)
    highs = []
    for chunk in range(CHUNKS):
        here = [(number, (number * half + chunk * width) // LANES) for number in range(2)]
        positions = jnp.concatenate(
            [
                order_ref[first + at : first + at + 1, :]
                for _, first in here
                for at in range(width // LANES)
            ],
            axis=1,
        )
        marks_ref[chunk] = one_hot(positions & 255)
        highs.append(positions >> 8)
    for copy in copies:
        copy.wait()
    for chunk in range(CHUNKS):
        here = [(number, (number * half + chunk * width) // LANES) for number in range(2)]
        high = jnp.broadcast_to(highs[chunk], (2 * OWN, 2 * width))
        totals = []
        for number, first in here:
            rows = slice(number * OWN, (number + 1) * OWN)
            total = -own_ref[:, first * LANES : first * LANES + width]
            for index in range(REPS - 1):
                total = total - got_ref[index, :, chunk * width : (chunk + 1) * width].astype(F32)[rows]
            totals.append(total)
        total = jnp.concatenate(totals, axis=1)
        rounded = total.astype(BF16).astype(F32)
        terms = jnp.concatenate([rounded, total - rounded], axis=0)
        rows = jnp.concatenate(
            [jnp.where(high == source, terms, 0.0).astype(BF16) for source in range(LEAVES)], axis=0
        )
        scattered = scattered + dot_nt(rows, marks_ref[chunk])
    for source in range(LEAVES):
        first = source * 2 * OWN
        out_ref[:, source * LEAF : (source + 1) * LEAF] = (
            scattered[first : first + OWN] + scattered[first + OWN : first + 2 * OWN]
        )


def vmem(count):
    return [pl.BlockSpec(memory_space=pltpu.VMEM)] * count


def shape(dims, dtype):
    return jax.ShapeDtypeStruct(dims, dtype)


def params(collective_id=None):
    if collective_id is None:
        return pltpu.CompilerParams(vmem_limit_bytes=VMEM_LIMIT)
    return pltpu.CompilerParams(
        collective_id=collective_id, has_side_effects=True, vmem_limit_bytes=VMEM_LIMIT
    )


def on_device(
    count,
    coords,
    right_sides,
    leaf_order,
    leaf_basis,
    leaf_transfer,
    top_transfer,
    skel_leaf,
    skel_root,
    admissible,
    near_leaves,
    near_count,
):
    levels = count.bit_length() - 1
    spans = phases_of(levels)
    order = leaf_order.reshape(BLOCKS, LANES)
    dma = pltpu.SemaphoreType.DMA
    sorted_vectors = pl.pallas_call(
        vectors_kernel,
        out_shape=shape((LEAVES, OWN, LEAF), F32),
        in_specs=vmem(2),
        out_specs=pl.BlockSpec(memory_space=pltpu.VMEM),
        compiler_params=params(),
        cost_estimate=pl.CostEstimate(flops=10**9, bytes_accessed=10**6, transcendentals=0),
        name="vectors",
    )(
        right_sides.reshape(OWN, LEAVES, LEAF).transpose(1, 0, 2).reshape(LEAVES * OWN, LEAF),
        order,
    )
    halo, columns, window_vectors, t_root, times, skel_here = pl.pallas_call(
        functools.partial(gather_kernel, count, levels),
        out_shape=(
            shape((2, QUARTER, DIM, LEAF), BF16),
            shape((REPS, QUARTER, DIM, LEAF), BF16),
            shape((SIDES, REPS, 2 * OWN, 2 * LEAF), BF16),
            shape((OWN, RANK), F32),
            shape((LEAVES, LANES), I32),
            shape((LEAVES, RANK), I32),
        ),
        in_specs=vmem(11),
        out_specs=tuple(vmem(6)),
        scratch_shapes=[
            pltpu.VMEM((REPS, 2 * OWN, 2 * LEAF), BF16),
            pltpu.VMEM((levels, DIM, RANK), BF16),
            pltpu.VMEM((levels, DIM, RANK), BF16),
            pltpu.VMEM((levels, 2, RANK, RANK), BF16),
            pltpu.VMEM((levels, OWN, RANK), F32),
        ]
        + [pltpu.VMEM((1 << width, OWN, RANK), F32) for _, width in spans]
        + [dma((2, 1 << width)) for _, width in spans]
        + [
            dma((2, 2)),
            dma((2, REPS - 1)),
            dma((2, REPS + 1)),
            dma((2, levels, 1 << (max(PHASES) - 1))),
        ],
        compiler_params=params(0),
        name="gather",
    )(
        coords,
        sorted_vectors,
        order,
        leaf_basis,
        leaf_transfer,
        top_transfer[: levels - 1],
        skel_root,
        skel_leaf,
        admissible.T,
        near_leaves,
        near_count.reshape(1, LEAVES),
    )

    part, own_part = pl.pallas_call(
        near_kernel,
        out_shape=(shape((REPS, 2 * OWN, PTS // 2), BF16), shape((OWN, PTS), F32)),
        in_specs=[pl.BlockSpec(memory_space=pltpu.SMEM)] + vmem(7),
        out_specs=tuple(vmem(2)),
        scratch_shapes=[
            pltpu.SMEM((LEAVES * PARTNERS + 4 * WAYS + 8,), I32),
            pltpu.VMEM((PARTNERS, LEAF, LANES), BF16),
            pltpu.VMEM((LEAVES, LANES, LEAF), BF16),
            pltpu.VMEM((LEAVES, LANES, RANK), BF16),
            pltpu.VMEM((QUARTER, RANK, LANES), BF16),
            pltpu.VMEM((PARTNERS, RHS, LEAF), BF16),
            pltpu.VMEM((LEAVES, RHS, LEAF), F32),
            pltpu.VMEM((QUARTER, 2 * RHS, RANK), BF16),
            pltpu.VMEM((LEAVES, RHS, RANK), F32),
        ]
        + [pltpu.VMEM((WAYS, LEAF, LEAF), F32)] * 2
        + [pltpu.VMEM((WAYS, LEAF, LEAF), BF16)] * 2
        + [pltpu.VMEM((WAYS, RANK, RANK), F32)] * 2
        + [pltpu.VMEM((WAYS, 2, RANK, RANK), BF16)] * 2,
        compiler_params=params(),
        name="near",
    )(
        times,
        columns,
        skel_here,
        t_root,
        window_vectors,
        leaf_transfer,
        leaf_basis,
        halo,
    )

    negative = pl.pallas_call(
        combine_kernel,
        out_shape=shape((OWN, PTS), F32),
        in_specs=vmem(3),
        out_specs=pl.BlockSpec(memory_space=pltpu.VMEM),
        scratch_shapes=[
            pltpu.VMEM((REPS - 1, 2 * OWN, PTS // 2), BF16),
            pltpu.VMEM((CHUNKS, LEAF, PTS // CHUNKS), BF16),
            dma((2, REPS - 1)),
        ],
        compiler_params=params(1),
        name="combine",
    )(part, own_part, order)
    return -negative


def solution(mesh):
    placed = (
        P(None, "leaf"),
        P("rep", "leaf"),
        P("leaf"),
        P("leaf", None, None),
        P("leaf", None, None),
        P(),
        P("leaf", None),
        P("leaf", None),
        P("leaf", None),
        P("leaf", None),
        P("leaf"),
    )
    return jax.shard_map(
        functools.partial(on_device, mesh.shape["leaf"]),
        mesh=mesh,
        in_specs=placed,
        out_specs=P("rep", "leaf"),
        check_vma=False,
    )
```
